128 devices in a mesh: dp: 8 (over x_hi, z), context: 16 (over x_lo, y, core).
Axes of the slice: x: 4 (x_hi: 2, x_lo: 2; x = x_hi * 2 + x_lo), y: 4, z: 4, core: 2. Of those that a mesh axis runs over, the one named last changes fastest.
Arguments:
- queries: bfloat16 [65536, 1024], P(('dp', 'context')), parts along dimension 0, may hold values from -110 to 110
- key_rows: bfloat16 [65536, 128], P(('dp', 'context')), parts along dimension 0, may hold values from -5 to 5
- values: bfloat16 [65536, 128], P(('dp', 'context')), parts along dimension 0, may hold values from -6 to 6
- out_grad: bfloat16 [65536, 1024], P(('dp', 'context')), parts along dimension 0, may hold values from -6 to 6
- lengths: int32 [128], P('dp'), parts along dimension 0, may hold values from 1 to 4096, 8192 in all
- block_owner: int32 [1024], P('dp'), parts along dimension 0, may hold values from 0 to 15, as said below
Outputs:
- attn_out: bfloat16 [65536, 1024], P(('dp', 'context')), parts along dimension 0
- query_grad: bfloat16 [65536, 1024], P(('dp', 'context')), parts along dimension 0
- key_grad: bfloat16 [65536, 128], P(('dp', 'context')), parts along dimension 0
- value_grad: bfloat16 [65536, 128], P(('dp', 'context')), parts along dimension 0
- pair_count: float32 [128], P(('dp', 'context')), parts along dimension 0
The draws below stay inside these ranges and needn't reach their ends.
There are 8 independent parts, one for each index of `dp`. The reference program is written for one: setup_inputs(seed, part) draws one part's arguments, and reference() takes and returns one part's arrays. A program takes and returns all parts, laid end to end along the dimension named above; each array names one. Nothing has to cross between parts.
Inputs may be any that keep to these rules, and one draw needn't show every extreme that they name: Each pack's lengths sum to 8192; one document has exactly 4096 tokens. `block_owner`: each rank is assigned exactly 8 blocks, and at most one of the 8 blocks of any one rank's own rows.
All inputs are finite; a program needn't handle non-finite values.
Results may differ from the reference program's by a relative error of at most 0.035.
Values may be sent and summed in bfloat16 or wider, within the bound.
A program may use at most 64 MiB of HBM per device.

```python
import math
import jax
import jax.numpy as jnp
import numpy as np
from jax import lax

HEADS = 8
DH = 128
BPR = 8
TOKENS = 8192
DOCS = 16
RANKS = 16
NBLK = 128
BLOCK = 64
DOC_MAX = 4096


def drawn_keys(key):
    key_base = jnp.clip(jax.random.normal(key, (TOKENS, DH), jnp.float32), -5.0, 5.0)
    return key_base


def draw_key_rows(key, part):
    key_base = drawn_keys(key)
    return key_base.astype(jnp.bfloat16)


def draw_queries(key, part):
    key = jax.random.fold_in(key, 5)
    query_base = jnp.clip(jax.random.normal(key, (TOKENS, HEADS, DH), jnp.float32), -5.0, 5.0)
    return query_base.reshape(TOKENS, HEADS * DH).astype(jnp.bfloat16)


def draw_block_owner(key, part):
    key = jax.random.fold_in(key, 7)
    rank_count = NBLK // BPR
    offsets = jax.random.permutation(key, rank_count)[:BPR]
    source_line = jnp.arange(rank_count, dtype=jnp.int32)
    owners = (source_line[:, None] + offsets[None, :].astype(jnp.int32)) % rank_count
    return owners.reshape(NBLK).astype(jnp.int32)


def block_levels(own_key, extent, shards, smallest, largest):
    def one(axis_at, shards_of):
        draws = jax.random.uniform(jax.random.fold_in(jax.random.fold_in(own_key, 6), axis_at), (shards_of,), jnp.float32, smallest / len(shards), largest / len(shards))
        return jnp.repeat(jnp.exp(draws), extent[axis_at] // shards_of).reshape((-1,) + (1,) * (len(extent) - axis_at - 1))

    gain = one(*shards[0])
    for cut in shards[1:]:
        gain = gain * one(*cut)
    return gain


def profile(amount, total, most, lean):
    portions = [(1 << 20) // math.isqrt(standing ** lean) + 1 for standing in range(2, amount + 1)]
    surplus, counts = total - most - (amount - 1), [1] * (amount - 1)
    while surplus > 0:
        candidates = [i for i in range(amount - 1) if counts[i] < most]
        mass, remaining = sum([portions[i] for i in candidates]), surplus
        for i in candidates:
            extra = min(most - counts[i], max(1, remaining * portions[i] // mass), surplus)
            counts[i] = counts[i] + extra
            surplus = surplus - extra
    return np.array([most] + counts)


def uneven(key, count, total, limit, slope):
    if count == 2:
        one = jax.random.randint(key, (), max(1, total - limit), min(limit, total - 1) + 1)
        return jnp.stack([one, total - one])
    tallies = jnp.asarray(profile(count, total, limit, slope), jnp.int32)
    pairs = (count - 1) // 2
    source_of, sink = tallies[1:1 + 2 * pairs:2], tallies[2:2 + 2 * pairs:2]
    slack = jnp.minimum(source_of - 1, limit - sink)
    shifted = jax.random.randint(jax.random.fold_in(key, 1), (pairs,), 0, 1 << 20) % (slack + 1)
    tallies = tallies.at[1:1 + 2 * pairs:2].set(source_of - shifted).at[2:2 + 2 * pairs:2].set(sink + shifted)
    return tallies[jax.random.permutation(jax.random.fold_in(key, 2), count)]


def scatter_about(key, extent, deviation, limit, split=(), kind=jnp.bfloat16):
    drawn = deviation * jax.random.normal(key, extent, jnp.float32)
    if split:
        drawn = drawn * block_levels(key, extent, split, -0.22, 0.18)
    return jnp.clip(drawn, -limit, limit).astype(kind)


def setup_inputs(seed: int = 0, part: int = 0) -> dict:
    arg_keys = jax.random.split(jax.random.key(seed), 7)
    part_keys = jax.random.split(jax.random.fold_in(arg_keys[6], part), 7)
    return {
        "queries": draw_queries(jax.random.fold_in(jax.random.fold_in(arg_keys[6], part), 71), part),
        "key_rows": draw_key_rows(jax.random.fold_in(jax.random.fold_in(arg_keys[6], part), 71), part),
        "values": scatter_about(part_keys[2], (TOKENS, DH), 1.0, 6.0, ((0, 16),)),
        "out_grad": scatter_about(part_keys[3], (TOKENS, HEADS * DH), 1.0, 6.0, ((0, 16),)),
        "lengths": uneven(part_keys[4], DOCS, TOKENS, DOC_MAX, 2).astype(jnp.int32),
        "block_owner": draw_block_owner(jax.random.fold_in(jax.random.fold_in(arg_keys[6], part), 71), part),
    }


NEG_FILL = -1e+30

def doc_starts(lengths, total_rows):
    doc_ends = jnp.cumsum(lengths).astype(jnp.int32)
    position = jnp.arange(total_rows, dtype=jnp.int32)
    passed = doc_ends[None, :] <= position[:, None]
    starts = lax.optimization_barrier(jnp.sum(jnp.where(passed, lengths[None, :], 0), axis=1)).astype(jnp.int32)
    return (position, starts)

def rounded(array):
    return lax.optimization_barrier(array.astype(jnp.bfloat16)).astype(jnp.float32)

def reference(queries, key_rows, values, out_grad, lengths, block_owner):
    position, starts = doc_starts(lengths, TOKENS)
    score_scale = 1.0 / math.sqrt(DH)
    span_rows = BLOCK + DOC_MAX
    query_blocks = queries.reshape(NBLK, BLOCK, HEADS, DH)
    grad_blocks = out_grad.reshape(NBLK, BLOCK, HEADS, DH)
    block_line = jnp.arange(NBLK, dtype=jnp.int32)
    key_wide = key_rows.astype(jnp.float32)
    value_wide = values.astype(jnp.float32)

    def one_block(state_pair, inputs):
        key_acc, value_acc = state_pair
        query_part, grad_part, block_idx = inputs
        first = (block_idx * BLOCK).astype(jnp.int32)
        begin = jnp.maximum(first - DOC_MAX, 0).astype(jnp.int32)
        key_tile = lax.dynamic_slice_in_dim(key_wide, begin, span_rows, 0)
        value_tile = lax.dynamic_slice_in_dim(value_wide, begin, span_rows, 0)
        pos_tile = begin + jnp.arange(span_rows, dtype=jnp.int32)
        row_pos = first + jnp.arange(BLOCK, dtype=jnp.int32)
        row_start = lax.dynamic_slice_in_dim(starts, first, BLOCK, 0)
        query_wide = query_part.astype(jnp.float32)
        grad_wide = grad_part.astype(jnp.float32)
        allowed = (pos_tile[None, :] >= row_start[:, None]) & (pos_tile[None, :] <= row_pos[:, None])
        allowed = allowed[:, None, :]
        scores = jnp.einsum('rhd,kd->rhk', query_wide, key_tile) * score_scale
        row_peak = lax.optimization_barrier(jnp.max(jnp.where(allowed, scores, NEG_FILL), axis=-1))
        exp_total = lax.optimization_barrier(jnp.sum(jnp.where(allowed, jnp.exp(scores - row_peak[..., None]), 0.0), axis=-1))
        log_total = row_peak + jnp.log(exp_total)
        weights = jnp.where(allowed, jnp.exp(scores - log_total[..., None]), 0.0)
        weights_low = rounded(weights)
        attn_part = jnp.einsum('rhk,kd->rhd', weights_low, value_tile).astype(jnp.bfloat16)
        grad_dot = lax.optimization_barrier(jnp.sum(grad_wide * attn_part.astype(jnp.float32), axis=-1))
        grad_weights = jnp.einsum('rhd,kd->rhk', grad_wide, value_tile)
        grad_scores = rounded(weights * (grad_weights - grad_dot[..., None]))
        query_part_grad = (jnp.einsum('rhk,kd->rhd', grad_scores, key_tile) * score_scale).astype(jnp.bfloat16)
        key_term = jnp.einsum('rhk,rhd->kd', grad_scores, query_wide)
        value_term = jnp.einsum('rhk,rhd->kd', weights_low, grad_wide)
        key_old = lax.dynamic_slice_in_dim(key_acc, begin, span_rows, 0)
        value_old = lax.dynamic_slice_in_dim(value_acc, begin, span_rows, 0)
        key_acc = lax.dynamic_update_slice_in_dim(key_acc, key_old + key_term, begin, 0)
        value_acc = lax.dynamic_update_slice_in_dim(value_acc, value_old + value_term, begin, 0)
        return ((key_acc, value_acc), (attn_part, query_part_grad))
    initial = (jnp.zeros((TOKENS, DH), jnp.float32), jnp.zeros((TOKENS, DH), jnp.float32))
    (key_acc, value_acc), (attn_all, query_all) = lax.scan(one_block, initial, (query_blocks, grad_blocks, block_line))
    row_total = (position - starts + 1).astype(jnp.float32)
    block_total_pairs = lax.optimization_barrier(jnp.sum(row_total.reshape(NBLK, BLOCK), axis=1))
    owner_hit = block_owner[:, None] == jnp.arange(RANKS, dtype=jnp.int32)[None, :]
    pair_count = lax.optimization_barrier(jnp.sum(jnp.where(owner_hit, block_total_pairs[:, None], 0.0), axis=0))
    attn_out = attn_all.reshape(TOKENS, HEADS * DH)
    query_grad = query_all.reshape(TOKENS, HEADS * DH)
    key_grad = (key_acc * score_scale).astype(jnp.bfloat16)
    value_grad = value_acc.astype(jnp.bfloat16)
    return (attn_out, query_grad, key_grad, value_grad, pair_count)
```

```python
import functools
import math

import jax
import jax.numpy as jnp
from jax import lax
from jax.experimental import pallas as pl
from jax.experimental.pallas import tpu as pltpu
from jax.sharding import PartitionSpec as P

NEG_FILL = -1e30
MESH = pl.DeviceIdType.MESH
YS = 4
HD = 128
GROUP = 4
TILE = 256
SPAN = 4
PASS = 512
ONES = 16
LARGE = 1e12
QBLOCK = 256
DOC_MAX = 4096


def place():
    me = lax.axis_index("context")
    return me // (2 * YS), (me // 2) % YS, me % 2


def rank_of(x, y, core):
    return (x * YS + y) * 2 + core


def remote(src, dst, send_sem, recv_sem, rank):
    return pltpu.make_async_remote_copy(
        src_ref=src,
        dst_ref=dst,
        send_sem=send_sem,
        recv_sem=recv_sem,
        device_id={"context": rank},
        device_id_type=MESH,
    )


def enter(x, y, core):
    barrier = pltpu.get_barrier_semaphore()
    others = [
        rank_of(x, y, 1 - core),
        rank_of(1 - x, y, core),
        rank_of(1 - x, y, 1 - core),
        rank_of(x, (y + 1) % YS, core),
        rank_of(x, (y + YS - 1) % YS, core),
    ]
    for other in others:
        pl.semaphore_signal(barrier, inc=1, device_id={"context": other}, device_id_type=MESH)
    pl.semaphore_wait(barrier, len(others))


def rows_at(begin, count):
    return pl.ds(pl.multiple_of(begin, count), count)


def gather_kernel(
    q_ref, g_ref, k_ref, v_ref, qa_ref, ga_ref, ka_ref, va_ref,
    own_sem, kv_send, kv_recv, core_send, core_recv, row_send, row_recv,
):
    x, y, core = place()
    shard = k_ref.shape[0]
    half = shard // 2
    width = qa_ref.shape[1]
    up, down, far = (y + 1) % YS, (y + YS - 1) % YS, (y + 2) % YS
    slot = x * 2 + core
    x_rank = rank_of(1 - x, y, core)
    core_rank = rank_of(x, y, 1 - core)
    up_rank, down_rank = rank_of(x, up, core), rank_of(x, down, core)
    enter(x, y, core)
    started = []

    def send(src, dst, send_sem, recv_sem, rank):
        copy = remote(src, dst, send_sem, recv_sem, rank)
        copy.start()
        started.append(copy)

    def landed(ref, recv_sem):
        remote(ref, ref, recv_sem, recv_sem, x_rank).wait_recv()

    own = []
    pairs = ((k_ref, ka_ref), (v_ref, va_ref))
    my_rows = rows_at(rank_of(x, y, core) * shard, shard)
    for a, (src, dst) in enumerate(pairs):
        send(src, dst.at[my_rows], kv_send.at[a, 0], kv_recv.at[a, 0], x_rank)
        send(src, dst.at[my_rows], kv_send.at[a, 1], kv_recv.at[a, 1], up_rank)
        send(src, dst.at[my_rows], kv_send.at[a, 2], kv_recv.at[a, 2], down_rank)
        send(src, dst.at[my_rows], core_send.at[a, 0], core_recv.at[a, 0], core_rank)
        copy = pltpu.make_async_copy(src, dst.at[my_rows], own_sem.at[a])
        copy.start()
        own.append(copy)

    def head_cols(owner):
        return pl.ds(pl.multiple_of(owner * width, width), width)

    for a, (src, dst) in enumerate(((q_ref, qa_ref), (g_ref, ga_ref))):
        copy = pltpu.make_async_copy(
            src.at[:, head_cols(slot)], dst.at[rows_at(slot * shard, shard)], own_sem.at[2 + a]
        )
        copy.start()
        own.append(copy)
        for d, (dx, dc) in enumerate(((0, 1), (1, 0), (1, 1))):
            tx, tc = (x + dx) % 2, (core + dc) % 2
            send(
                src.at[:, head_cols(tx * 2 + tc)],
                dst.at[rows_at(slot * shard, shard)],
                row_send.at[a, d],
                row_recv.at[a, d],
                rank_of(tx, y, tc),
            )

    def forward(a, n, ref, rows, rank, relay):
        send(ref.at[rows], ref.at[rows], relay[0].at[a, n], relay[1].at[a, n], rank)

    y_relay, c_relay = (kv_send, kv_recv), (core_send, core_recv)

    def shard_rows(sx, sy, sc):
        return rows_at(rank_of(sx, sy, sc) * shard, shard)

    def half_rows(sx, sy, sc, h):
        return rows_at(rank_of(sx, sy, sc) * shard + h * half, half)

    for a, (_, dst) in enumerate(pairs):
        rows = shard_rows(1 - x, y, core)
        landed(dst.at[rows], kv_recv.at[a, 0])
        forward(a, 3, dst, rows, up_rank, y_relay)
        forward(a, 4, dst, rows, down_rank, y_relay)
        forward(a, 1, dst, rows, core_rank, c_relay)
    for n, sx in ((1, x), (3, 1 - x)):
        for a, (_, dst) in enumerate(pairs):
            landed(dst.at[shard_rows(sx, down, core)], kv_recv.at[a, n])
            forward(a, 4 + n, dst, half_rows(sx, down, core, 0), up_rank, y_relay)
            landed(dst.at[shard_rows(sx, up, core)], kv_recv.at[a, n + 1])
            forward(a, 5 + n, dst, half_rows(sx, up, core, 1), down_rank, y_relay)
            forward(a, 1 + n, dst, shard_rows(sx, down, core), core_rank, c_relay)
            forward(a, 2 + n, dst, shard_rows(sx, up, core), core_rank, c_relay)
    for n, sx in ((1, x), (3, 1 - x)):
        for a, (_, dst) in enumerate(pairs):
            for h in range(2):
                rows = half_rows(sx, far, core, h)
                landed(dst.at[rows], kv_recv.at[a, 4 + n + h])
                forward(a, 5 + n + h, dst, rows, core_rank, c_relay)
    for a, (_, dst) in enumerate(pairs):
        oc = 1 - core
        whole = ((x, y), (1 - x, y), (x, down), (x, up), (1 - x, down), (1 - x, up))
        for n, (sx, sy) in enumerate(whole):
            landed(dst.at[shard_rows(sx, sy, oc)], core_recv.at[a, n])
        for n, sx in ((1, x), (3, 1 - x)):
            for h in range(2):
                landed(dst.at[half_rows(sx, far, oc, h)], core_recv.at[a, 5 + n + h])
    for a, dst in enumerate((qa_ref, ga_ref)):
        for d, (dx, dc) in enumerate(((0, 1), (1, 0), (1, 1))):
            tx, tc = (x + dx) % 2, (core + dc) % 2
            landed(dst.at[rows_at((tx * 2 + tc) * shard, shard)], row_recv.at[a, d])
    for copy in own:
        copy.wait()
    for copy in started:
        copy.wait_send()


def gather(queries, out_grad, keys, values, ranks):
    shard, feature = queries.shape
    width = feature // GROUP
    bf16 = jnp.bfloat16
    any_spec = pl.BlockSpec(memory_space=pl.ANY)
    dma = pltpu.SemaphoreType.DMA
    return pl.pallas_call(
        gather_kernel,
        in_specs=[any_spec] * 4,
        out_specs=[any_spec] * 4,
        out_shape=[
            jax.ShapeDtypeStruct((GROUP * shard, width), bf16),
            jax.ShapeDtypeStruct((GROUP * shard, width), bf16),
            jax.ShapeDtypeStruct((ranks * shard, HD), bf16),
            jax.ShapeDtypeStruct((ranks * shard, HD), bf16),
        ],
        scratch_shapes=[
            dma((4,)), dma((2, 9)), dma((2, 9)), dma((2, 10)), dma((2, 10)), dma((2, 3)), dma((2, 3)),
        ],
        compiler_params=pltpu.CompilerParams(collective_id=0, has_side_effects=True),
        name="gather",
    )(queries, out_grad, keys, values)


def dot(a, b):
    return jnp.dot(a, b, preferred_element_type=jnp.float32)


def attend_kernel(
    len_ref, owner_ref, q_ref, g_ref, k_ref, v_ref, o_ref, dq_ref, dk_ref, dv_ref, pair_ref,
    kt_ref, vt_ref, p_ref, qt_ref, gt_ref, qn_ref, gn_ref, dka_ref, dva_ref, ds_ref, acc_ref,
):
    blk = pl.program_id(0)
    block, width = q_ref.shape
    heads = width // HD
    cols = block * heads
    tokens = k_ref.shape[0]
    docs = len_ref.shape[0]
    f32, bf16 = jnp.float32, jnp.bfloat16
    scale = 1.0 / math.sqrt(HD)
    scale2 = scale * math.log2(math.e)
    _, y, _ = place()
    per_chip = tokens // (2 * YS)
    per_range = pl.num_programs(0) // 2

    @pl.when(blk == 0)
    def _():
        def prepare(i, carry):
            rows = rows_at(i * PASS, PASS)
            kt_ref[:, rows] = k_ref[rows, :].T
            vt_ref[0:HD, rows] = v_ref[rows, :].T
            vt_ref[HD:, rows] = jnp.ones((ONES, PASS), bf16)
            dka_ref[rows, :] = jnp.zeros((PASS, HD), f32)
            dva_ref[rows, :] = jnp.zeros((PASS, HD), f32)
            return carry

        lax.fori_loop(0, tokens // PASS, prepare, 0)
        blocks = owner_ref.shape[1]
        block_rows = tokens // blocks
        shape = (block_rows, blocks)
        pos = lax.broadcasted_iota(jnp.int32, shape, 1) * block_rows
        pos = pos + lax.broadcasted_iota(jnp.int32, shape, 0)
        begin, end = jnp.zeros(shape, jnp.int32), jnp.int32(0)
        for d in range(docs):
            end = end + len_ref[d]
            begin = jnp.where(pos >= end, end, begin)
        counts = (pos - begin + 1).astype(f32)
        counts = jnp.where(owner_ref[...] == lax.axis_index("context"), counts, 0.0)
        pair_ref[0] = jnp.sum(counts)

    first = (blk // per_range) * (tokens // 2) + y * per_chip + lax.rem(blk, per_range) * block
    row_pos = first + lax.rem(lax.broadcasted_iota(jnp.int32, (1, cols), 1), block)
    row_start = jnp.zeros((1, cols), jnp.int32)
    first_start, last_start, end = jnp.int32(0), jnp.int32(0), jnp.int32(0)
    for d in range(docs):
        end = end + len_ref[d]
        row_start = jnp.where(row_pos >= end, end, row_start)
        first_start = jnp.where(first >= end, end, first_start)
        last_start = jnp.where(first + block - 1 >= end, end, last_start)
    low = lax.div(first_start, TILE)
    high = lax.div(first + block - 1, TILE) + 1

    own_keys = kt_ref[:, rows_at(first, block)].astype(f32)
    shift = []
    for h in range(heads):
        q_t = q_ref[:, h * HD : (h + 1) * HD].T
        qt_ref[:, h * block : (h + 1) * block] = q_t
        gt_ref[:, h * block : (h + 1) * block] = g_ref[:, h * HD : (h + 1) * HD].T
        shift.append(jnp.sum(q_t.astype(f32) * own_keys, axis=0, keepdims=True) * scale2)
    shift = jnp.concatenate(shift, axis=1)

    def key_rows(t, count):
        return pl.ds(pl.multiple_of(t * TILE, TILE), count)

    def kept_rows(t, count):
        return pl.ds(pl.multiple_of((t - low) * TILE, TILE), count)

    def sweep(piece):
        count = high - low
        groups = lax.div(count, SPAN)

        def one(g, carry):
            piece(low + g * SPAN, SPAN * TILE, False)
            return carry

        lax.fori_loop(0, groups, one, 0)
        at = low + groups * SPAN
        size = SPAN // 2
        while size:
            has = lax.rem(lax.div(count, size), 2)

            @pl.when(has == 1)
            def _(at=at, size=size):
                piece(at, size * TILE, True)

            at = at + has * size
            size //= 2

    def forward(shift):
        acc_ref[...] = jnp.zeros(acc_ref.shape, f32)

        def piece(t, rows, last):
            def run(mask):
                acc = None
                part = min(rows, PASS)
                for i in range(0, rows, part):
                    tile = t + i // TILE
                    s = dot(k_ref[key_rows(tile, part), :], qt_ref[...]) * scale2 - shift
                    if mask:
                        pos = t * TILE + i + lax.broadcasted_iota(jnp.int32, s.shape, 0)
                        s = jnp.where((pos >= row_start) & (pos <= row_pos), s, NEG_FILL)
                    p_ref[kept_rows(tile, part), :] = jnp.exp2(s).astype(bf16)
                    term = dot(vt_ref[:, key_rows(tile, part)], p_ref[kept_rows(tile, part), :])
                    acc = term if acc is None else acc + term
                acc_ref[...] += acc

            if last:
                run(True)
            else:
                edge = (t * TILE < last_start) | (t * TILE + rows - 1 > first)
                pl.when(edge)(lambda: run(True))
                pl.when(jnp.logical_not(edge))(lambda: run(False))

        sweep(piece)

    forward(shift)

    @pl.when(jnp.logical_not(jnp.max(acc_ref[HD : HD + 1, :]) < LARGE))
    def _():
        def peak_pass(t, peak):
            s = dot(k_ref[key_rows(t, TILE), :], qt_ref[...]) * scale2
            pos = t * TILE + lax.broadcasted_iota(jnp.int32, s.shape, 0)
            s = jnp.where((pos >= row_start) & (pos <= row_pos), s, NEG_FILL)
            return jnp.maximum(peak, jnp.max(s.reshape(TILE // 8, 8, cols), axis=0))

        peak = lax.fori_loop(low, high, peak_pass, jnp.full((8, cols), NEG_FILL, f32))
        forward(jnp.max(peak, axis=0, keepdims=True))

    inverse = 1.0 / acc_ref[HD : HD + 1, :]
    out = (acc_ref[0:HD, :] * inverse).astype(bf16)
    grad_t = gt_ref[...].astype(f32)
    grad_dot = jnp.sum(out.astype(f32) * grad_t, axis=0, keepdims=True)
    gn_ref[...] = (grad_t * inverse).astype(bf16).T
    qn_ref[...] = (qt_ref[...].astype(f32) * inverse).astype(bf16).T
    out = out.T
    for h in range(heads):
        o_ref[:, h * HD : (h + 1) * HD] = out[h * block : (h + 1) * block, :]
    acc_ref[0:HD, :] = jnp.zeros((HD, cols), f32)

    def backward(t, rows, last):
        keys, kept = key_rows(t, rows), kept_rows(t, rows)
        grad_p = dot(v_ref[keys, :], gt_ref[...])
        ds_ref[0:rows, :] = (p_ref[kept, :].astype(f32) * (grad_p - grad_dot)).astype(bf16)
        dva_ref[keys, :] += dot(p_ref[kept, :], gn_ref[...])
        dka_ref[keys, :] += dot(ds_ref[0:rows, :], qn_ref[...])
        acc_ref[0:HD, :] += dot(kt_ref[:, keys], ds_ref[0:rows, :])

    sweep(backward)
    query_grad = (acc_ref[0:HD, :] * (inverse * scale)).astype(bf16).T
    for h in range(heads):
        dq_ref[:, h * HD : (h + 1) * HD] = query_grad[h * block : (h + 1) * block, :]

    @pl.when(blk == pl.num_programs(0) - 1)
    def _():
        def finish(i, carry):
            rows = rows_at(i * PASS, PASS)
            dk_ref[rows, :] = (dka_ref[rows, :] * scale).astype(bf16)
            dv_ref[rows, :] = dva_ref[rows, :].astype(bf16)
            return carry

        lax.fori_loop(0, tokens // PASS, finish, 0)


def attend(queries, out_grad, keys, values, lengths, block_owner):
    rows, width = queries.shape
    tokens = keys.shape[0]
    cols = QBLOCK * (width // HD)
    span = ((DOC_MAX + QBLOCK + TILE - 2) // TILE + 1) * TILE
    row_spec = pl.BlockSpec((QBLOCK, width), lambda i, *_: (i, 0))
    full_spec = pl.BlockSpec((tokens, HD), lambda i, *_: (0, 0))
    owner_spec = pl.BlockSpec((1, block_owner.shape[0]), lambda i, *_: (0, 0))
    bf16, f32 = jnp.bfloat16, jnp.float32
    return pl.pallas_call(
        attend_kernel,
        grid_spec=pltpu.PrefetchScalarGridSpec(
            num_scalar_prefetch=1,
            grid=(rows // QBLOCK,),
            in_specs=[owner_spec, row_spec, row_spec, full_spec, full_spec],
            out_specs=[
                row_spec, row_spec, full_spec, full_spec, pl.BlockSpec(memory_space=pltpu.SMEM),
            ],
            scratch_shapes=[
                pltpu.VMEM((HD, tokens), bf16),
                pltpu.VMEM((HD + ONES, tokens), bf16),
                pltpu.VMEM((span, cols), bf16),
                pltpu.VMEM((HD, cols), bf16),
                pltpu.VMEM((HD, cols), bf16),
                pltpu.VMEM((cols, HD), bf16),
                pltpu.VMEM((cols, HD), bf16),
                pltpu.VMEM((tokens, HD), f32),
                pltpu.VMEM((tokens, HD), f32),
                pltpu.VMEM((SPAN * TILE, cols), bf16),
                pltpu.VMEM((HD + ONES, cols), f32),
            ],
        ),
        out_shape=[
            jax.ShapeDtypeStruct((rows, width), bf16),
            jax.ShapeDtypeStruct((rows, width), bf16),
            jax.ShapeDtypeStruct((tokens, HD), bf16),
            jax.ShapeDtypeStruct((tokens, HD), bf16),
            jax.ShapeDtypeStruct((1,), f32),
        ],
        compiler_params=pltpu.CompilerParams(vmem_limit_bytes=62 * 2**20),
        name="attend",
    )(lengths, block_owner.reshape(1, -1), queries, out_grad, keys, values)


def scatter_kernel(
    oa_ref, qa_ref, dk_ref, dv_ref, o_ref, q_ref, key_ref, value_ref,
    part, from_core, from_far, from_near, from_x,
    own_sem, part_sem, core_send, core_recv, far_send, far_recv, near_send, near_recv,
    x_send, x_recv, row_send, row_recv,
):
    x, y, core = place()
    shard = key_ref.shape[0]
    half = shard // 2
    width = oa_ref.shape[1]
    up, down, far = (y + 1) % YS, (y + YS - 1) % YS, (y + 2) % YS
    slot = x * 2 + core
    x_rank = rank_of(1 - x, y, core)
    core_rank = rank_of(x, y, 1 - core)
    up_rank, down_rank = rank_of(x, up, core), rank_of(x, down, core)
    started, own = [], []

    def send(src, dst, send_sem, recv_sem, rank):
        copy = remote(src, dst, send_sem, recv_sem, rank)
        copy.start()
        started.append(copy)

    def landed(ref, recv_sem):
        remote(ref, ref, recv_sem, recv_sem, x_rank).wait_recv()

    pairs = (dk_ref, dv_ref)
    order = [(1 - x, far), (x, far), (1 - x, up), (x, up), (1 - x, down), (x, down), (1 - x, y), (x, y)]
    loads = []
    for n, (sx, sy) in enumerate(order):
        for a, src in enumerate(pairs):
            rows = rows_at(rank_of(sx, sy, core) * shard, shard)
            copy = pltpu.make_async_copy(src.at[rows], part.at[a, n], part_sem.at[a, n])
            copy.start()
            loads.append(copy)
    enter(x, y, core)
    for n, (sx, sy) in enumerate(order):
        for a, src in enumerate(pairs):
            rows = rows_at(rank_of(sx, sy, 1 - core) * shard, shard)
            send(src.at[rows], from_core.at[a, n], core_send.at[a, n], core_recv.at[a, n], core_rank)

    def head_cols(owner):
        return pl.ds(pl.multiple_of(owner * width, width), width)

    for a, (src, dst) in enumerate(((oa_ref, o_ref), (qa_ref, q_ref))):
        copy = pltpu.make_async_copy(
            src.at[rows_at(slot * shard, shard)], dst.at[:, head_cols(slot)], own_sem.at[a]
        )
        copy.start()
        own.append(copy)
        for d, (dx, dc) in enumerate(((0, 1), (1, 0), (1, 1))):
            tx, tc = (x + dx) % 2, (core + dc) % 2
            send(
                src.at[rows_at((tx * 2 + tc) * shard, shard)],
                dst.at[:, head_cols(slot)],
                row_send.at[a, d],
                row_recv.at[a, d],
                rank_of(tx, y, tc),
            )

    def add(ref, other):
        ref[...] = (ref[...].astype(jnp.float32) + other[...].astype(jnp.float32)).astype(jnp.bfloat16)

    def core_sum(a, n):
        loads[2 * n + a].wait()
        landed(from_core.at[a, n], core_recv.at[a, n])
        add(part.at[a, n], from_core.at[a, n])

    for n in range(2):
        for a in range(2):
            core_sum(a, n)
            for h, rank in ((0, up_rank), (1, down_rank)):
                send(
                    part.at[a, n, pl.ds(h * half, half)], from_far.at[a, n, h],
                    far_send.at[a, n, h], far_recv.at[a, n, h], rank,
                )
    for n in range(2):
        for a in range(2):
            for j, rank in ((0, up_rank), (1, down_rank)):
                core_sum(a, 2 + 2 * j + n)
                free = 1 - j
                send(
                    part.at[a, 2 + 2 * j + n, pl.ds(free * half, half)],
                    from_near.at[a, n, j, pl.ds(free * half, half)],
                    near_send.at[a, n, j, free], near_recv.at[a, n, j, free], rank,
                )
    for n in range(2):
        for a in range(2):
            for j, rank in ((0, up_rank), (1, down_rank)):
                landed(from_far.at[a, n, j], far_recv.at[a, n, j])
                mine = part.at[a, 2 + 2 * j + n, pl.ds(j * half, half)]
                add(mine, from_far.at[a, n, j])
                send(
                    mine, from_near.at[a, n, j, pl.ds(j * half, half)],
                    near_send.at[a, n, j, j], near_recv.at[a, n, j, j], rank,
                )
    for n in range(2):
        for a in range(2):
            core_sum(a, 6 + n)
            for j in range(2):
                for h in (1 - j, j):
                    landed(from_near.at[a, n, j, pl.ds(h * half, half)], near_recv.at[a, n, j, h])
            total = part[a, 6 + n].astype(jnp.float32)
            total = total + from_near[a, n, 0].astype(jnp.float32)
            total = total + from_near[a, n, 1].astype(jnp.float32)
            part[a, 6 + n] = total.astype(jnp.bfloat16)
            if n == 0:
                send(part.at[a, 6], from_x.at[a], x_send.at[a], x_recv.at[a], x_rank)
    for a, dst in enumerate((key_ref, value_ref)):
        landed(from_x.at[a], x_recv.at[a])
        dst[...] = (part[a, 7].astype(jnp.float32) + from_x[a].astype(jnp.float32)).astype(jnp.bfloat16)
    for a, dst in enumerate((o_ref, q_ref)):
        for d, (dx, dc) in enumerate(((0, 1), (1, 0), (1, 1))):
            tx, tc = (x + dx) % 2, (core + dc) % 2
            landed(dst.at[:, head_cols(tx * 2 + tc)], row_recv.at[a, d])
    for copy in own:
        copy.wait()
    for copy in started:
        copy.wait_send()


def scatter(out_rows, query_rows, key_terms, value_terms, ranks):
    rows, width = out_rows.shape
    shard = rows // GROUP
    half = shard // 2
    bf16 = jnp.bfloat16
    any_spec = pl.BlockSpec(memory_space=pl.ANY)
    vmem_spec = pl.BlockSpec(memory_space=pltpu.VMEM)
    dma = pltpu.SemaphoreType.DMA
    return pl.pallas_call(
        scatter_kernel,
        in_specs=[any_spec] * 4,
        out_specs=[any_spec, any_spec, vmem_spec, vmem_spec],
        out_shape=[
            jax.ShapeDtypeStruct((shard, width * GROUP), bf16),
            jax.ShapeDtypeStruct((shard, width * GROUP), bf16),
            jax.ShapeDtypeStruct((shard, HD), bf16),
            jax.ShapeDtypeStruct((shard, HD), bf16),
        ],
        scratch_shapes=[
            pltpu.VMEM((2, ranks // 2, shard, HD), bf16),
            pltpu.VMEM((2, ranks // 2, shard, HD), bf16),
            pltpu.VMEM((2, 2, 2, half, HD), bf16),
            pltpu.VMEM((2, 2, 2, shard, HD), bf16),
            pltpu.VMEM((2, shard, HD), bf16),
            dma((2,)), dma((2, 8)), dma((2, 8)), dma((2, 8)), dma((2, 2, 2)), dma((2, 2, 2)),
            dma((2, 2, 2, 2)), dma((2, 2, 2, 2)), dma((2,)), dma((2,)), dma((2, 3)), dma((2, 3)),
        ],
        compiler_params=pltpu.CompilerParams(
            collective_id=1, has_side_effects=True, vmem_limit_bytes=40 * 2**20
        ),
        name="scatter",
    )(out_rows, query_rows, key_terms, value_terms)


def body(queries, key_rows, values, out_grad, lengths, block_owner):
    ranks = lax.axis_size("context")
    queries, out_grad, keys, values = gather(queries, out_grad, key_rows, values, ranks)
    out, query_grad, key_terms, value_terms, pair_count = attend(
        queries, out_grad, keys, values, lengths, block_owner
    )
    out, query_grad, key_grad, value_grad = scatter(out, query_grad, key_terms, value_terms, ranks)
    return out, query_grad, key_grad, value_grad, pair_count


def solution(mesh):
    rows = P(("dp", "context"), None)
    return jax.shard_map(
        body,
        mesh=mesh,
        in_specs=(rows, rows, rows, rows, P("dp"), P("dp")),
        out_specs=(rows, rows, rows, rows, P(("dp", "context"))),
        check_vma=False,
    )
```

```python
import functools
import math

import jax
import jax.numpy as jnp
from jax import lax
from jax.experimental import pallas as pl
from jax.experimental.pallas import tpu as pltpu
from jax.sharding import PartitionSpec as P

NEG_FILL = -1e30
MESH = pl.DeviceIdType.MESH
YS = 4
HD = 128
HEADS_HERE = 2
GROUP = 4
TILE = 256
SPAN = 4
PASS = 512
ONES = 16
LARGE = 1e12
QBLOCK = 256
DOC_MAX = 4096


def place():
    me = lax.axis_index("context")
    return me // (2 * YS), (me // 2) % YS, me % 2


def rank_of(x, y, core):
    return (x * YS + y) * 2 + core


def remote(src, dst, send_sem, recv_sem, rank):
    return pltpu.make_async_remote_copy(
        src_ref=src,
        dst_ref=dst,
        send_sem=send_sem,
        recv_sem=recv_sem,
        device_id={"context": rank},
        device_id_type=MESH,
    )


def enter(x, y, core):
    barrier = pltpu.get_barrier_semaphore()
    others = [
        rank_of(x, y, 1 - core),
        rank_of(1 - x, y, core),
        rank_of(x, (y + 1) % YS, core),
        rank_of(x, (y + YS - 1) % YS, core),
    ]
    for other in others:
        pl.semaphore_signal(barrier, inc=1, device_id={"context": other}, device_id_type=MESH)
    pl.semaphore_wait(barrier, len(others))


def rows_at(begin, count):
    return pl.ds(pl.multiple_of(begin, count), count)


def gather_kernel(
    q_ref, g_ref, k_ref, v_ref, rows_ref, ka_ref, va_ref,
    own_sem, kv_send, kv_recv, core_send, core_recv, row_send, row_recv,
):
    x, y, core = place()
    shard = k_ref.shape[0]
    half = shard // 2
    width = q_ref.shape[1] // GROUP
    up, down, far = (y + 1) % YS, (y + YS - 1) % YS, (y + 2) % YS
    x_rank = rank_of(1 - x, y, core)
    core_rank = rank_of(x, y, 1 - core)
    up_rank, down_rank = rank_of(x, up, core), rank_of(x, down, core)
    enter(x, y, core)
    started = []

    def send(src, dst, send_sem, recv_sem, rank):
        copy = remote(src, dst, send_sem, recv_sem, rank)
        copy.start()
        started.append(copy)

    def landed(ref, recv_sem):
        remote(ref, ref, recv_sem, recv_sem, x_rank).wait_recv()

    own = []
    pairs = ((k_ref, ka_ref), (v_ref, va_ref))
    my_rows = rows_at(rank_of(x, y, core) * shard, shard)
    for a, (src, dst) in enumerate(pairs):
        send(src, dst.at[my_rows], kv_send.at[a, 0], kv_recv.at[a, 0], x_rank)
        send(src, dst.at[my_rows], kv_send.at[a, 1], kv_recv.at[a, 1], up_rank)
        send(src, dst.at[my_rows], kv_send.at[a, 2], kv_recv.at[a, 2], down_rank)
        send(src, dst.at[my_rows], core_send.at[a, 0], core_recv.at[a, 0], core_rank)
        copy = pltpu.make_async_copy(src, dst.at[my_rows], own_sem.at[a])
        copy.start()
        own.append(copy)

    for a, src in enumerate((q_ref, g_ref)):
        cols = pl.ds(pl.multiple_of((x * 2 + 1 - core) * width, width), width)
        send(
            src.at[:, cols], rows_ref.at[:, pl.ds(a * width, width)],
            row_send.at[a], row_recv.at[a], core_rank,
        )

    def forward(a, n, ref, rows, rank, relay):
        send(ref.at[rows], ref.at[rows], relay[0].at[a, n], relay[1].at[a, n], rank)

    y_relay, c_relay = (kv_send, kv_recv), (core_send, core_recv)

    def shard_rows(sx, sy, sc):
        return rows_at(rank_of(sx, sy, sc) * shard, shard)

    def half_rows(sx, sy, sc, h):
        return rows_at(rank_of(sx, sy, sc) * shard + h * half, half)

    for a, (_, dst) in enumerate(pairs):
        rows = shard_rows(1 - x, y, core)
        landed(dst.at[rows], kv_recv.at[a, 0])
        forward(a, 3, dst, rows, up_rank, y_relay)
        forward(a, 4, dst, rows, down_rank, y_relay)
        forward(a, 1, dst, rows, core_rank, c_relay)
    for n, sx in ((1, x), (3, 1 - x)):
        for a, (_, dst) in enumerate(pairs):
            landed(dst.at[shard_rows(sx, down, core)], kv_recv.at[a, n])
            forward(a, 4 + n, dst, half_rows(sx, down, core, 0), up_rank, y_relay)
            landed(dst.at[shard_rows(sx, up, core)], kv_recv.at[a, n + 1])
            forward(a, 5 + n, dst, half_rows(sx, up, core, 1), down_rank, y_relay)
            forward(a, 1 + n, dst, shard_rows(sx, down, core), core_rank, c_relay)
            forward(a, 2 + n, dst, shard_rows(sx, up, core), core_rank, c_relay)
    for n, sx in ((1, x), (3, 1 - x)):
        for a, (_, dst) in enumerate(pairs):
            for h in range(2):
                rows = half_rows(sx, far, core, h)
                landed(dst.at[rows], kv_recv.at[a, 4 + n + h])
                forward(a, 5 + n + h, dst, rows, core_rank, c_relay)
    for a, (_, dst) in enumerate(pairs):
        oc = 1 - core
        whole = ((x, y), (1 - x, y), (x, down), (x, up), (1 - x, down), (1 - x, up))
        for n, (sx, sy) in enumerate(whole):
            landed(dst.at[shard_rows(sx, sy, oc)], core_recv.at[a, n])
        for n, sx in ((1, x), (3, 1 - x)):
            for h in range(2):
                landed(dst.at[half_rows(sx, far, oc, h)], core_recv.at[a, 5 + n + h])
    for a in range(2):
        landed(rows_ref.at[:, pl.ds(a * width, width)], row_recv.at[a])
    for copy in own:
        copy.wait()
    for copy in started:
        copy.wait_send()


def gather(queries, out_grad, keys, values, ranks):
    shard, feature = queries.shape
    width = feature // GROUP
    bf16 = jnp.bfloat16
    any_spec = pl.BlockSpec(memory_space=pl.ANY)
    dma = pltpu.SemaphoreType.DMA
    return pl.pallas_call(
        gather_kernel,
        in_specs=[any_spec] * 4,
        out_specs=[any_spec] * 3,
        out_shape=[
            jax.ShapeDtypeStruct((shard, 2 * width), bf16),
            jax.ShapeDtypeStruct((ranks * shard, HD), bf16),
            jax.ShapeDtypeStruct((ranks * shard, HD), bf16),
        ],
        scratch_shapes=[
            dma((2,)), dma((2, 9)), dma((2, 9)), dma((2, 10)), dma((2, 10)), dma((2,)), dma((2,)),
        ],
        compiler_params=pltpu.CompilerParams(collective_id=0, has_side_effects=True, vmem_limit_bytes=62 * 2**20),
        name="gather",
    )(queries, out_grad, keys, values)


def dot(a, b):
    return jnp.dot(a, b, preferred_element_type=jnp.float32)


def attend_kernel(
    second, len_ref, col_ref, *refs,
):
    if second:
        old_dk_ref, old_dv_ref, *refs = refs
    else:
        owner_ref, *refs = refs
    q0_ref, g0_ref, q1_ref, g1_ref, k_ref, v_ref, r0_ref, r1_ref, dk_ref, dv_ref, *refs = refs
    if not second:
        pair_ref, *refs = refs
    attend_block(
        second, len_ref, None if second else owner_ref, (q0_ref, q1_ref), (g0_ref, g1_ref), k_ref, v_ref,
        (r0_ref, r1_ref), dk_ref, dv_ref, None if second else pair_ref,
        (old_dk_ref, old_dv_ref) if second else None, *refs,
    )


def attend_block(
    second, len_ref, owner_ref, q_refs, g_refs, k_ref, v_ref, r_refs, dk_ref, dv_ref, pair_ref, old,
    kt_ref, vt_ref, p_ref, qt_ref, gt_ref, qn_ref, gn_ref, dka_ref, dva_ref, ds_ref, acc_ref,
):
    blk = pl.program_id(0)
    block, width = q_refs[0].shape
    heads = width // HD
    cols = block * heads
    tokens = k_ref.shape[0]
    docs = len_ref.shape[0]
    f32, bf16 = jnp.float32, jnp.bfloat16
    scale = 1.0 / math.sqrt(HD)
    scale2 = scale * math.log2(math.e)
    x, y, core = place()
    if second:
        x = 1 - x
    per_chip = tokens // (2 * YS)
    per_core = pl.num_programs(0) // 2
    chip_first = (x * YS + y) * per_chip
    chip_start, end = jnp.int32(0), jnp.int32(0)
    for d in range(docs):
        end = end + len_ref[d]
        chip_start = jnp.where(chip_first >= end, end, chip_start)
    chunk_low = lax.div(chip_start, PASS)
    chunk_high = lax.div(chip_first + per_chip, PASS)

    @pl.when(blk == 0)
    def _():
        def prepare(i, carry):
            rows = rows_at(i * PASS, PASS)
            kt_ref[:, rows] = k_ref[rows, :].T
            vt_ref[0:HD, rows] = v_ref[rows, :].T
            vt_ref[HD:, rows] = jnp.ones((ONES, PASS), bf16)
            dka_ref[rows, :] = jnp.zeros((PASS, HD), f32)
            dva_ref[rows, :] = jnp.zeros((PASS, HD), f32)
            return carry

        lax.fori_loop(chunk_low, chunk_high, prepare, 0)
        if not second:
            blocks = owner_ref.shape[1]
            block_rows = tokens // blocks
            shape = (block_rows, blocks)
            pos = lax.broadcasted_iota(jnp.int32, shape, 1) * block_rows
            pos = pos + lax.broadcasted_iota(jnp.int32, shape, 0)
            begin, end = jnp.zeros(shape, jnp.int32), jnp.int32(0)
            for d in range(docs):
                end = end + len_ref[d]
                begin = jnp.where(pos >= end, end, begin)
            counts = (pos - begin + 1).astype(f32)
            counts = jnp.where(owner_ref[...] == lax.axis_index("context"), counts, 0.0)
            pair_ref[0] = jnp.sum(counts)

    half = lax.div(blk, per_core)
    row_core = jnp.where(half == 0, core, 1 - core)
    first = chip_first + row_core * (per_chip // 2) + lax.rem(blk, per_core) * block
    row_pos = first + lax.rem(lax.broadcasted_iota(jnp.int32, (1, cols), 1), block)
    row_start = jnp.zeros((1, cols), jnp.int32)
    first_start, last_start, end = jnp.int32(0), jnp.int32(0), jnp.int32(0)
    for d in range(docs):
        end = end + len_ref[d]
        row_start = jnp.where(row_pos >= end, end, row_start)
        first_start = jnp.where(first >= end, end, first_start)
        last_start = jnp.where(first + block - 1 >= end, end, last_start)
    low = lax.div(first_start, TILE)
    high = lax.div(first + block - 1, TILE) + 1

    own_keys = kt_ref[:, rows_at(first, block)].astype(f32)
    shift = []
    for h in range(heads):
        for n in range(2):

            @pl.when(half == n)
            def _(n=n, h=h):
                qt_ref[:, h * block : (h + 1) * block] = q_refs[n][:, h * HD : (h + 1) * HD].T
                gt_ref[:, h * block : (h + 1) * block] = g_refs[n][:, h * HD : (h + 1) * HD].T

        q_t = qt_ref[:, h * block : (h + 1) * block]
        shift.append(jnp.sum(q_t.astype(f32) * own_keys, axis=0, keepdims=True) * scale2)
    shift = jnp.concatenate(shift, axis=1)

    def keep(result, at):
        for n in range(2):

            @pl.when(half == n)
            def _(n=n):
                for h in range(heads):
                    cut = result[h * block : (h + 1) * block, :]
                    r_refs[n][:, (at + h) * HD : (at + h + 1) * HD] = cut

    def key_rows(t, count):
        return pl.ds(pl.multiple_of(t * TILE, TILE), count)

    def kept_rows(t, count):
        return pl.ds(pl.multiple_of((t - low) * TILE, TILE), count)

    def sweep(piece):
        count = high - low
        groups = lax.div(count, SPAN)

        def one(g, carry):
            piece(low + g * SPAN, SPAN * TILE, False)
            return carry

        lax.fori_loop(0, groups, one, 0)
        at = low + groups * SPAN
        size = SPAN // 2
        while size:
            has = lax.rem(lax.div(count, size), 2)

            @pl.when(has == 1)
            def _(at=at, size=size):
                piece(at, size * TILE, True)

            at = at + has * size
            size //= 2

    def forward(shift):
        acc_ref[...] = jnp.zeros(acc_ref.shape, f32)

        def piece(t, rows, last):
            def run(mask):
                acc = None
                part = min(rows, PASS)
                for i in range(0, rows, part):
                    tile = t + i // TILE
                    s = dot(k_ref[key_rows(tile, part), :], qt_ref[...]) * scale2 - shift
                    if mask:
                        pos = t * TILE + i + lax.broadcasted_iota(jnp.int32, s.shape, 0)
                        s = jnp.where((pos >= row_start) & (pos <= row_pos), s, NEG_FILL)
                    p_ref[kept_rows(tile, part), :] = jnp.exp2(s).astype(bf16)
                    term = dot(vt_ref[:, key_rows(tile, part)], p_ref[kept_rows(tile, part), :])
                    acc = term if acc is None else acc + term
                acc_ref[...] += acc

            if last:
                run(True)
            else:
                edge = (t * TILE < last_start) | (t * TILE + rows - 1 > first)
                pl.when(edge)(lambda: run(True))
                pl.when(jnp.logical_not(edge))(lambda: run(False))

        sweep(piece)

    forward(shift)

    @pl.when(jnp.logical_not(jnp.max(acc_ref[HD : HD + 1, :]) < LARGE))
    def _():
        def peak_pass(t, peak):
            s = dot(k_ref[key_rows(t, TILE), :], qt_ref[...]) * scale2
            pos = t * TILE + lax.broadcasted_iota(jnp.int32, s.shape, 0)
            s = jnp.where((pos >= row_start) & (pos <= row_pos), s, NEG_FILL)
            return jnp.maximum(peak, jnp.max(s.reshape(TILE // 8, 8, cols), axis=0))

        peak = lax.fori_loop(low, high, peak_pass, jnp.full((8, cols), NEG_FILL, f32))
        forward(jnp.max(peak, axis=0, keepdims=True))

    inverse = 1.0 / acc_ref[HD : HD + 1, :]
    out = (acc_ref[0:HD, :] * inverse).astype(bf16)
    grad_t = gt_ref[...].astype(f32)
    grad_dot = jnp.sum(out.astype(f32) * grad_t, axis=0, keepdims=True)
    gn_ref[...] = (grad_t * inverse).astype(bf16).T
    qn_ref[...] = (qt_ref[...].astype(f32) * inverse).astype(bf16).T
    keep(out.T, 0)
    acc_ref[0:HD, :] = jnp.zeros((HD, cols), f32)

    def backward(t, rows, last):
        keys, kept = key_rows(t, rows), kept_rows(t, rows)
        grad_p = dot(v_ref[keys, :], gt_ref[...])
        ds_ref[0:rows, :] = (p_ref[kept, :].astype(f32) * (grad_p - grad_dot)).astype(bf16)
        dva_ref[keys, :] += dot(p_ref[kept, :], gn_ref[...])
        dka_ref[keys, :] += dot(ds_ref[0:rows, :], qn_ref[...])
        acc_ref[0:HD, :] += dot(kt_ref[:, keys], ds_ref[0:rows, :])

    sweep(backward)
    query_grad = (acc_ref[0:HD, :] * (inverse * scale)).astype(bf16).T
    keep(query_grad, heads)

    @pl.when(blk == pl.num_programs(0) - 1)
    def _():
        def finish(i, carry):
            rows = rows_at(i * PASS, PASS)
            inside = (i >= chunk_low) & (i < chunk_high)
            for n, (sums, out_ref, factor) in enumerate(((dka_ref, dk_ref, scale), (dva_ref, dv_ref, 1.0))):

                @pl.when(inside)
                def _(n=n, sums=sums, out_ref=out_ref, factor=factor):
                    total = sums[rows, :] * factor
                    if second:
                        total = total + old[n][rows, :].astype(f32)
                    out_ref[rows, :] = total.astype(bf16)

                @pl.when(jnp.logical_not(inside))
                def _(n=n, out_ref=out_ref):
                    out_ref[rows, :] = old[n][rows, :] if second else jnp.zeros((PASS, HD), bf16)

            return carry

        lax.fori_loop(0, tokens // PASS, finish, 0)


def attend(rows, cols, keys, values, lengths, block_owner=None, old=None):
    second = old is not None
    tokens = keys.shape[0]
    shard = rows[0].shape[0]
    per_core = shard // QBLOCK
    width = HEADS_HERE * HD
    span = ((DOC_MAX + QBLOCK + TILE - 2) // TILE + 1) * TILE
    qcols = QBLOCK * HEADS_HERE

    def own(i):
        return jnp.minimum(i, per_core - 1)

    def other(i):
        return jnp.maximum(i - per_core, 0)

    def row_spec(n):
        where = own if n < 2 else other
        return pl.BlockSpec((QBLOCK, width), lambda i, _, col: (where(i), col[n]))

    full_spec = pl.BlockSpec((tokens, HD), lambda i, *_: (0, 0))
    bf16, f32 = jnp.bfloat16, jnp.float32
    if second:
        extra, extra_specs = list(old), [full_spec] * 2
    else:
        extra = [block_owner.reshape(1, -1)]
        extra_specs = [pl.BlockSpec((1, block_owner.shape[0]), lambda i, *_: (0, 0))]
    out_specs = [
        pl.BlockSpec((QBLOCK, 2 * width), lambda i, *_: (own(i), 0)),
        pl.BlockSpec((QBLOCK, 2 * width), lambda i, *_: (other(i), 0)),
        full_spec, full_spec,
    ]
    out_shape = [
        jax.ShapeDtypeStruct((shard, 2 * width), bf16),
        jax.ShapeDtypeStruct((shard, 2 * width), bf16),
        jax.ShapeDtypeStruct((tokens, HD), bf16),
        jax.ShapeDtypeStruct((tokens, HD), bf16),
    ]
    if not second:
        out_specs.append(pl.BlockSpec(memory_space=pltpu.SMEM))
        out_shape.append(jax.ShapeDtypeStruct((1,), f32))
    return pl.pallas_call(
        functools.partial(attend_kernel, second),
        grid_spec=pltpu.PrefetchScalarGridSpec(
            num_scalar_prefetch=2,
            grid=(2 * per_core,),
            in_specs=extra_specs + [row_spec(n) for n in range(4)] + [full_spec, full_spec],
            out_specs=out_specs,
            scratch_shapes=[
                pltpu.VMEM((HD, tokens), bf16),
                pltpu.VMEM((HD + ONES, tokens), bf16),
                pltpu.VMEM((span, qcols), bf16),
                pltpu.VMEM((HD, qcols), bf16),
                pltpu.VMEM((HD, qcols), bf16),
                pltpu.VMEM((qcols, HD), bf16),
                pltpu.VMEM((qcols, HD), bf16),
                pltpu.VMEM((tokens, HD), f32),
                pltpu.VMEM((tokens, HD), f32),
                pltpu.VMEM((SPAN * TILE, qcols), bf16),
                pltpu.VMEM((HD + ONES, qcols), f32),
            ],
        ),
        out_shape=out_shape,
        cost_estimate=pl.CostEstimate(flops=2 * 10**10, bytes_accessed=2 * 10**7, transcendentals=5 * 10**6),
        compiler_params=pltpu.CompilerParams(vmem_limit_bytes=62 * 2**20),
        name="attend_far" if second else "attend_near",
    )(lengths, cols, *extra, *rows, keys, values)


def scatter_kernel(
    dk_ref, dv_ref, rows_ref, back_ref, key_ref, value_ref,
    part, from_core, from_far, from_near, from_x,
    part_sem, core_send, core_recv, far_send, far_recv, near_send, near_recv,
    x_send, x_recv, row_send, row_recv,
):
    x, y, core = place()
    shard = key_ref.shape[0]
    half = shard // 2
    up, down, far = (y + 1) % YS, (y + YS - 1) % YS, (y + 2) % YS
    x_rank = rank_of(1 - x, y, core)
    core_rank = rank_of(x, y, 1 - core)
    up_rank, down_rank = rank_of(x, up, core), rank_of(x, down, core)
    started = []

    def send(src, dst, send_sem, recv_sem, rank):
        copy = remote(src, dst, send_sem, recv_sem, rank)
        copy.start()
        started.append(copy)

    def landed(ref, recv_sem):
        remote(ref, ref, recv_sem, recv_sem, x_rank).wait_recv()

    pairs = (dk_ref, dv_ref)
    order = [(1 - x, far), (x, far), (1 - x, up), (x, up), (1 - x, down), (x, down), (1 - x, y), (x, y)]
    loads = []
    for n, (sx, sy) in enumerate(order):
        for a, src in enumerate(pairs):
            rows = rows_at(rank_of(sx, sy, core) * shard, shard)
            copy = pltpu.make_async_copy(src.at[rows], part.at[a, n], part_sem.at[a, n])
            copy.start()
            loads.append(copy)
    enter(x, y, core)
    for n, (sx, sy) in enumerate(order):
        for a, src in enumerate(pairs):
            rows = rows_at(rank_of(sx, sy, 1 - core) * shard, shard)
            send(src.at[rows], from_core.at[a, n], core_send.at[a, n], core_recv.at[a, n], core_rank)

    send(rows_ref, back_ref, row_send, row_recv, core_rank)

    def add(ref, other):
        ref[...] = (ref[...].astype(jnp.float32) + other[...].astype(jnp.float32)).astype(jnp.bfloat16)

    def core_sum(a, n):
        loads[2 * n + a].wait()
        landed(from_core.at[a, n], core_recv.at[a, n])
        add(part.at[a, n], from_core.at[a, n])

    for n in range(2):
        for a in range(2):
            core_sum(a, n)
            for h, rank in ((0, up_rank), (1, down_rank)):
                send(
                    part.at[a, n, pl.ds(h * half, half)], from_far.at[a, n, h],
                    far_send.at[a, n, h], far_recv.at[a, n, h], rank,
                )
    for n in range(2):
        for a in range(2):
            for j, rank in ((0, up_rank), (1, down_rank)):
                core_sum(a, 2 + 2 * j + n)
                free = 1 - j
                send(
                    part.at[a, 2 + 2 * j + n, pl.ds(free * half, half)],
                    from_near.at[a, n, j, pl.ds(free * half, half)],
                    near_send.at[a, n, j, free], near_recv.at[a, n, j, free], rank,
                )
    for n in range(2):
        for a in range(2):
            for j, rank in ((0, up_rank), (1, down_rank)):
                landed(from_far.at[a, n, j], far_recv.at[a, n, j])
                mine = part.at[a, 2 + 2 * j + n, pl.ds(j * half, half)]
                add(mine, from_far.at[a, n, j])
                send(
                    mine, from_near.at[a, n, j, pl.ds(j * half, half)],
                    near_send.at[a, n, j, j], near_recv.at[a, n, j, j], rank,
                )
    for n in range(2):
        for a in range(2):
            core_sum(a, 6 + n)
            for j in range(2):
                for h in (1 - j, j):
                    landed(from_near.at[a, n, j, pl.ds(h * half, half)], near_recv.at[a, n, j, h])
            total = part[a, 6 + n].astype(jnp.float32)
            total = total + from_near[a, n, 0].astype(jnp.float32)
            total = total + from_near[a, n, 1].astype(jnp.float32)
            part[a, 6 + n] = total.astype(jnp.bfloat16)
            if n == 0:
                send(part.at[a, 6], from_x.at[a], x_send.at[a], x_recv.at[a], x_rank)
    for a, dst in enumerate((key_ref, value_ref)):
        landed(from_x.at[a], x_recv.at[a])
        dst[...] = (part[a, 7].astype(jnp.float32) + from_x[a].astype(jnp.float32)).astype(jnp.bfloat16)
    landed(back_ref, row_recv)
    for copy in started:
        copy.wait_send()


def scatter(key_terms, value_terms, rows, ranks):
    tokens = key_terms.shape[0]
    shard = tokens // ranks
    half = shard // 2
    bf16 = jnp.bfloat16
    any_spec = pl.BlockSpec(memory_space=pl.ANY)
    vmem_spec = pl.BlockSpec(memory_space=pltpu.VMEM)
    dma = pltpu.SemaphoreType.DMA
    return pl.pallas_call(
        scatter_kernel,
        in_specs=[any_spec] * 3,
        out_specs=[any_spec, vmem_spec, vmem_spec],
        out_shape=[
            jax.ShapeDtypeStruct(rows.shape, bf16),
            jax.ShapeDtypeStruct((shard, HD), bf16),
            jax.ShapeDtypeStruct((shard, HD), bf16),
        ],
        scratch_shapes=[
            pltpu.VMEM((2, ranks // 2, shard, HD), bf16),
            pltpu.VMEM((2, ranks // 2, shard, HD), bf16),
            pltpu.VMEM((2, 2, 2, half, HD), bf16),
            pltpu.VMEM((2, 2, 2, shard, HD), bf16),
            pltpu.VMEM((2, shard, HD), bf16),
            dma((2, 8)), dma((2, 8)), dma((2, 8)), dma((2, 2, 2)), dma((2, 2, 2)),
            dma((2, 2, 2, 2)), dma((2, 2, 2, 2)), dma((2,)), dma((2,)), dma, dma,
        ],
        cost_estimate=pl.CostEstimate(flops=2 * 10**7, bytes_accessed=2 * 10**7, transcendentals=0),
        compiler_params=pltpu.CompilerParams(
            collective_id=1, has_side_effects=True, vmem_limit_bytes=62 * 2**20
        ),
        name="scatter",
    )(key_terms, value_terms, rows)


def place_kernel(a_ref, b_ref, c_ref, d_ref, o_ref, q_ref, sem):
    x, _, core = place()
    width = a_ref.shape[1] // 2
    copies = []
    for n, (ref, slot) in enumerate((
        (a_ref, x * 2 + core), (b_ref, x * 2 + 1 - core),
        (c_ref, (1 - x) * 2 + core), (d_ref, (1 - x) * 2 + 1 - core),
    )):
        cols = pl.ds(pl.multiple_of(slot * width, width), width)
        for a, dst in enumerate((o_ref, q_ref)):
            copy = pltpu.make_async_copy(ref.at[:, pl.ds(a * width, width)], dst.at[:, cols], sem.at[n, a])
            copy.start()
            copies.append(copy)
    for copy in copies:
        copy.wait()


def place_columns(pieces):
    shard, width = pieces[0].shape
    shape = jax.ShapeDtypeStruct((shard, width * 2), jnp.bfloat16)
    any_spec = pl.BlockSpec(memory_space=pl.ANY)
    return pl.pallas_call(
        place_kernel,
        in_specs=[any_spec] * 4,
        out_specs=[any_spec] * 2,
        out_shape=[shape, shape],
        scratch_shapes=[pltpu.SemaphoreType.DMA((4, 2))],
        compiler_params=pltpu.CompilerParams(vmem_limit_bytes=62 * 2**20),
        name="place",
    )(*pieces)


def body(queries, key_rows, values, out_grad, lengths, block_owner):
    ranks = lax.axis_size("context")
    x, _, core = place()
    width = queries.shape[1] // GROUP
    same = [(rank_of(a, b, c), rank_of(1 - a, b, c)) for a in range(2) for b in range(YS) for c in range(2)]
    cross = [(rank_of(a, b, c), rank_of(1 - a, b, 1 - c)) for a in range(2) for b in range(YS) for c in range(2)]

    def heads_of(slot):
        cut = [lax.dynamic_slice_in_dim(t, slot * width, width, 1) for t in (queries, out_grad)]
        return jnp.concatenate(cut, axis=1)

    far_same = lax.ppermute(heads_of((1 - x) * 2 + core), "context", same)
    far_cross = lax.ppermute(heads_of((1 - x) * 2 + 1 - core), "context", cross)
    near, keys, all_values = gather(queries, out_grad, key_rows, values, ranks)
    slot = (x * 2 + core).astype(jnp.int32)
    zero, one = jnp.int32(0), jnp.int32(1)
    own_rows, near_rows, dk, dv, pair_count = attend(
        (queries, out_grad, near, near), jnp.stack([slot, slot, zero, one]), keys, all_values, lengths,
        block_owner=block_owner,
    )
    same_rows, cross_rows, dk, dv = attend(
        (far_same, far_same, far_cross, far_cross), jnp.stack([zero, one, zero, one]), keys, all_values, lengths,
        old=(dk, dv),
    )
    same_rows = lax.ppermute(same_rows, "context", same)
    cross_rows = lax.ppermute(cross_rows, "context", cross)
    near_rows, key_grad, value_grad = scatter(dk, dv, near_rows, ranks)
    out, query_grad = place_columns((own_rows, near_rows, same_rows, cross_rows))
    return out, query_grad, key_grad, value_grad, pair_count


def solution(mesh):
    rows = P(("dp", "context"), None)
    return jax.shard_map(
        body,
        mesh=mesh,
        in_specs=(rows, rows, rows, rows, P("dp"), P("dp")),
        out_specs=(rows, rows, rows, rows, P(("dp", "context"))),
        check_vma=False,
    )
```

```python
import functools
import math

import jax
import jax.numpy as jnp
from jax import lax
from jax.experimental import pallas as pl
from jax.experimental.pallas import tpu as pltpu
from jax.sharding import PartitionSpec as P

NEG_FILL = -1e30
MESH = pl.DeviceIdType.MESH
YS = 4
HD = 128
HEADS_HERE = 2
GROUP = 4
TILE = 256
SPAN = 4
PASS = 512
ONES = 16
LARGE = 1e12
QBLOCK = 256
DOC_MAX = 4096


def place():
    me = lax.axis_index("context")
    return me // (2 * YS), (me // 2) % YS, me % 2


def rank_of(x, y, core):
    return (x * YS + y) * 2 + core


def remote(src, dst, send_sem, recv_sem, rank):
    return pltpu.make_async_remote_copy(
        src_ref=src,
        dst_ref=dst,
        send_sem=send_sem,
        recv_sem=recv_sem,
        device_id={"context": rank},
        device_id_type=MESH,
    )


def enter(x, y, core, rows=False):
    barrier = pltpu.get_barrier_semaphore()
    others = [
        rank_of(x, y, 1 - core),
        rank_of(1 - x, y, core),
        rank_of(x, (y + 1) % YS, core),
        rank_of(x, (y + YS - 1) % YS, core),
    ]
    if rows:
        others.append(rank_of(1 - x, y, 1 - core))
    for other in others:
        pl.semaphore_signal(barrier, inc=1, device_id={"context": other}, device_id_type=MESH)
    pl.semaphore_wait(barrier, len(others))


def rows_at(begin, count):
    return pl.ds(pl.multiple_of(begin, count), count)


def gather_kernel(
    q_ref, g_ref, k_ref, v_ref, rows_ref, ka_ref, va_ref,
    own_sem, kv_send, kv_recv, core_send, core_recv, row_send, row_recv,
):
    x, y, core = place()
    shard = k_ref.shape[0]
    half = shard // 2
    width = q_ref.shape[1] // GROUP
    up, down, far = (y + 1) % YS, (y + YS - 1) % YS, (y + 2) % YS
    x_rank = rank_of(1 - x, y, core)
    core_rank = rank_of(x, y, 1 - core)
    up_rank, down_rank = rank_of(x, up, core), rank_of(x, down, core)
    enter(x, y, core, rows=True)
    started = []

    def send(src, dst, send_sem, recv_sem, rank):
        copy = remote(src, dst, send_sem, recv_sem, rank)
        copy.start()
        started.append(copy)

    def landed(ref, recv_sem):
        remote(ref, ref, recv_sem, recv_sem, x_rank).wait_recv()

    own = []
    pairs = ((k_ref, ka_ref), (v_ref, va_ref))
    my_rows = rows_at(rank_of(x, y, core) * shard, shard)
    for a, (src, dst) in enumerate(pairs):
        send(src, dst.at[my_rows], kv_send.at[a, 0], kv_recv.at[a, 0], x_rank)
        send(src, dst.at[my_rows], kv_send.at[a, 1], kv_recv.at[a, 1], up_rank)
        send(src, dst.at[my_rows], kv_send.at[a, 2], kv_recv.at[a, 2], down_rank)
        send(src, dst.at[my_rows], core_send.at[a, 0], core_recv.at[a, 0], core_rank)
        copy = pltpu.make_async_copy(src, dst.at[my_rows], own_sem.at[a])
        copy.start()
        own.append(copy)

    for a, src in enumerate((q_ref, g_ref)):
        for d in range(1, GROUP):
            tx, tc = (x + d // 2) % 2, (core + d % 2) % 2
            cols = pl.ds(pl.multiple_of((tx * 2 + tc) * width, width), width)
            send(
                src.at[:, cols], rows_ref.at[pl.ds((d - 1) * shard, shard), pl.ds(a * width, width)],
                row_send.at[a, d - 1], row_recv.at[a, d - 1], rank_of(tx, y, tc),
            )

    def forward(a, n, ref, rows, rank, relay):
        send(ref.at[rows], ref.at[rows], relay[0].at[a, n], relay[1].at[a, n], rank)

    y_relay, c_relay = (kv_send, kv_recv), (core_send, core_recv)

    def shard_rows(sx, sy, sc):
        return rows_at(rank_of(sx, sy, sc) * shard, shard)

    def half_rows(sx, sy, sc, h):
        return rows_at(rank_of(sx, sy, sc) * shard + h * half, half)

    for a, (_, dst) in enumerate(pairs):
        rows = shard_rows(1 - x, y, core)
        landed(dst.at[rows], kv_recv.at[a, 0])
        forward(a, 3, dst, rows, up_rank, y_relay)
        forward(a, 4, dst, rows, down_rank, y_relay)
        forward(a, 1, dst, rows, core_rank, c_relay)
    for n, sx in ((1, x), (3, 1 - x)):
        for a, (_, dst) in enumerate(pairs):
            landed(dst.at[shard_rows(sx, down, core)], kv_recv.at[a, n])
            forward(a, 4 + n, dst, half_rows(sx, down, core, 0), up_rank, y_relay)
            landed(dst.at[shard_rows(sx, up, core)], kv_recv.at[a, n + 1])
            forward(a, 5 + n, dst, half_rows(sx, up, core, 1), down_rank, y_relay)
            forward(a, 1 + n, dst, shard_rows(sx, down, core), core_rank, c_relay)
            forward(a, 2 + n, dst, shard_rows(sx, up, core), core_rank, c_relay)
    for n, sx in ((1, x), (3, 1 - x)):
        for a, (_, dst) in enumerate(pairs):
            for h in range(2):
                rows = half_rows(sx, far, core, h)
                landed(dst.at[rows], kv_recv.at[a, 4 + n + h])
                forward(a, 5 + n + h, dst, rows, core_rank, c_relay)
    for a, (_, dst) in enumerate(pairs):
        oc = 1 - core
        whole = ((x, y), (1 - x, y), (x, down), (x, up), (1 - x, down), (1 - x, up))
        for n, (sx, sy) in enumerate(whole):
            landed(dst.at[shard_rows(sx, sy, oc)], core_recv.at[a, n])
        for n, sx in ((1, x), (3, 1 - x)):
            for h in range(2):
                landed(dst.at[half_rows(sx, far, oc, h)], core_recv.at[a, 5 + n + h])
    for a in range(2):
        for d in range(1, GROUP):
            landed(rows_ref.at[pl.ds((d - 1) * shard, shard), pl.ds(a * width, width)], row_recv.at[a, d - 1])
    for copy in own:
        copy.wait()
    for copy in started:
        copy.wait_send()


def gather(queries, out_grad, keys, values, ranks):
    shard, feature = queries.shape
    width = feature // GROUP
    bf16 = jnp.bfloat16
    any_spec = pl.BlockSpec(memory_space=pl.ANY)
    dma = pltpu.SemaphoreType.DMA
    return pl.pallas_call(
        gather_kernel,
        in_specs=[any_spec] * 4,
        out_specs=[any_spec] * 3,
        out_shape=[
            jax.ShapeDtypeStruct(((GROUP - 1) * shard, 2 * width), bf16),
            jax.ShapeDtypeStruct((ranks * shard, HD), bf16),
            jax.ShapeDtypeStruct((ranks * shard, HD), bf16),
        ],
        scratch_shapes=[
            dma((2,)), dma((2, 9)), dma((2, 9)), dma((2, 10)), dma((2, 10)), dma((2, 3)), dma((2, 3)),
        ],
        compiler_params=pltpu.CompilerParams(collective_id=0, has_side_effects=True, vmem_limit_bytes=62 * 2**20),
        name="gather",
    )(queries, out_grad, keys, values)


def dot(a, b):
    return jnp.dot(a, b, preferred_element_type=jnp.float32)


def attend_kernel(
    len_ref, slot_ref, owner_ref, q0_ref, g0_ref, q1_ref, g1_ref, k_ref, v_ref,
    r0_ref, r1_ref, r2_ref, r3_ref, dk_ref, dv_ref, pair_ref,
    kt_ref, vt_ref, p_ref, qt_ref, gt_ref, qn_ref, gn_ref, dka_ref, dva_ref, ds_ref, acc_ref,
):
    blk = pl.program_id(0)
    q_refs, g_refs, r_refs = (q0_ref, q1_ref), (g0_ref, g1_ref), (r0_ref, r1_ref, r2_ref, r3_ref)
    block, width = q0_ref.shape
    heads = width // HD
    cols = block * heads
    tokens = k_ref.shape[0]
    docs = len_ref.shape[0]
    f32, bf16 = jnp.float32, jnp.bfloat16
    scale = 1.0 / math.sqrt(HD)
    scale2 = scale * math.log2(math.e)
    x, y, core = place()
    per_chip = tokens // (2 * YS)
    per_core = pl.num_programs(0) // GROUP

    reach = []
    for chip in (y, YS + y):
        begin, end = jnp.int32(0), jnp.int32(0)
        for d in range(docs):
            end = end + len_ref[d]
            begin = jnp.where(chip * per_chip >= end, end, begin)
        reach.append((lax.div(begin, PASS), lax.div((chip + 1) * per_chip, PASS)))
    reach[1] = (jnp.maximum(reach[1][0], reach[0][1]), reach[1][1])

    @pl.when(blk == 0)
    def _():
        def prepare(i, carry):
            rows = rows_at(i * PASS, PASS)
            kt_ref[:, rows] = k_ref[rows, :].T
            vt_ref[0:HD, rows] = v_ref[rows, :].T
            vt_ref[HD:, rows] = jnp.ones((ONES, PASS), bf16)
            dka_ref[rows, :] = jnp.zeros((PASS, HD), f32)
            dva_ref[rows, :] = jnp.zeros((PASS, HD), f32)
            return carry

        for low_chunk, high_chunk in reach:
            lax.fori_loop(low_chunk, high_chunk, prepare, 0)
        blocks = owner_ref.shape[1]
        block_rows = tokens // blocks
        shape = (block_rows, blocks)
        pos = lax.broadcasted_iota(jnp.int32, shape, 1) * block_rows
        pos = pos + lax.broadcasted_iota(jnp.int32, shape, 0)
        begin, end = jnp.zeros(shape, jnp.int32), jnp.int32(0)
        for d in range(docs):
            end = end + len_ref[d]
            begin = jnp.where(pos >= end, end, begin)
        counts = (pos - begin + 1).astype(f32)
        counts = jnp.where(owner_ref[...] == lax.axis_index("context"), counts, 0.0)
        pair_ref[0] = jnp.sum(counts)

    part = lax.div(blk, per_core)
    chip = lax.rem(x + lax.div(part, 2), 2) * YS + y
    row_core = lax.rem(core + part, 2)
    first = chip * per_chip + row_core * (per_chip // 2) + lax.rem(blk, per_core) * block
    row_pos = first + lax.rem(lax.broadcasted_iota(jnp.int32, (1, cols), 1), block)
    row_start = jnp.zeros((1, cols), jnp.int32)
    first_start, last_start, end = jnp.int32(0), jnp.int32(0), jnp.int32(0)
    for d in range(docs):
        end = end + len_ref[d]
        row_start = jnp.where(row_pos >= end, end, row_start)
        first_start = jnp.where(first >= end, end, first_start)
        last_start = jnp.where(first + block - 1 >= end, end, last_start)
    low = lax.div(first_start, TILE)
    high = lax.div(first + block - 1, TILE) + 1

    own_keys = kt_ref[:, rows_at(first, block)].astype(f32)
    shift = []
    for h in range(heads):
        for n in range(2):

            @pl.when((part > 0) == bool(n))
            def _(n=n, h=h):
                qt_ref[:, h * block : (h + 1) * block] = q_refs[n][:, h * HD : (h + 1) * HD].T
                gt_ref[:, h * block : (h + 1) * block] = g_refs[n][:, h * HD : (h + 1) * HD].T

        q_t = qt_ref[:, h * block : (h + 1) * block]
        shift.append(jnp.sum(q_t.astype(f32) * own_keys, axis=0, keepdims=True) * scale2)
    shift = jnp.concatenate(shift, axis=1)

    def keep(result, at):
        for n in range(GROUP):

            @pl.when(part == n)
            def _(n=n):
                for h in range(heads):
                    cut = result[h * block : (h + 1) * block, :]
                    r_refs[n][:, (at + h) * HD : (at + h + 1) * HD] = cut

    def key_rows(t, count):
        return pl.ds(pl.multiple_of(t * TILE, TILE), count)

    def kept_rows(t, count):
        return pl.ds(pl.multiple_of((t - low) * TILE, TILE), count)

    def sweep(piece):
        count = high - low
        groups = lax.div(count, SPAN)

        def one(g, carry):
            piece(low + g * SPAN, SPAN * TILE, False)
            return carry

        lax.fori_loop(0, groups, one, 0)
        at = low + groups * SPAN
        size = SPAN // 2
        while size:
            has = lax.rem(lax.div(count, size), 2)

            @pl.when(has == 1)
            def _(at=at, size=size):
                piece(at, size * TILE, True)

            at = at + has * size
            size //= 2

    def forward(shift):
        acc_ref[...] = jnp.zeros(acc_ref.shape, f32)

        def piece(t, rows, last):
            def run(mask):
                acc = None
                part = min(rows, PASS)
                for i in range(0, rows, part):
                    tile = t + i // TILE
                    s = dot(k_ref[key_rows(tile, part), :], qt_ref[...]) * scale2 - shift
                    if mask:
                        pos = t * TILE + i + lax.broadcasted_iota(jnp.int32, s.shape, 0)
                        s = jnp.where((pos >= row_start) & (pos <= row_pos), s, NEG_FILL)
                    p_ref[kept_rows(tile, part), :] = jnp.exp2(s).astype(bf16)
                    term = dot(vt_ref[:, key_rows(tile, part)], p_ref[kept_rows(tile, part), :])
                    acc = term if acc is None else acc + term
                acc_ref[...] += acc

            if last:
                run(True)
            else:
                edge = (t * TILE < last_start) | (t * TILE + rows - 1 > first)
                pl.when(edge)(lambda: run(True))
                pl.when(jnp.logical_not(edge))(lambda: run(False))

        sweep(piece)

    forward(shift)

    @pl.when(jnp.logical_not(jnp.max(acc_ref[HD : HD + 1, :]) < LARGE))
    def _():
        def peak_pass(t, peak):
            s = dot(k_ref[key_rows(t, TILE), :], qt_ref[...]) * scale2
            pos = t * TILE + lax.broadcasted_iota(jnp.int32, s.shape, 0)
            s = jnp.where((pos >= row_start) & (pos <= row_pos), s, NEG_FILL)
            return jnp.maximum(peak, jnp.max(s.reshape(TILE // 8, 8, cols), axis=0))

        peak = lax.fori_loop(low, high, peak_pass, jnp.full((8, cols), NEG_FILL, f32))
        forward(jnp.max(peak, axis=0, keepdims=True))

    inverse = 1.0 / acc_ref[HD : HD + 1, :]
    out = (acc_ref[0:HD, :] * inverse).astype(bf16)
    grad_t = gt_ref[...].astype(f32)
    grad_dot = jnp.sum(out.astype(f32) * grad_t, axis=0, keepdims=True)
    gn_ref[...] = (grad_t * inverse).astype(bf16).T
    qn_ref[...] = (qt_ref[...].astype(f32) * inverse).astype(bf16).T
    keep(out.T, 0)
    acc_ref[0:HD, :] = jnp.zeros((HD, cols), f32)

    def backward(t, rows, last):
        keys, kept = key_rows(t, rows), kept_rows(t, rows)
        grad_p = dot(v_ref[keys, :], gt_ref[...])
        ds_ref[0:rows, :] = (p_ref[kept, :].astype(f32) * (grad_p - grad_dot)).astype(bf16)
        dva_ref[keys, :] += dot(p_ref[kept, :], gn_ref[...])
        dka_ref[keys, :] += dot(ds_ref[0:rows, :], qn_ref[...])
        acc_ref[0:HD, :] += dot(kt_ref[:, keys], ds_ref[0:rows, :])

    sweep(backward)
    query_grad = (acc_ref[0:HD, :] * (inverse * scale)).astype(bf16).T
    keep(query_grad, heads)

    @pl.when(blk == pl.num_programs(0) - 1)
    def _():
        def finish(i, carry):
            rows = rows_at(i * PASS, PASS)
            inside = jnp.bool_(False)
            for low_chunk, high_chunk in reach:
                inside = inside | ((i >= low_chunk) & (i < high_chunk))
            for sums, out_ref, factor in ((dka_ref, dk_ref, scale), (dva_ref, dv_ref, 1.0)):

                @pl.when(inside)
                def _(sums=sums, out_ref=out_ref, factor=factor):
                    out_ref[rows, :] = (sums[rows, :] * factor).astype(bf16)

                @pl.when(jnp.logical_not(inside))
                def _(out_ref=out_ref):
                    out_ref[rows, :] = jnp.zeros((PASS, HD), bf16)

            return carry

        lax.fori_loop(0, tokens // PASS, finish, 0)


def attend(queries, out_grad, rows, slot, keys, values, lengths, block_owner):
    tokens = keys.shape[0]
    shard = queries.shape[0]
    per_core = shard // QBLOCK
    width = HEADS_HERE * HD
    span = ((DOC_MAX + QBLOCK + TILE - 2) // TILE + 1) * TILE
    qcols = QBLOCK * HEADS_HERE

    def own_spec():
        return pl.BlockSpec((QBLOCK, width), lambda i, _, slot: (jnp.minimum(i, per_core - 1), slot[0]))

    def other_spec(col):
        return pl.BlockSpec((QBLOCK, width), lambda i, *_: (jnp.maximum(i - per_core, 0), col))

    def result_spec(n):
        return pl.BlockSpec((QBLOCK, 2 * width), lambda i, *_: (jnp.clip(i - n * per_core, 0, per_core - 1), 0))

    full_spec = pl.BlockSpec((tokens, HD), lambda i, *_: (0, 0))
    bf16, f32 = jnp.bfloat16, jnp.float32
    owner_spec = pl.BlockSpec((1, block_owner.shape[0]), lambda i, *_: (0, 0))
    return pl.pallas_call(
        attend_kernel,
        grid_spec=pltpu.PrefetchScalarGridSpec(
            num_scalar_prefetch=2,
            grid=(GROUP * per_core,),
            in_specs=[
                owner_spec, own_spec(), own_spec(), other_spec(0), other_spec(1), full_spec, full_spec,
            ],
            out_specs=[result_spec(n) for n in range(GROUP)]
            + [full_spec, full_spec, pl.BlockSpec(memory_space=pltpu.SMEM)],
            scratch_shapes=[
                pltpu.VMEM((HD, tokens), bf16),
                pltpu.VMEM((HD + ONES, tokens), bf16),
                pltpu.VMEM((span, qcols), bf16),
                pltpu.VMEM((HD, qcols), bf16),
                pltpu.VMEM((HD, qcols), bf16),
                pltpu.VMEM((qcols, HD), bf16),
                pltpu.VMEM((qcols, HD), bf16),
                pltpu.VMEM((tokens, HD), f32),
                pltpu.VMEM((tokens, HD), f32),
                pltpu.VMEM((SPAN * TILE, qcols), bf16),
                pltpu.VMEM((HD + ONES, qcols), f32),
            ],
        ),
        out_shape=[jax.ShapeDtypeStruct((shard, 2 * width), bf16)] * GROUP
        + [jax.ShapeDtypeStruct((tokens, HD), bf16)] * 2
        + [jax.ShapeDtypeStruct((1,), f32)],
        cost_estimate=pl.CostEstimate(flops=2 * 10**10, bytes_accessed=2 * 10**7, transcendentals=5 * 10**6),
        compiler_params=pltpu.CompilerParams(vmem_limit_bytes=62 * 2**20),
        name="attend",
    )(lengths, slot, block_owner.reshape(1, -1), queries, out_grad, rows, rows, keys, values)


def scatter_kernel(
    dk_ref, dv_ref, rows_ref, back_ref, key_ref, value_ref,
    part, from_core, from_far, from_near, from_x,
    part_sem, core_send, core_recv, far_send, far_recv, near_send, near_recv,
    x_send, x_recv, row_send, row_recv,
):
    x, y, core = place()
    shard = key_ref.shape[0]
    half = shard // 2
    up, down, far = (y + 1) % YS, (y + YS - 1) % YS, (y + 2) % YS
    x_rank = rank_of(1 - x, y, core)
    core_rank = rank_of(x, y, 1 - core)
    up_rank, down_rank = rank_of(x, up, core), rank_of(x, down, core)
    started = []

    def send(src, dst, send_sem, recv_sem, rank):
        copy = remote(src, dst, send_sem, recv_sem, rank)
        copy.start()
        started.append(copy)

    def landed(ref, recv_sem):
        remote(ref, ref, recv_sem, recv_sem, x_rank).wait_recv()

    pairs = (dk_ref, dv_ref)
    order = [(1 - x, far), (x, far), (1 - x, up), (x, up), (1 - x, down), (x, down), (1 - x, y), (x, y)]
    loads = []
    for n, (sx, sy) in enumerate(order):
        for a, src in enumerate(pairs):
            rows = rows_at(rank_of(sx, sy, core) * shard, shard)
            copy = pltpu.make_async_copy(src.at[rows], part.at[a, n], part_sem.at[a, n])
            copy.start()
            loads.append(copy)
    enter(x, y, core)
    for n, (sx, sy) in enumerate(order):
        for a, src in enumerate(pairs):
            rows = rows_at(rank_of(sx, sy, 1 - core) * shard, shard)
            send(src.at[rows], from_core.at[a, n], core_send.at[a, n], core_recv.at[a, n], core_rank)

    send(rows_ref, back_ref, row_send, row_recv, core_rank)

    def add(ref, other):
        ref[...] = (ref[...].astype(jnp.float32) + other[...].astype(jnp.float32)).astype(jnp.bfloat16)

    def core_sum(a, n):
        loads[2 * n + a].wait()
        landed(from_core.at[a, n], core_recv.at[a, n])
        add(part.at[a, n], from_core.at[a, n])

    for n in range(2):
        for a in range(2):
            core_sum(a, n)
            for h, rank in ((0, up_rank), (1, down_rank)):
                send(
                    part.at[a, n, pl.ds(h * half, half)], from_far.at[a, n, h],
                    far_send.at[a, n, h], far_recv.at[a, n, h], rank,
                )
    for n in range(2):
        for a in range(2):
            for j, rank in ((0, up_rank), (1, down_rank)):
                core_sum(a, 2 + 2 * j + n)
                free = 1 - j
                send(
                    part.at[a, 2 + 2 * j + n, pl.ds(free * half, half)],
                    from_near.at[a, n, j, pl.ds(free * half, half)],
                    near_send.at[a, n, j, free], near_recv.at[a, n, j, free], rank,
                )
    for n in range(2):
        for a in range(2):
            for j, rank in ((0, up_rank), (1, down_rank)):
                landed(from_far.at[a, n, j], far_recv.at[a, n, j])
                mine = part.at[a, 2 + 2 * j + n, pl.ds(j * half, half)]
                add(mine, from_far.at[a, n, j])
                send(
                    mine, from_near.at[a, n, j, pl.ds(j * half, half)],
                    near_send.at[a, n, j, j], near_recv.at[a, n, j, j], rank,
                )
    for n in range(2):
        for a in range(2):
            core_sum(a, 6 + n)
            for j in range(2):
                for h in (1 - j, j):
                    landed(from_near.at[a, n, j, pl.ds(h * half, half)], near_recv.at[a, n, j, h])
            total = part[a, 6 + n].astype(jnp.float32)
            total = total + from_near[a, n, 0].astype(jnp.float32)
            total = total + from_near[a, n, 1].astype(jnp.float32)
            part[a, 6 + n] = total.astype(jnp.bfloat16)
            if n == 0:
                send(part.at[a, 6], from_x.at[a], x_send.at[a], x_recv.at[a], x_rank)
    for a, dst in enumerate((key_ref, value_ref)):
        landed(from_x.at[a], x_recv.at[a])
        dst[...] = (part[a, 7].astype(jnp.float32) + from_x[a].astype(jnp.float32)).astype(jnp.bfloat16)
    landed(back_ref, row_recv)
    for copy in started:
        copy.wait_send()


def scatter(key_terms, value_terms, rows, ranks):
    tokens = key_terms.shape[0]
    shard = tokens // ranks
    half = shard // 2
    bf16 = jnp.bfloat16
    any_spec = pl.BlockSpec(memory_space=pl.ANY)
    vmem_spec = pl.BlockSpec(memory_space=pltpu.VMEM)
    dma = pltpu.SemaphoreType.DMA
    return pl.pallas_call(
        scatter_kernel,
        in_specs=[any_spec] * 3,
        out_specs=[any_spec, vmem_spec, vmem_spec],
        out_shape=[
            jax.ShapeDtypeStruct(rows.shape, bf16),
            jax.ShapeDtypeStruct((shard, HD), bf16),
            jax.ShapeDtypeStruct((shard, HD), bf16),
        ],
        scratch_shapes=[
            pltpu.VMEM((2, ranks // 2, shard, HD), bf16),
            pltpu.VMEM((2, ranks // 2, shard, HD), bf16),
            pltpu.VMEM((2, 2, 2, half, HD), bf16),
            pltpu.VMEM((2, 2, 2, shard, HD), bf16),
            pltpu.VMEM((2, shard, HD), bf16),
            dma((2, 8)), dma((2, 8)), dma((2, 8)), dma((2, 2, 2)), dma((2, 2, 2)),
            dma((2, 2, 2, 2)), dma((2, 2, 2, 2)), dma((2,)), dma((2,)), dma, dma,
        ],
        cost_estimate=pl.CostEstimate(flops=2 * 10**7, bytes_accessed=2 * 10**7, transcendentals=0),
        compiler_params=pltpu.CompilerParams(
            collective_id=1, has_side_effects=True, vmem_limit_bytes=62 * 2**20
        ),
        name="scatter",
    )(key_terms, value_terms, rows)


def place_kernel(a_ref, b_ref, c_ref, d_ref, o_ref, q_ref):
    x, _, core = place()
    width = a_ref.shape[1] // 2
    for d, ref in enumerate((a_ref, b_ref, c_ref, d_ref)):
        slot = ((x + d // 2) % 2) * 2 + (core + d % 2) % 2
        cols = pl.ds(pl.multiple_of(slot * width, width), width)
        o_ref[:, cols] = ref[:, :width]
        q_ref[:, cols] = ref[:, width:]


def place_columns(pieces):
    shard, width = pieces[0].shape
    block = shard // 4
    shape = jax.ShapeDtypeStruct((shard, width * 2), jnp.bfloat16)
    return pl.pallas_call(
        place_kernel,
        grid=(shard // block,),
        in_specs=[pl.BlockSpec((block, width), lambda i: (i, 0))] * GROUP,
        out_specs=[pl.BlockSpec((block, width * 2), lambda i: (i, 0))] * 2,
        out_shape=[shape, shape],
        compiler_params=pltpu.CompilerParams(vmem_limit_bytes=62 * 2**20),
        name="place",
    )(*pieces)


def body(queries, key_rows, values, out_grad, lengths, block_owner):
    ranks = lax.axis_size("context")
    x, _, core = place()
    chips = [(a, b, c) for a in range(2) for b in range(YS) for c in range(2)]
    same = [(rank_of(a, b, c), rank_of(1 - a, b, c)) for a, b, c in chips]
    cross = [(rank_of(a, b, c), rank_of(1 - a, b, 1 - c)) for a, b, c in chips]
    rows, keys, all_values = gather(queries, out_grad, key_rows, values, ranks)
    slot = (x * 2 + core).astype(jnp.int32).reshape(1)
    own, near, far_same, far_cross, dk, dv, pair_count = attend(
        queries, out_grad, rows, slot, keys, all_values, lengths, block_owner
    )
    far_same = lax.ppermute(far_same, "context", same)
    far_cross = lax.ppermute(far_cross, "context", cross)
    near, key_grad, value_grad = scatter(dk, dv, near, ranks)
    out, query_grad = place_columns((own, near, far_same, far_cross))
    return out, query_grad, key_grad, value_grad, pair_count


def solution(mesh):
    rows = P(("dp", "context"), None)
    return jax.shard_map(
        body,
        mesh=mesh,
        in_specs=(rows, rows, rows, rows, P("dp"), P("dp")),
        out_specs=(rows, rows, rows, rows, P(("dp", "context"))),
        check_vma=False,
    )
```

```python
import functools
import math

import jax
import jax.numpy as jnp
from jax import lax
from jax.experimental import pallas as pl
from jax.experimental.pallas import tpu as pltpu
from jax.sharding import PartitionSpec as P

NEG_FILL = -1e30
MESH = pl.DeviceIdType.MESH
YS = 4
HD = 128
NEAR = 3
FAR = 1
GROUP = 4
TILE = 256
SPAN = 4
PASS = 512
ONES = 16
LARGE = 1e12
QBLOCK = 256
DOC_MAX = 4096


def place():
    me = lax.axis_index("context")
    return me // (2 * YS), (me // 2) % YS, me % 2


def rank_of(x, y, core):
    return (x * YS + y) * 2 + core


def remote(src, dst, send_sem, recv_sem, rank):
    return pltpu.make_async_remote_copy(
        src_ref=src,
        dst_ref=dst,
        send_sem=send_sem,
        recv_sem=recv_sem,
        device_id={"context": rank},
        device_id_type=MESH,
    )


def enter(x, y, core, rows=False):
    barrier = pltpu.get_barrier_semaphore()
    others = [
        rank_of(x, y, 1 - core),
        rank_of(1 - x, y, core),
        rank_of(x, (y + 1) % YS, core),
        rank_of(x, (y + YS - 1) % YS, core),
    ]
    if rows:
        others.append(rank_of(1 - x, y, 1 - core))
    for other in others:
        pl.semaphore_signal(barrier, inc=1, device_id={"context": other}, device_id_type=MESH)
    pl.semaphore_wait(barrier, len(others))


def rows_at(begin, count):
    return pl.ds(pl.multiple_of(begin, count), count)


def head_cols(d, core):
    heads = NEAR if d < 2 else FAR
    at = core * NEAR * HD if d < 2 else 2 * NEAR * HD + core * FAR * HD
    return pl.ds(pl.multiple_of(at, HD), heads * HD)


def rows_from(near_ref, far_ref, d, a):
    if d < 2:
        return near_ref.at[:, pl.ds(a * NEAR * HD, NEAR * HD)]
    shard = near_ref.shape[0]
    return far_ref.at[pl.ds((d - 2) * shard, shard), pl.ds(a * FAR * HD, FAR * HD)]


def gather_kernel(
    q_ref, g_ref, k_ref, v_ref, near_ref, far_ref, ka_ref, va_ref,
    own_sem, kv_send, kv_recv, core_send, core_recv, row_send, row_recv,
):
    x, y, core = place()
    shard = k_ref.shape[0]
    half = shard // 2
    up, down, far = (y + 1) % YS, (y + YS - 1) % YS, (y + 2) % YS
    x_rank = rank_of(1 - x, y, core)
    core_rank = rank_of(x, y, 1 - core)
    up_rank, down_rank = rank_of(x, up, core), rank_of(x, down, core)
    enter(x, y, core, rows=True)
    started = []

    def send(src, dst, send_sem, recv_sem, rank):
        copy = remote(src, dst, send_sem, recv_sem, rank)
        copy.start()
        started.append(copy)

    def landed(ref, recv_sem):
        remote(ref, ref, recv_sem, recv_sem, x_rank).wait_recv()

    own = []
    pairs = ((k_ref, ka_ref), (v_ref, va_ref))
    my_rows = rows_at(rank_of(x, y, core) * shard, shard)
    for a, (src, dst) in enumerate(pairs):
        send(src, dst.at[my_rows], kv_send.at[a, 0], kv_recv.at[a, 0], x_rank)
        send(src, dst.at[my_rows], kv_send.at[a, 1], kv_recv.at[a, 1], up_rank)
        send(src, dst.at[my_rows], kv_send.at[a, 2], kv_recv.at[a, 2], down_rank)
        send(src, dst.at[my_rows], core_send.at[a, 0], core_recv.at[a, 0], core_rank)
        copy = pltpu.make_async_copy(src, dst.at[my_rows], own_sem.at[a])
        copy.start()
        own.append(copy)

    for a, src in enumerate((q_ref, g_ref)):
        for d in range(1, GROUP):
            tx, tc = (x + d // 2) % 2, (core + d % 2) % 2
            send(
                src.at[:, head_cols(d, tc)], rows_from(near_ref, far_ref, d, a),
                row_send.at[a, d - 1], row_recv.at[a, d - 1], rank_of(tx, y, tc),
            )

    def forward(a, n, ref, rows, rank, relay):
        send(ref.at[rows], ref.at[rows], relay[0].at[a, n], relay[1].at[a, n], rank)

    y_relay, c_relay = (kv_send, kv_recv), (core_send, core_recv)

    def shard_rows(sx, sy, sc):
        return rows_at(rank_of(sx, sy, sc) * shard, shard)

    def half_rows(sx, sy, sc, h):
        return rows_at(rank_of(sx, sy, sc) * shard + h * half, half)

    for a, (_, dst) in enumerate(pairs):
        rows = shard_rows(1 - x, y, core)
        landed(dst.at[rows], kv_recv.at[a, 0])
        forward(a, 3, dst, rows, up_rank, y_relay)
        forward(a, 4, dst, rows, down_rank, y_relay)
        forward(a, 1, dst, rows, core_rank, c_relay)
    for n, sx in ((1, x), (3, 1 - x)):
        for a, (_, dst) in enumerate(pairs):
            landed(dst.at[shard_rows(sx, down, core)], kv_recv.at[a, n])
            forward(a, 4 + n, dst, half_rows(sx, down, core, 0), up_rank, y_relay)
            landed(dst.at[shard_rows(sx, up, core)], kv_recv.at[a, n + 1])
            forward(a, 5 + n, dst, half_rows(sx, up, core, 1), down_rank, y_relay)
            forward(a, 1 + n, dst, shard_rows(sx, down, core), core_rank, c_relay)
            forward(a, 2 + n, dst, shard_rows(sx, up, core), core_rank, c_relay)
    for n, sx in ((1, x), (3, 1 - x)):
        for a, (_, dst) in enumerate(pairs):
            for h in range(2):
                rows = half_rows(sx, far, core, h)
                landed(dst.at[rows], kv_recv.at[a, 4 + n + h])
                forward(a, 5 + n + h, dst, rows, core_rank, c_relay)
    for a, (_, dst) in enumerate(pairs):
        oc = 1 - core
        whole = ((x, y), (1 - x, y), (x, down), (x, up), (1 - x, down), (1 - x, up))
        for n, (sx, sy) in enumerate(whole):
            landed(dst.at[shard_rows(sx, sy, oc)], core_recv.at[a, n])
        for n, sx in ((1, x), (3, 1 - x)):
            for h in range(2):
                landed(dst.at[half_rows(sx, far, oc, h)], core_recv.at[a, 5 + n + h])
    for a in range(2):
        for d in range(1, GROUP):
            landed(rows_from(near_ref, far_ref, d, a), row_recv.at[a, d - 1])
    for copy in own:
        copy.wait()
    for copy in started:
        copy.wait_send()


def gather(queries, out_grad, keys, values, ranks):
    shard = queries.shape[0]
    bf16 = jnp.bfloat16
    any_spec = pl.BlockSpec(memory_space=pl.ANY)
    dma = pltpu.SemaphoreType.DMA
    return pl.pallas_call(
        gather_kernel,
        in_specs=[any_spec] * 4,
        out_specs=[any_spec] * 4,
        out_shape=[
            jax.ShapeDtypeStruct((shard, 2 * NEAR * HD), bf16),
            jax.ShapeDtypeStruct((2 * shard, 2 * FAR * HD), bf16),
            jax.ShapeDtypeStruct((ranks * shard, HD), bf16),
            jax.ShapeDtypeStruct((ranks * shard, HD), bf16),
        ],
        scratch_shapes=[
            dma((2,)), dma((2, 9)), dma((2, 9)), dma((2, 10)), dma((2, 10)), dma((2, 3)), dma((2, 3)),
        ],
        compiler_params=pltpu.CompilerParams(collective_id=0, has_side_effects=True, vmem_limit_bytes=62 * 2**20),
        name="gather",
    )(queries, out_grad, keys, values)


def dot(a, b):
    return jnp.dot(a, b, preferred_element_type=jnp.float32)


def attend_block(
    heads, block, first, len_ref, inputs, outputs, k_ref, v_ref, kt_ref, vt_ref, dka_ref, dva_ref,
    p_ref, qt_ref, gt_ref, qn_ref, gn_ref, ds_ref, acc_ref,
):
    f32, bf16 = jnp.float32, jnp.bfloat16
    cols = block * heads
    docs = len_ref.shape[0]
    scale = 1.0 / math.sqrt(HD)
    scale2 = scale * math.log2(math.e)
    row_pos = first + lax.rem(lax.broadcasted_iota(jnp.int32, (1, cols), 1), block)
    row_start = jnp.zeros((1, cols), jnp.int32)
    first_start, last_start, end = jnp.int32(0), jnp.int32(0), jnp.int32(0)
    for d in range(docs):
        end = end + len_ref[d]
        row_start = jnp.where(row_pos >= end, end, row_start)
        first_start = jnp.where(first >= end, end, first_start)
        last_start = jnp.where(first + block - 1 >= end, end, last_start)
    low = lax.div(first_start, TILE)
    high = lax.div(first + block - 1, TILE) + 1

    own_keys = kt_ref[:, rows_at(first, block)].astype(f32)
    shift = []
    for h in range(heads):
        for chosen, q_ref, g_ref in inputs:

            @pl.when(chosen)
            def _(h=h, q_ref=q_ref, g_ref=g_ref):
                qt_ref[:, h * block : (h + 1) * block] = q_ref[:, h * HD : (h + 1) * HD].T
                gt_ref[:, h * block : (h + 1) * block] = g_ref[:, h * HD : (h + 1) * HD].T

        q_t = qt_ref[:, h * block : (h + 1) * block]
        shift.append(jnp.sum(q_t.astype(f32) * own_keys, axis=0, keepdims=True) * scale2)
    shift = jnp.concatenate(shift, axis=1)

    def keep(result, at):
        for chosen, r_ref in outputs:

            @pl.when(chosen)
            def _(r_ref=r_ref):
                for h in range(heads):
                    cut = result[h * block : (h + 1) * block, :]
                    r_ref[:, (at + h) * HD : (at + h + 1) * HD] = cut

    def key_rows(t, count):
        return pl.ds(pl.multiple_of(t * TILE, TILE), count)

    def kept_rows(t, count):
        return pl.ds(pl.multiple_of((t - low) * TILE, TILE), count)

    def sweep(piece):
        count = high - low
        groups = lax.div(count, SPAN)

        def one(g, carry):
            piece(low + g * SPAN, SPAN * TILE, False)
            return carry

        lax.fori_loop(0, groups, one, 0)
        at = low + groups * SPAN
        size = SPAN // 2
        while size:
            has = lax.rem(lax.div(count, size), 2)

            @pl.when(has == 1)
            def _(at=at, size=size):
                piece(at, size * TILE, True)

            at = at + has * size
            size //= 2

    def forward(shift):
        acc_ref[...] = jnp.zeros(acc_ref.shape, f32)

        def piece(t, rows, last):
            def run(mask):
                acc = None
                part = min(rows, PASS)
                for i in range(0, rows, part):
                    tile = t + i // TILE
                    s = dot(k_ref[key_rows(tile, part), :], qt_ref[...]) * scale2 - shift
                    if mask:
                        pos = t * TILE + i + lax.broadcasted_iota(jnp.int32, s.shape, 0)
                        s = jnp.where((pos >= row_start) & (pos <= row_pos), s, NEG_FILL)
                    p_ref[kept_rows(tile, part), :] = jnp.exp2(s).astype(bf16)
                    term = dot(vt_ref[:, key_rows(tile, part)], p_ref[kept_rows(tile, part), :])
                    acc = term if acc is None else acc + term
                acc_ref[...] += acc

            if last:
                run(True)
            else:
                edge = (t * TILE < last_start) | (t * TILE + rows - 1 > first)
                pl.when(edge)(lambda: run(True))
                pl.when(jnp.logical_not(edge))(lambda: run(False))

        sweep(piece)

    forward(shift)

    @pl.when(jnp.logical_not(jnp.max(acc_ref[HD : HD + 1, :]) < LARGE))
    def _():
        def peak_pass(t, peak):
            s = dot(k_ref[key_rows(t, TILE), :], qt_ref[...]) * scale2
            pos = t * TILE + lax.broadcasted_iota(jnp.int32, s.shape, 0)
            s = jnp.where((pos >= row_start) & (pos <= row_pos), s, NEG_FILL)
            return jnp.maximum(peak, jnp.max(s.reshape(TILE // 8, 8, cols), axis=0))

        peak = lax.fori_loop(low, high, peak_pass, jnp.full((8, cols), NEG_FILL, f32))
        forward(jnp.max(peak, axis=0, keepdims=True))

    inverse = 1.0 / acc_ref[HD : HD + 1, :]
    out = (acc_ref[0:HD, :] * inverse).astype(bf16)
    grad_t = gt_ref[...].astype(f32)
    grad_dot = jnp.sum(out.astype(f32) * grad_t, axis=0, keepdims=True)
    gn_ref[...] = (grad_t * inverse).astype(bf16).T
    qn_ref[...] = (qt_ref[...].astype(f32) * inverse).astype(bf16).T
    keep(out.T, 0)
    acc_ref[0:HD, :] = jnp.zeros((HD, cols), f32)

    def backward(t, rows, last):
        keys, kept = key_rows(t, rows), kept_rows(t, rows)
        grad_p = dot(v_ref[keys, :], gt_ref[...])
        ds_ref[0:rows, :] = (p_ref[kept, :].astype(f32) * (grad_p - grad_dot)).astype(bf16)
        dva_ref[keys, :] += dot(p_ref[kept, :], gn_ref[...])
        dka_ref[keys, :] += dot(ds_ref[0:rows, :], qn_ref[...])
        acc_ref[0:HD, :] += dot(kt_ref[:, keys], ds_ref[0:rows, :])

    sweep(backward)
    query_grad = (acc_ref[0:HD, :] * (inverse * scale)).astype(bf16).T
    keep(query_grad, heads)


def attend_kernel(
    len_ref, core_ref, owner_ref, q0_ref, g0_ref, q1_ref, g1_ref, q2_ref, g2_ref, k_ref, v_ref,
    r0_ref, r1_ref, r2_ref, r3_ref, dk_ref, dv_ref, pair_ref,
    kt_ref, vt_ref, p_ref, qt_ref, gt_ref, qn_ref, gn_ref, dka_ref, dva_ref, ds_ref, acc_ref,
):
    blk = pl.program_id(0)
    block = q0_ref.shape[0]
    tokens = k_ref.shape[0]
    docs = len_ref.shape[0]
    f32, bf16 = jnp.float32, jnp.bfloat16
    scale = 1.0 / math.sqrt(HD)
    x, y, core = place()
    per_chip = tokens // (2 * YS)
    per_core = pl.num_programs(0) // GROUP

    reach = []
    for chip in (y, YS + y):
        begin, end = jnp.int32(0), jnp.int32(0)
        for d in range(docs):
            end = end + len_ref[d]
            begin = jnp.where(chip * per_chip >= end, end, begin)
        reach.append((lax.div(begin, PASS), lax.div((chip + 1) * per_chip, PASS)))
    reach[1] = (jnp.maximum(reach[1][0], reach[0][1]), reach[1][1])

    @pl.when(blk == 0)
    def _():
        def prepare(i, carry):
            rows = rows_at(i * PASS, PASS)
            kt_ref[:, rows] = k_ref[rows, :].T
            vt_ref[0:HD, rows] = v_ref[rows, :].T
            vt_ref[HD:, rows] = jnp.ones((ONES, PASS), bf16)
            dka_ref[rows, :] = jnp.zeros((PASS, HD), f32)
            dva_ref[rows, :] = jnp.zeros((PASS, HD), f32)
            return carry

        for low_chunk, high_chunk in reach:
            lax.fori_loop(low_chunk, high_chunk, prepare, 0)
        blocks = owner_ref.shape[1]
        block_rows = tokens // blocks
        shape = (block_rows, blocks)
        pos = lax.broadcasted_iota(jnp.int32, shape, 1) * block_rows
        pos = pos + lax.broadcasted_iota(jnp.int32, shape, 0)
        begin, end = jnp.zeros(shape, jnp.int32), jnp.int32(0)
        for d in range(docs):
            end = end + len_ref[d]
            begin = jnp.where(pos >= end, end, begin)
        counts = (pos - begin + 1).astype(f32)
        counts = jnp.where(owner_ref[...] == lax.axis_index("context"), counts, 0.0)
        pair_ref[0] = jnp.sum(counts)

    part = lax.div(blk, per_core)
    chip = lax.rem(x + lax.div(part, 2), 2) * YS + y
    row_core = lax.rem(core + part, 2)
    first = chip * per_chip + row_core * (per_chip // 2) + lax.rem(blk, per_core) * block

    def work(heads, inputs, outputs):
        cols = block * heads
        scratch = (
            p_ref.at[:, 0:cols], qt_ref.at[:, 0:cols], gt_ref.at[:, 0:cols], qn_ref.at[0:cols], gn_ref.at[0:cols],
            ds_ref.at[:, 0:cols], acc_ref.at[:, 0:cols],
        )
        attend_block(
            heads, block, first, len_ref, inputs, outputs, k_ref, v_ref, kt_ref, vt_ref, dka_ref, dva_ref, *scratch
        )

    @pl.when(part < 2)
    def _():
        work(
            NEAR, ((part == 0, q0_ref, g0_ref), (part == 1, q1_ref, g1_ref)),
            ((part == 0, r0_ref), (part == 1, r1_ref)),
        )

    @pl.when(part >= 2)
    def _():
        work(FAR, ((part >= 2, q2_ref, g2_ref),), ((part == 2, r2_ref), (part == 3, r3_ref)))

    @pl.when(blk == pl.num_programs(0) - 1)
    def _():
        def finish(i, carry):
            rows = rows_at(i * PASS, PASS)
            inside = jnp.bool_(False)
            for low_chunk, high_chunk in reach:
                inside = inside | ((i >= low_chunk) & (i < high_chunk))
            for sums, out_ref, factor in ((dka_ref, dk_ref, scale), (dva_ref, dv_ref, 1.0)):

                @pl.when(inside)
                def _(sums=sums, out_ref=out_ref, factor=factor):
                    out_ref[rows, :] = (sums[rows, :] * factor).astype(bf16)

                @pl.when(jnp.logical_not(inside))
                def _(out_ref=out_ref):
                    out_ref[rows, :] = jnp.zeros((PASS, HD), bf16)

            return carry

        lax.fori_loop(0, tokens // PASS, finish, 0)


def attend(queries, out_grad, near, far, core, keys, values, lengths, block_owner):
    tokens = keys.shape[0]
    shard = queries.shape[0]
    per_core = shard // QBLOCK
    span = ((DOC_MAX + QBLOCK + TILE - 2) // TILE + 1) * TILE
    qcols = QBLOCK * NEAR

    def step(i, n):
        return jnp.clip(i - n * per_core, 0, per_core - 1)

    own_spec = pl.BlockSpec((QBLOCK, NEAR * HD), lambda i, _, core: (step(i, 0), core[0]))

    def near_spec(col):
        return pl.BlockSpec((QBLOCK, NEAR * HD), lambda i, *_: (step(i, 1), col))

    def far_spec(col):
        return pl.BlockSpec((QBLOCK, FAR * HD), lambda i, *_: (jnp.maximum(i - 2 * per_core, 0), col))

    def result_spec(n):
        heads = NEAR if n < 2 else FAR
        return pl.BlockSpec((QBLOCK, 2 * heads * HD), lambda i, *_: (step(i, n), 0))

    full_spec = pl.BlockSpec((tokens, HD), lambda i, *_: (0, 0))
    bf16, f32 = jnp.bfloat16, jnp.float32
    owner_spec = pl.BlockSpec((1, block_owner.shape[0]), lambda i, *_: (0, 0))
    return pl.pallas_call(
        attend_kernel,
        grid_spec=pltpu.PrefetchScalarGridSpec(
            num_scalar_prefetch=2,
            grid=(GROUP * per_core,),
            in_specs=[
                owner_spec, own_spec, own_spec, near_spec(0), near_spec(1), far_spec(0), far_spec(1),
                full_spec, full_spec,
            ],
            out_specs=[result_spec(n) for n in range(GROUP)]
            + [full_spec, full_spec, pl.BlockSpec(memory_space=pltpu.SMEM)],
            scratch_shapes=[
                pltpu.VMEM((HD, tokens), bf16),
                pltpu.VMEM((HD + ONES, tokens), bf16),
                pltpu.VMEM((span, qcols), bf16),
                pltpu.VMEM((HD, qcols), bf16),
                pltpu.VMEM((HD, qcols), bf16),
                pltpu.VMEM((qcols, HD), bf16),
                pltpu.VMEM((qcols, HD), bf16),
                pltpu.VMEM((tokens, HD), f32),
                pltpu.VMEM((tokens, HD), f32),
                pltpu.VMEM((SPAN * TILE, qcols), bf16),
                pltpu.VMEM((HD + ONES, qcols), f32),
            ],
        ),
        out_shape=[jax.ShapeDtypeStruct((shard, 2 * NEAR * HD), bf16)] * 2
        + [jax.ShapeDtypeStruct((shard, 2 * FAR * HD), bf16)] * 2
        + [jax.ShapeDtypeStruct((tokens, HD), bf16)] * 2
        + [jax.ShapeDtypeStruct((1,), f32)],
        cost_estimate=pl.CostEstimate(flops=2 * 10**10, bytes_accessed=2 * 10**7, transcendentals=5 * 10**6),
        compiler_params=pltpu.CompilerParams(vmem_limit_bytes=62 * 2**20),
        name="attend",
    )(lengths, core, block_owner.reshape(1, -1), queries, out_grad, near, near, far, far, keys, values)


def scatter_kernel(
    dk_ref, dv_ref, rows_ref, back_ref, key_ref, value_ref,
    part, from_core, from_far, from_near, from_x,
    part_sem, core_send, core_recv, far_send, far_recv, near_send, near_recv,
    x_send, x_recv, row_send, row_recv,
):
    x, y, core = place()
    shard = key_ref.shape[0]
    half = shard // 2
    up, down, far = (y + 1) % YS, (y + YS - 1) % YS, (y + 2) % YS
    x_rank = rank_of(1 - x, y, core)
    core_rank = rank_of(x, y, 1 - core)
    up_rank, down_rank = rank_of(x, up, core), rank_of(x, down, core)
    started = []

    def send(src, dst, send_sem, recv_sem, rank):
        copy = remote(src, dst, send_sem, recv_sem, rank)
        copy.start()
        started.append(copy)

    def landed(ref, recv_sem):
        remote(ref, ref, recv_sem, recv_sem, x_rank).wait_recv()

    pairs = (dk_ref, dv_ref)
    order = [(1 - x, far), (x, far), (1 - x, up), (x, up), (1 - x, down), (x, down), (1 - x, y), (x, y)]
    loads = []
    for n, (sx, sy) in enumerate(order):
        for a, src in enumerate(pairs):
            rows = rows_at(rank_of(sx, sy, core) * shard, shard)
            copy = pltpu.make_async_copy(src.at[rows], part.at[a, n], part_sem.at[a, n])
            copy.start()
            loads.append(copy)
    enter(x, y, core)
    for n, (sx, sy) in enumerate(order):
        for a, src in enumerate(pairs):
            rows = rows_at(rank_of(sx, sy, 1 - core) * shard, shard)
            send(src.at[rows], from_core.at[a, n], core_send.at[a, n], core_recv.at[a, n], core_rank)

    send(rows_ref, back_ref, row_send, row_recv, core_rank)

    def add(ref, other):
        ref[...] = (ref[...].astype(jnp.float32) + other[...].astype(jnp.float32)).astype(jnp.bfloat16)

    def core_sum(a, n):
        loads[2 * n + a].wait()
        landed(from_core.at[a, n], core_recv.at[a, n])
        add(part.at[a, n], from_core.at[a, n])

    for n in range(2):
        for a in range(2):
            core_sum(a, n)
            for h, rank in ((0, up_rank), (1, down_rank)):
                send(
                    part.at[a, n, pl.ds(h * half, half)], from_far.at[a, n, h],
                    far_send.at[a, n, h], far_recv.at[a, n, h], rank,
                )
    for n in range(2):
        for a in range(2):
            for j, rank in ((0, up_rank), (1, down_rank)):
                core_sum(a, 2 + 2 * j + n)
                free = 1 - j
                send(
                    part.at[a, 2 + 2 * j + n, pl.ds(free * half, half)],
                    from_near.at[a, n, j, pl.ds(free * half, half)],
                    near_send.at[a, n, j, free], near_recv.at[a, n, j, free], rank,
                )
    for n in range(2):
        for a in range(2):
            for j, rank in ((0, up_rank), (1, down_rank)):
                landed(from_far.at[a, n, j], far_recv.at[a, n, j])
                mine = part.at[a, 2 + 2 * j + n, pl.ds(j * half, half)]
                add(mine, from_far.at[a, n, j])
                send(
                    mine, from_near.at[a, n, j, pl.ds(j * half, half)],
                    near_send.at[a, n, j, j], near_recv.at[a, n, j, j], rank,
                )
    for n in range(2):
        for a in range(2):
            core_sum(a, 6 + n)
            for j in range(2):
                for h in (1 - j, j):
                    landed(from_near.at[a, n, j, pl.ds(h * half, half)], near_recv.at[a, n, j, h])
            total = part[a, 6 + n].astype(jnp.float32)
            total = total + from_near[a, n, 0].astype(jnp.float32)
            total = total + from_near[a, n, 1].astype(jnp.float32)
            part[a, 6 + n] = total.astype(jnp.bfloat16)
            if n == 0:
                send(part.at[a, 6], from_x.at[a], x_send.at[a], x_recv.at[a], x_rank)
    for a, dst in enumerate((key_ref, value_ref)):
        landed(from_x.at[a], x_recv.at[a])
        dst[...] = (part[a, 7].astype(jnp.float32) + from_x[a].astype(jnp.float32)).astype(jnp.bfloat16)
    landed(back_ref, row_recv)
    for copy in started:
        copy.wait_send()


def scatter(key_terms, value_terms, rows, ranks):
    tokens = key_terms.shape[0]
    shard = tokens // ranks
    half = shard // 2
    bf16 = jnp.bfloat16
    any_spec = pl.BlockSpec(memory_space=pl.ANY)
    vmem_spec = pl.BlockSpec(memory_space=pltpu.VMEM)
    dma = pltpu.SemaphoreType.DMA
    return pl.pallas_call(
        scatter_kernel,
        in_specs=[any_spec] * 3,
        out_specs=[any_spec, vmem_spec, vmem_spec],
        out_shape=[
            jax.ShapeDtypeStruct(rows.shape, bf16),
            jax.ShapeDtypeStruct((shard, HD), bf16),
            jax.ShapeDtypeStruct((shard, HD), bf16),
        ],
        scratch_shapes=[
            pltpu.VMEM((2, ranks // 2, shard, HD), bf16),
            pltpu.VMEM((2, ranks // 2, shard, HD), bf16),
            pltpu.VMEM((2, 2, 2, half, HD), bf16),
            pltpu.VMEM((2, 2, 2, shard, HD), bf16),
            pltpu.VMEM((2, shard, HD), bf16),
            dma((2, 8)), dma((2, 8)), dma((2, 8)), dma((2, 2, 2)), dma((2, 2, 2)),
            dma((2, 2, 2, 2)), dma((2, 2, 2, 2)), dma((2,)), dma((2,)), dma, dma,
        ],
        cost_estimate=pl.CostEstimate(flops=2 * 10**7, bytes_accessed=2 * 10**7, transcendentals=0),
        compiler_params=pltpu.CompilerParams(
            collective_id=1, has_side_effects=True, vmem_limit_bytes=62 * 2**20
        ),
        name="scatter",
    )(key_terms, value_terms, rows)


def place_kernel(a_ref, b_ref, c_ref, d_ref, k_ref, v_ref, o_ref, q_ref, key_ref, value_ref):
    _, _, core = place()
    for d, ref in enumerate((a_ref, b_ref, c_ref, d_ref)):
        cols = head_cols(d, (core + d % 2) % 2)
        width = ref.shape[1] // 2
        o_ref[:, cols] = ref[:, :width]
        q_ref[:, cols] = ref[:, width:]
    key_ref[...] = k_ref[...]
    value_ref[...] = v_ref[...]


def place_columns(pieces, key_grad, value_grad):
    shard = key_grad.shape[0]
    block = shard // 2
    feature = sum(piece.shape[1] for piece in pieces) // 2

    def spec(width):
        return pl.BlockSpec((block, width), lambda i: (i, 0))

    return pl.pallas_call(
        place_kernel,
        grid=(shard // block,),
        in_specs=[spec(piece.shape[1]) for piece in pieces] + [spec(HD)] * 2,
        out_specs=[spec(feature)] * 2 + [spec(HD)] * 2,
        out_shape=[jax.ShapeDtypeStruct((shard, feature), jnp.bfloat16)] * 2
        + [jax.ShapeDtypeStruct((shard, HD), jnp.bfloat16)] * 2,
        compiler_params=pltpu.CompilerParams(vmem_limit_bytes=62 * 2**20),
        name="place",
    )(*pieces, key_grad, value_grad)


def body(queries, key_rows, values, out_grad, lengths, block_owner):
    ranks = lax.axis_size("context")
    _, _, core = place()
    chips = [(a, b, c) for a in range(2) for b in range(YS) for c in range(2)]
    same = [(rank_of(a, b, c), rank_of(1 - a, b, c)) for a, b, c in chips]
    cross = [(rank_of(a, b, c), rank_of(1 - a, b, 1 - c)) for a, b, c in chips]
    near, far, keys, all_values = gather(queries, out_grad, key_rows, values, ranks)
    own, near, far_same, far_cross, dk, dv, pair_count = attend(
        queries, out_grad, near, far, core.astype(jnp.int32).reshape(1), keys, all_values, lengths, block_owner
    )
    far_same = lax.ppermute(far_same, "context", same)
    far_cross = lax.ppermute(far_cross, "context", cross)
    near, key_grad, value_grad = scatter(dk, dv, near, ranks)
    out, query_grad, key_grad, value_grad = place_columns(
        (own, near, far_same, far_cross), key_grad, value_grad
    )
    return out, query_grad, key_grad, value_grad, pair_count


def solution(mesh):
    rows = P(("dp", "context"), None)
    return jax.shard_map(
        body,
        mesh=mesh,
        in_specs=(rows, rows, rows, rows, P("dp"), P("dp")),
        out_specs=(rows, rows, rows, rows, P(("dp", "context"))),
        check_vma=False,
    )
```

```python
import functools
import math

import jax
import jax.numpy as jnp
from jax import lax
from jax.experimental import pallas as pl
from jax.experimental.pallas import tpu as pltpu
from jax.sharding import PartitionSpec as P

NEG_FILL = -1e30
MESH = pl.DeviceIdType.MESH
YS = 4
HD = 128
HEADS = (3, 2, 2, 1)
GROUP = 4
TILE = 256
SPAN = 4
PASS = 512
ONES = 16
LARGE = 1e12
QBLOCK = 256
DOC_MAX = 4096


def place():
    me = lax.axis_index("context")
    return me // (2 * YS), (me // 2) % YS, me % 2


def rank_of(x, y, core):
    return (x * YS + y) * 2 + core


def remote(src, dst, send_sem, recv_sem, rank):
    return pltpu.make_async_remote_copy(
        src_ref=src,
        dst_ref=dst,
        send_sem=send_sem,
        recv_sem=recv_sem,
        device_id={"context": rank},
        device_id_type=MESH,
    )


def enter(x, y, core, rows=False):
    barrier = pltpu.get_barrier_semaphore()
    others = [
        rank_of(x, y, 1 - core),
        rank_of(1 - x, y, core),
        rank_of(x, (y + 1) % YS, core),
        rank_of(x, (y + YS - 1) % YS, core),
    ]
    if rows:
        others.append(rank_of(1 - x, y, 1 - core))
    for other in others:
        pl.semaphore_signal(barrier, inc=1, device_id={"context": other}, device_id_type=MESH)
    pl.semaphore_wait(barrier, len(others))


def rows_at(begin, count):
    return pl.ds(pl.multiple_of(begin, count), count)


def head_cols(d):
    return pl.ds(sum(HEADS[:d]) * HD, HEADS[d] * HD)


def gather_kernel(
    q_ref, g_ref, k_ref, v_ref, rows1_ref, rows2_ref, rows3_ref, ka_ref, va_ref,
    own_sem, kv_send, kv_recv, core_send, core_recv, row_send, row_recv,
):
    x, y, core = place()
    shard = k_ref.shape[0]
    half = shard // 2
    up, down, far = (y + 1) % YS, (y + YS - 1) % YS, (y + 2) % YS
    x_rank = rank_of(1 - x, y, core)
    core_rank = rank_of(x, y, 1 - core)
    up_rank, down_rank = rank_of(x, up, core), rank_of(x, down, core)
    enter(x, y, core, rows=True)
    started = []

    def send(src, dst, send_sem, recv_sem, rank):
        copy = remote(src, dst, send_sem, recv_sem, rank)
        copy.start()
        started.append(copy)

    def landed(ref, recv_sem):
        remote(ref, ref, recv_sem, recv_sem, x_rank).wait_recv()

    own = []
    pairs = ((k_ref, ka_ref), (v_ref, va_ref))
    my_rows = rows_at(rank_of(x, y, core) * shard, shard)
    for a, (src, dst) in enumerate(pairs):
        send(src, dst.at[my_rows], kv_send.at[a, 0], kv_recv.at[a, 0], x_rank)
        send(src, dst.at[my_rows], kv_send.at[a, 1], kv_recv.at[a, 1], up_rank)
        send(src, dst.at[my_rows], kv_send.at[a, 2], kv_recv.at[a, 2], down_rank)
        send(src, dst.at[my_rows], core_send.at[a, 0], core_recv.at[a, 0], core_rank)
        copy = pltpu.make_async_copy(src, dst.at[my_rows], own_sem.at[a])
        copy.start()
        own.append(copy)

    landing = (rows1_ref, rows2_ref, rows3_ref)
    for a, src in enumerate((q_ref, g_ref)):
        for d in range(1, GROUP):
            tx, tc = (x + d // 2) % 2, (core + d % 2) % 2
            send(
                src.at[:, head_cols(d)], landing[d - 1].at[:, pl.ds(a * HEADS[d] * HD, HEADS[d] * HD)],
                row_send.at[a, d - 1], row_recv.at[a, d - 1], rank_of(tx, y, tc),
            )

    def forward(a, n, ref, rows, rank, relay):
        send(ref.at[rows], ref.at[rows], relay[0].at[a, n], relay[1].at[a, n], rank)

    y_relay, c_relay = (kv_send, kv_recv), (core_send, core_recv)

    def shard_rows(sx, sy, sc):
        return rows_at(rank_of(sx, sy, sc) * shard, shard)

    def half_rows(sx, sy, sc, h):
        return rows_at(rank_of(sx, sy, sc) * shard + h * half, half)

    for a, (_, dst) in enumerate(pairs):
        rows = shard_rows(1 - x, y, core)
        landed(dst.at[rows], kv_recv.at[a, 0])
        forward(a, 3, dst, rows, up_rank, y_relay)
        forward(a, 4, dst, rows, down_rank, y_relay)
        forward(a, 1, dst, rows, core_rank, c_relay)
    for n, sx in ((1, x), (3, 1 - x)):
        for a, (_, dst) in enumerate(pairs):
            landed(dst.at[shard_rows(sx, down, core)], kv_recv.at[a, n])
            forward(a, 4 + n, dst, half_rows(sx, down, core, 0), up_rank, y_relay)
            landed(dst.at[shard_rows(sx, up, core)], kv_recv.at[a, n + 1])
            forward(a, 5 + n, dst, half_rows(sx, up, core, 1), down_rank, y_relay)
            forward(a, 1 + n, dst, shard_rows(sx, down, core), core_rank, c_relay)
            forward(a, 2 + n, dst, shard_rows(sx, up, core), core_rank, c_relay)
    for n, sx in ((1, x), (3, 1 - x)):
        for a, (_, dst) in enumerate(pairs):
            for h in range(2):
                rows = half_rows(sx, far, core, h)
                landed(dst.at[rows], kv_recv.at[a, 4 + n + h])
                forward(a, 5 + n + h, dst, rows, core_rank, c_relay)
    for a, (_, dst) in enumerate(pairs):
        oc = 1 - core
        whole = ((x, y), (1 - x, y), (x, down), (x, up), (1 - x, down), (1 - x, up))
        for n, (sx, sy) in enumerate(whole):
            landed(dst.at[shard_rows(sx, sy, oc)], core_recv.at[a, n])
        for n, sx in ((1, x), (3, 1 - x)):
            for h in range(2):
                landed(dst.at[half_rows(sx, far, oc, h)], core_recv.at[a, 5 + n + h])
    for a in range(2):
        for d in range(1, GROUP):
            landed(landing[d - 1].at[:, pl.ds(a * HEADS[d] * HD, HEADS[d] * HD)], row_recv.at[a, d - 1])
    for copy in own:
        copy.wait()
    for copy in started:
        copy.wait_send()


def gather(queries, out_grad, keys, values, ranks):
    shard = queries.shape[0]
    bf16 = jnp.bfloat16
    any_spec = pl.BlockSpec(memory_space=pl.ANY)
    dma = pltpu.SemaphoreType.DMA
    return pl.pallas_call(
        gather_kernel,
        in_specs=[any_spec] * 4,
        out_specs=[any_spec] * 5,
        out_shape=[
            *[jax.ShapeDtypeStruct((shard, 2 * heads * HD), bf16) for heads in HEADS[1:]],
            jax.ShapeDtypeStruct((ranks * shard, HD), bf16),
            jax.ShapeDtypeStruct((ranks * shard, HD), bf16),
        ],
        scratch_shapes=[
            dma((2,)), dma((2, 9)), dma((2, 9)), dma((2, 10)), dma((2, 10)), dma((2, 3)), dma((2, 3)),
        ],
        compiler_params=pltpu.CompilerParams(collective_id=0, has_side_effects=True, vmem_limit_bytes=62 * 2**20),
        name="gather",
    )(queries, out_grad, keys, values)


def dot(a, b):
    return jnp.dot(a, b, preferred_element_type=jnp.float32)


def attend_block(
    heads, block, first, len_ref, inputs, outputs, k_ref, v_ref, kt_ref, vt_ref, dka_ref, dva_ref,
    p_ref, qt_ref, gt_ref, qn_ref, gn_ref, ds_ref, acc_ref,
):
    f32, bf16 = jnp.float32, jnp.bfloat16
    cols = block * heads
    docs = len_ref.shape[0]
    scale = 1.0 / math.sqrt(HD)
    scale2 = scale * math.log2(math.e)
    row_pos = first + lax.rem(lax.broadcasted_iota(jnp.int32, (1, cols), 1), block)
    row_start = jnp.zeros((1, cols), jnp.int32)
    first_start, last_start, end = jnp.int32(0), jnp.int32(0), jnp.int32(0)
    for d in range(docs):
        end = end + len_ref[d]
        row_start = jnp.where(row_pos >= end, end, row_start)
        first_start = jnp.where(first >= end, end, first_start)
        last_start = jnp.where(first + block - 1 >= end, end, last_start)
    low = lax.div(first_start, TILE)
    high = lax.div(first + block - 1, TILE) + 1

    own_keys = kt_ref[:, rows_at(first, block)].astype(f32)
    shift = []
    for h in range(heads):
        for chosen, q_ref, g_ref in inputs:

            @pl.when(chosen)
            def _(h=h, q_ref=q_ref, g_ref=g_ref):
                qt_ref[:, h * block : (h + 1) * block] = q_ref[:, h * HD : (h + 1) * HD].T
                gt_ref[:, h * block : (h + 1) * block] = g_ref[:, h * HD : (h + 1) * HD].T

        q_t = qt_ref[:, h * block : (h + 1) * block]
        shift.append(jnp.sum(q_t.astype(f32) * own_keys, axis=0, keepdims=True) * scale2)
    shift = jnp.concatenate(shift, axis=1)

    def keep(result, at):
        for chosen, r_ref in outputs:

            @pl.when(chosen)
            def _(r_ref=r_ref):
                for h in range(heads):
                    cut = result[h * block : (h + 1) * block, :]
                    r_ref[:, (at + h) * HD : (at + h + 1) * HD] = cut

    def key_rows(t, count):
        return pl.ds(pl.multiple_of(t * TILE, TILE), count)

    def kept_rows(t, count):
        return pl.ds(pl.multiple_of((t - low) * TILE, TILE), count)

    def sweep(piece):
        count = high - low
        groups = lax.div(count, SPAN)

        def one(g, carry):
            piece(low + g * SPAN, SPAN * TILE, False)
            return carry

        lax.fori_loop(0, groups, one, 0)
        at = low + groups * SPAN
        size = SPAN // 2
        while size:
            has = lax.rem(lax.div(count, size), 2)

            @pl.when(has == 1)
            def _(at=at, size=size):
                piece(at, size * TILE, True)

            at = at + has * size
            size //= 2

    def forward(shift):
        acc_ref[...] = jnp.zeros(acc_ref.shape, f32)

        def piece(t, rows, last):
            def run(mask):
                acc = None
                part = min(rows, PASS)
                for i in range(0, rows, part):
                    tile = t + i // TILE
                    s = dot(k_ref[key_rows(tile, part), :], qt_ref[...]) * scale2 - shift
                    if mask:
                        pos = t * TILE + i + lax.broadcasted_iota(jnp.int32, s.shape, 0)
                        s = jnp.where((pos >= row_start) & (pos <= row_pos), s, NEG_FILL)
                    p_ref[kept_rows(tile, part), :] = jnp.exp2(s).astype(bf16)
                    term = dot(vt_ref[:, key_rows(tile, part)], p_ref[kept_rows(tile, part), :])
                    acc = term if acc is None else acc + term
                acc_ref[...] += acc

            if last:
                run(True)
            else:
                edge = (t * TILE < last_start) | (t * TILE + rows - 1 > first)
                pl.when(edge)(lambda: run(True))
                pl.when(jnp.logical_not(edge))(lambda: run(False))

        sweep(piece)

    forward(shift)

    @pl.when(jnp.logical_not(jnp.max(acc_ref[HD : HD + 1, :]) < LARGE))
    def _():
        def peak_pass(t, peak):
            s = dot(k_ref[key_rows(t, TILE), :], qt_ref[...]) * scale2
            pos = t * TILE + lax.broadcasted_iota(jnp.int32, s.shape, 0)
            s = jnp.where((pos >= row_start) & (pos <= row_pos), s, NEG_FILL)
            return jnp.maximum(peak, jnp.max(s.reshape(TILE // 8, 8, cols), axis=0))

        peak = lax.fori_loop(low, high, peak_pass, jnp.full((8, cols), NEG_FILL, f32))
        forward(jnp.max(peak, axis=0, keepdims=True))

    inverse = 1.0 / acc_ref[HD : HD + 1, :]
    out = (acc_ref[0:HD, :] * inverse).astype(bf16)
    grad_t = gt_ref[...].astype(f32)
    grad_dot = jnp.sum(out.astype(f32) * grad_t, axis=0, keepdims=True)
    gn_ref[...] = (grad_t * inverse).astype(bf16).T
    qn_ref[...] = (qt_ref[...].astype(f32) * inverse).astype(bf16).T
    keep(out.T, 0)
    acc_ref[0:HD, :] = jnp.zeros((HD, cols), f32)

    def backward(t, rows, last):
        keys, kept = key_rows(t, rows), kept_rows(t, rows)
        grad_p = dot(v_ref[keys, :], gt_ref[...])
        ds_ref[0:rows, :] = (p_ref[kept, :].astype(f32) * (grad_p - grad_dot)).astype(bf16)
        dva_ref[keys, :] += dot(p_ref[kept, :], gn_ref[...])
        dka_ref[keys, :] += dot(ds_ref[0:rows, :], qn_ref[...])
        acc_ref[0:HD, :] += dot(kt_ref[:, keys], ds_ref[0:rows, :])

    sweep(backward)
    query_grad = (acc_ref[0:HD, :] * (inverse * scale)).astype(bf16).T
    keep(query_grad, heads)


def attend_kernel(
    len_ref, owner_ref, q0_ref, g0_ref, q1_ref, g1_ref, q2_ref, g2_ref, q3_ref, g3_ref, k_ref, v_ref,
    r0_ref, r1_ref, r2_ref, r3_ref, dk_ref, dv_ref, pair_ref,
    kt_ref, vt_ref, p_ref, qt_ref, gt_ref, qn_ref, gn_ref, dka_ref, dva_ref, ds_ref, acc_ref,
):
    blk = pl.program_id(0)
    block = q0_ref.shape[0]
    tokens = k_ref.shape[0]
    docs = len_ref.shape[0]
    f32, bf16 = jnp.float32, jnp.bfloat16
    scale = 1.0 / math.sqrt(HD)
    x, y, core = place()
    per_chip = tokens // (2 * YS)
    per_core = pl.num_programs(0) // GROUP

    reach = []
    for chip in (y, YS + y):
        begin, end = jnp.int32(0), jnp.int32(0)
        for d in range(docs):
            end = end + len_ref[d]
            begin = jnp.where(chip * per_chip >= end, end, begin)
        reach.append((lax.div(begin, PASS), lax.div((chip + 1) * per_chip, PASS)))
    reach[1] = (jnp.maximum(reach[1][0], reach[0][1]), reach[1][1])

    @pl.when(blk == 0)
    def _():
        def prepare(i, carry):
            rows = rows_at(i * PASS, PASS)
            kt_ref[:, rows] = k_ref[rows, :].T
            vt_ref[0:HD, rows] = v_ref[rows, :].T
            vt_ref[HD:, rows] = jnp.ones((ONES, PASS), bf16)
            dka_ref[rows, :] = jnp.zeros((PASS, HD), f32)
            dva_ref[rows, :] = jnp.zeros((PASS, HD), f32)
            return carry

        for low_chunk, high_chunk in reach:
            lax.fori_loop(low_chunk, high_chunk, prepare, 0)
        blocks = owner_ref.shape[1]
        block_rows = tokens // blocks
        shape = (block_rows, blocks)
        pos = lax.broadcasted_iota(jnp.int32, shape, 1) * block_rows
        pos = pos + lax.broadcasted_iota(jnp.int32, shape, 0)
        begin, end = jnp.zeros(shape, jnp.int32), jnp.int32(0)
        for d in range(docs):
            end = end + len_ref[d]
            begin = jnp.where(pos >= end, end, begin)
        counts = (pos - begin + 1).astype(f32)
        counts = jnp.where(owner_ref[...] == lax.axis_index("context"), counts, 0.0)
        pair_ref[0] = jnp.sum(counts)

    part = lax.div(blk, per_core)
    chip = lax.rem(x + lax.div(part, 2), 2) * YS + y
    row_core = lax.rem(core + part, 2)
    first = chip * per_chip + row_core * (per_chip // 2) + lax.rem(blk, per_core) * block

    def work(heads, inputs, outputs):
        cols = block * heads
        scratch = (
            p_ref.at[:, 0:cols], qt_ref.at[:, 0:cols], gt_ref.at[:, 0:cols], qn_ref.at[0:cols], gn_ref.at[0:cols],
            ds_ref.at[:, 0:cols], acc_ref.at[:, 0:cols],
        )
        attend_block(
            heads, block, first, len_ref, inputs, outputs, k_ref, v_ref, kt_ref, vt_ref, dka_ref, dva_ref, *scratch
        )

    inputs = ((q0_ref, g0_ref), (q1_ref, g1_ref), (q2_ref, g2_ref), (q3_ref, g3_ref))
    outputs = (r0_ref, r1_ref, r2_ref, r3_ref)
    for heads in sorted(set(HEADS)):
        parts = [n for n in range(GROUP) if HEADS[n] == heads]
        chosen = [part == n for n in parts]

        @pl.when(functools.reduce(jnp.logical_or, chosen))
        def _(heads=heads, parts=parts, chosen=chosen):
            work(
                heads, [(c, *inputs[n]) for c, n in zip(chosen, parts)],
                [(c, outputs[n]) for c, n in zip(chosen, parts)],
            )

    @pl.when(blk == pl.num_programs(0) - 1)
    def _():
        def finish(i, carry):
            rows = rows_at(i * PASS, PASS)
            inside = jnp.bool_(False)
            for low_chunk, high_chunk in reach:
                inside = inside | ((i >= low_chunk) & (i < high_chunk))
            for sums, out_ref, factor in ((dka_ref, dk_ref, scale), (dva_ref, dv_ref, 1.0)):

                @pl.when(inside)
                def _(sums=sums, out_ref=out_ref, factor=factor):
                    out_ref[rows, :] = (sums[rows, :] * factor).astype(bf16)

                @pl.when(jnp.logical_not(inside))
                def _(out_ref=out_ref):
                    out_ref[rows, :] = jnp.zeros((PASS, HD), bf16)

            return carry

        lax.fori_loop(0, tokens // PASS, finish, 0)


def attend(queries, out_grad, rows, keys, values, lengths, block_owner):
    tokens = keys.shape[0]
    shard = queries.shape[0]
    per_core = shard // QBLOCK
    span = ((DOC_MAX + QBLOCK + TILE - 2) // TILE + 1) * TILE
    qcols = QBLOCK * max(HEADS)

    def spec(n, width, col):
        return pl.BlockSpec((QBLOCK, width), lambda i, *_: (jnp.clip(i - n * per_core, 0, per_core - 1), col))

    row_specs, row_args = [spec(0, HEADS[0] * HD, 0)] * 2, [queries, out_grad]
    for n in range(1, GROUP):
        row_specs += [spec(n, HEADS[n] * HD, 0), spec(n, HEADS[n] * HD, 1)]
        row_args += [rows[n - 1]] * 2
    full_spec = pl.BlockSpec((tokens, HD), lambda i, *_: (0, 0))
    bf16, f32 = jnp.bfloat16, jnp.float32
    owner_spec = pl.BlockSpec((1, block_owner.shape[0]), lambda i, *_: (0, 0))
    return pl.pallas_call(
        attend_kernel,
        grid_spec=pltpu.PrefetchScalarGridSpec(
            num_scalar_prefetch=1,
            grid=(GROUP * per_core,),
            in_specs=[
                owner_spec, *row_specs, full_spec, full_spec,
            ],
            out_specs=[spec(n, 2 * HEADS[n] * HD, 0) for n in range(GROUP)]
            + [full_spec, full_spec, pl.BlockSpec(memory_space=pltpu.SMEM)],
            scratch_shapes=[
                pltpu.VMEM((HD, tokens), bf16),
                pltpu.VMEM((HD + ONES, tokens), bf16),
                pltpu.VMEM((span, qcols), bf16),
                pltpu.VMEM((HD, qcols), bf16),
                pltpu.VMEM((HD, qcols), bf16),
                pltpu.VMEM((qcols, HD), bf16),
                pltpu.VMEM((qcols, HD), bf16),
                pltpu.VMEM((tokens, HD), f32),
                pltpu.VMEM((tokens, HD), f32),
                pltpu.VMEM((SPAN * TILE, qcols), bf16),
                pltpu.VMEM((HD + ONES, qcols), f32),
            ],
        ),
        out_shape=[jax.ShapeDtypeStruct((shard, 2 * heads * HD), bf16) for heads in HEADS]
        + [jax.ShapeDtypeStruct((tokens, HD), bf16)] * 2
        + [jax.ShapeDtypeStruct((1,), f32)],
        cost_estimate=pl.CostEstimate(flops=2 * 10**10, bytes_accessed=2 * 10**7, transcendentals=5 * 10**6),
        compiler_params=pltpu.CompilerParams(vmem_limit_bytes=62 * 2**20),
        name="attend",
    )(lengths, block_owner.reshape(1, -1), *row_args, keys, values)


def scatter_kernel(
    dk_ref, dv_ref, rows_ref, back_ref, key_ref, value_ref,
    part, from_core, from_far, from_near, from_x,
    part_sem, core_send, core_recv, far_send, far_recv, near_send, near_recv,
    x_send, x_recv, row_send, row_recv,
):
    x, y, core = place()
    shard = key_ref.shape[0]
    half = shard // 2
    up, down, far = (y + 1) % YS, (y + YS - 1) % YS, (y + 2) % YS
    x_rank = rank_of(1 - x, y, core)
    core_rank = rank_of(x, y, 1 - core)
    up_rank, down_rank = rank_of(x, up, core), rank_of(x, down, core)
    started = []

    def send(src, dst, send_sem, recv_sem, rank):
        copy = remote(src, dst, send_sem, recv_sem, rank)
        copy.start()
        started.append(copy)

    def landed(ref, recv_sem):
        remote(ref, ref, recv_sem, recv_sem, x_rank).wait_recv()

    pairs = (dk_ref, dv_ref)
    order = [(1 - x, far), (x, far), (1 - x, up), (x, up), (1 - x, down), (x, down), (1 - x, y), (x, y)]
    loads = []
    for n, (sx, sy) in enumerate(order):
        for a, src in enumerate(pairs):
            rows = rows_at(rank_of(sx, sy, core) * shard, shard)
            copy = pltpu.make_async_copy(src.at[rows], part.at[a, n], part_sem.at[a, n])
            copy.start()
            loads.append(copy)
    enter(x, y, core)
    for n, (sx, sy) in enumerate(order):
        for a, src in enumerate(pairs):
            rows = rows_at(rank_of(sx, sy, 1 - core) * shard, shard)
            send(src.at[rows], from_core.at[a, n], core_send.at[a, n], core_recv.at[a, n], core_rank)

    send(rows_ref, back_ref, row_send, row_recv, core_rank)

    def add(ref, other):
        ref[...] = (ref[...].astype(jnp.float32) + other[...].astype(jnp.float32)).astype(jnp.bfloat16)

    def core_sum(a, n):
        loads[2 * n + a].wait()
        landed(from_core.at[a, n], core_recv.at[a, n])
        add(part.at[a, n], from_core.at[a, n])

    for n in range(2):
        for a in range(2):
            core_sum(a, n)
            for h, rank in ((0, up_rank), (1, down_rank)):
                send(
                    part.at[a, n, pl.ds(h * half, half)], from_far.at[a, n, h],
                    far_send.at[a, n, h], far_recv.at[a, n, h], rank,
                )
    for n in range(2):
        for a in range(2):
            for j, rank in ((0, up_rank), (1, down_rank)):
                core_sum(a, 2 + 2 * j + n)
                free = 1 - j
                send(
                    part.at[a, 2 + 2 * j + n, pl.ds(free * half, half)],
                    from_near.at[a, n, j, pl.ds(free * half, half)],
                    near_send.at[a, n, j, free], near_recv.at[a, n, j, free], rank,
                )
    for n in range(2):
        for a in range(2):
            for j, rank in ((0, up_rank), (1, down_rank)):
                landed(from_far.at[a, n, j], far_recv.at[a, n, j])
                mine = part.at[a, 2 + 2 * j + n, pl.ds(j * half, half)]
                add(mine, from_far.at[a, n, j])
                send(
                    mine, from_near.at[a, n, j, pl.ds(j * half, half)],
                    near_send.at[a, n, j, j], near_recv.at[a, n, j, j], rank,
                )
    for n in range(2):
        for a in range(2):
            core_sum(a, 6 + n)
            for j in range(2):
                for h in (1 - j, j):
                    landed(from_near.at[a, n, j, pl.ds(h * half, half)], near_recv.at[a, n, j, h])
            total = part[a, 6 + n].astype(jnp.float32)
            total = total + from_near[a, n, 0].astype(jnp.float32)
            total = total + from_near[a, n, 1].astype(jnp.float32)
            part[a, 6 + n] = total.astype(jnp.bfloat16)
            if n == 0:
                send(part.at[a, 6], from_x.at[a], x_send.at[a], x_recv.at[a], x_rank)
    for a, dst in enumerate((key_ref, value_ref)):
        landed(from_x.at[a], x_recv.at[a])
        dst[...] = (part[a, 7].astype(jnp.float32) + from_x[a].astype(jnp.float32)).astype(jnp.bfloat16)
    landed(back_ref, row_recv)
    for copy in started:
        copy.wait_send()


def scatter(key_terms, value_terms, rows, ranks):
    tokens = key_terms.shape[0]
    shard = tokens // ranks
    half = shard // 2
    bf16 = jnp.bfloat16
    any_spec = pl.BlockSpec(memory_space=pl.ANY)
    vmem_spec = pl.BlockSpec(memory_space=pltpu.VMEM)
    dma = pltpu.SemaphoreType.DMA
    return pl.pallas_call(
        scatter_kernel,
        in_specs=[any_spec] * 3,
        out_specs=[any_spec, vmem_spec, vmem_spec],
        out_shape=[
            jax.ShapeDtypeStruct(rows.shape, bf16),
            jax.ShapeDtypeStruct((shard, HD), bf16),
            jax.ShapeDtypeStruct((shard, HD), bf16),
        ],
        scratch_shapes=[
            pltpu.VMEM((2, ranks // 2, shard, HD), bf16),
            pltpu.VMEM((2, ranks // 2, shard, HD), bf16),
            pltpu.VMEM((2, 2, 2, half, HD), bf16),
            pltpu.VMEM((2, 2, 2, shard, HD), bf16),
            pltpu.VMEM((2, shard, HD), bf16),
            dma((2, 8)), dma((2, 8)), dma((2, 8)), dma((2, 2, 2)), dma((2, 2, 2)),
            dma((2, 2, 2, 2)), dma((2, 2, 2, 2)), dma((2,)), dma((2,)), dma, dma,
        ],
        cost_estimate=pl.CostEstimate(flops=2 * 10**7, bytes_accessed=2 * 10**7, transcendentals=0),
        compiler_params=pltpu.CompilerParams(
            collective_id=1, has_side_effects=True, vmem_limit_bytes=62 * 2**20
        ),
        name="scatter",
    )(key_terms, value_terms, rows)


def place_kernel(a_ref, b_ref, c_ref, d_ref, k_ref, v_ref, o_ref, q_ref, key_ref, value_ref):
    for d, ref in enumerate((a_ref, b_ref, c_ref, d_ref)):
        cols = head_cols(d)
        width = ref.shape[1] // 2
        o_ref[:, cols] = ref[:, :width]
        q_ref[:, cols] = ref[:, width:]
    key_ref[...] = k_ref[...]
    value_ref[...] = v_ref[...]


def place_columns(pieces, key_grad, value_grad):
    shard = key_grad.shape[0]
    block = shard // 2
    feature = sum(piece.shape[1] for piece in pieces) // 2

    def spec(width):
        return pl.BlockSpec((block, width), lambda i: (i, 0))

    return pl.pallas_call(
        place_kernel,
        grid=(shard // block,),
        in_specs=[spec(piece.shape[1]) for piece in pieces] + [spec(HD)] * 2,
        out_specs=[spec(feature)] * 2 + [spec(HD)] * 2,
        out_shape=[jax.ShapeDtypeStruct((shard, feature), jnp.bfloat16)] * 2
        + [jax.ShapeDtypeStruct((shard, HD), jnp.bfloat16)] * 2,
        compiler_params=pltpu.CompilerParams(vmem_limit_bytes=62 * 2**20),
        name="place",
    )(*pieces, key_grad, value_grad)


def body(queries, key_rows, values, out_grad, lengths, block_owner):
    ranks = lax.axis_size("context")
    chips = [(a, b, c) for a in range(2) for b in range(YS) for c in range(2)]
    same = [(rank_of(a, b, c), rank_of(1 - a, b, c)) for a, b, c in chips]
    cross = [(rank_of(a, b, c), rank_of(1 - a, b, 1 - c)) for a, b, c in chips]
    *rows, keys, all_values = gather(queries, out_grad, key_rows, values, ranks)
    own, near, far_same, far_cross, dk, dv, pair_count = attend(
        queries, out_grad, rows, keys, all_values, lengths, block_owner
    )
    far_same = lax.ppermute(far_same, "context", same)
    far_cross = lax.ppermute(far_cross, "context", cross)
    near, key_grad, value_grad = scatter(dk, dv, near, ranks)
    out, query_grad, key_grad, value_grad = place_columns(
        (own, near, far_same, far_cross), key_grad, value_grad
    )
    return out, query_grad, key_grad, value_grad, pair_count


def solution(mesh):
    rows = P(("dp", "context"), None)
    return jax.shard_map(
        body,
        mesh=mesh,
        in_specs=(rows, rows, rows, rows, P("dp"), P("dp")),
        out_specs=(rows, rows, rows, rows, P(("dp", "context"))),
        check_vma=False,
    )
```

```python
import functools
import math

import jax
import jax.numpy as jnp
from jax import lax
from jax.experimental import pallas as pl
from jax.experimental.pallas import tpu as pltpu
from jax.sharding import PartitionSpec as P

NEG_FILL = -1e30
MESH = pl.DeviceIdType.MESH
YS = 4
HD = 128
HEADS = (3, 2, 2, 1)
GROUP = 4
TILE = 256
SPAN = 4
PASS = 512
ONES = 16
LARGE = 1e12
QBLOCK = 256
DOC_MAX = 4096


def place():
    me = lax.axis_index("context")
    return me // (2 * YS), (me // 2) % YS, me % 2


def rank_of(x, y, core):
    return (x * YS + y) * 2 + core


def remote(src, dst, send_sem, recv_sem, rank):
    return pltpu.make_async_remote_copy(
        src_ref=src,
        dst_ref=dst,
        send_sem=send_sem,
        recv_sem=recv_sem,
        device_id={"context": rank},
        device_id_type=MESH,
    )


def enter(x, y, core, rows=False):
    barrier = pltpu.get_barrier_semaphore()
    others = [
        rank_of(x, y, 1 - core),
        rank_of(1 - x, y, core),
        rank_of(x, (y + 1) % YS, core),
        rank_of(x, (y + YS - 1) % YS, core),
    ]
    if rows:
        others.append(rank_of(1 - x, y, 1 - core))
    for other in others:
        pl.semaphore_signal(barrier, inc=1, device_id={"context": other}, device_id_type=MESH)
    pl.semaphore_wait(barrier, len(others))


def rows_at(begin, count):
    return pl.ds(pl.multiple_of(begin, count), count)


def head_cols(d):
    return pl.ds(sum(HEADS[:d]) * HD, HEADS[d] * HD)


def gather_kernel(
    q_ref, g_ref, k_ref, v_ref, rows1_ref, rows2_ref, rows3_ref, ka_ref, va_ref,
    own_sem, kv_send, kv_recv, core_send, core_recv, row_send, row_recv,
):
    x, y, core = place()
    shard = k_ref.shape[0]
    half = shard // 2
    up, down, far = (y + 1) % YS, (y + YS - 1) % YS, (y + 2) % YS
    x_rank = rank_of(1 - x, y, core)
    core_rank = rank_of(x, y, 1 - core)
    up_rank, down_rank = rank_of(x, up, core), rank_of(x, down, core)
    enter(x, y, core, rows=True)
    started = []

    def send(src, dst, send_sem, recv_sem, rank):
        copy = remote(src, dst, send_sem, recv_sem, rank)
        copy.start()
        started.append(copy)

    def landed(ref, recv_sem):
        remote(ref, ref, recv_sem, recv_sem, x_rank).wait_recv()

    own = []
    pairs = ((k_ref, ka_ref), (v_ref, va_ref))
    my_rows = rows_at(rank_of(x, y, core) * shard, shard)
    for a, (src, dst) in enumerate(pairs):
        send(src, dst.at[my_rows], kv_send.at[a, 0], kv_recv.at[a, 0], x_rank)
        send(src, dst.at[my_rows], kv_send.at[a, 1], kv_recv.at[a, 1], up_rank)
        send(src, dst.at[my_rows], kv_send.at[a, 2], kv_recv.at[a, 2], down_rank)
        send(src, dst.at[my_rows], core_send.at[a, 0], core_recv.at[a, 0], core_rank)
        copy = pltpu.make_async_copy(src, dst.at[my_rows], own_sem.at[a])
        copy.start()
        own.append(copy)

    landing = (rows1_ref, rows2_ref, rows3_ref)
    for a, src in enumerate((q_ref, g_ref)):
        for d in range(1, GROUP):
            tx, tc = (x + d // 2) % 2, (core + d % 2) % 2
            send(
                src.at[:, head_cols(d)], landing[d - 1].at[:, pl.ds(a * HEADS[d] * HD, HEADS[d] * HD)],
                row_send.at[a, d - 1], row_recv.at[a, d - 1], rank_of(tx, y, tc),
            )

    def forward(a, n, ref, rows, rank, relay):
        send(ref.at[rows], ref.at[rows], relay[0].at[a, n], relay[1].at[a, n], rank)

    y_relay, c_relay = (kv_send, kv_recv), (core_send, core_recv)

    def shard_rows(sx, sy, sc):
        return rows_at(rank_of(sx, sy, sc) * shard, shard)

    def half_rows(sx, sy, sc, h):
        return rows_at(rank_of(sx, sy, sc) * shard + h * half, half)

    for a, (_, dst) in enumerate(pairs):
        rows = shard_rows(1 - x, y, core)
        landed(dst.at[rows], kv_recv.at[a, 0])
        forward(a, 3, dst, rows, up_rank, y_relay)
        forward(a, 4, dst, rows, down_rank, y_relay)
        forward(a, 1, dst, rows, core_rank, c_relay)
    for n, sx in ((1, x), (3, 1 - x)):
        for a, (_, dst) in enumerate(pairs):
            landed(dst.at[shard_rows(sx, down, core)], kv_recv.at[a, n])
            forward(a, 4 + n, dst, half_rows(sx, down, core, 0), up_rank, y_relay)
            landed(dst.at[shard_rows(sx, up, core)], kv_recv.at[a, n + 1])
            forward(a, 5 + n, dst, half_rows(sx, up, core, 1), down_rank, y_relay)
            forward(a, 1 + n, dst, shard_rows(sx, down, core), core_rank, c_relay)
            forward(a, 2 + n, dst, shard_rows(sx, up, core), core_rank, c_relay)
    for n, sx in ((1, x), (3, 1 - x)):
        for a, (_, dst) in enumerate(pairs):
            for h in range(2):
                rows = half_rows(sx, far, core, h)
                landed(dst.at[rows], kv_recv.at[a, 4 + n + h])
                forward(a, 5 + n + h, dst, rows, core_rank, c_relay)
    for a, (_, dst) in enumerate(pairs):
        oc = 1 - core
        whole = ((x, y), (1 - x, y), (x, down), (x, up), (1 - x, down), (1 - x, up))
        for n, (sx, sy) in enumerate(whole):
            landed(dst.at[shard_rows(sx, sy, oc)], core_recv.at[a, n])
        for n, sx in ((1, x), (3, 1 - x)):
            for h in range(2):
                landed(dst.at[half_rows(sx, far, oc, h)], core_recv.at[a, 5 + n + h])
    for a in range(2):
        for d in range(1, GROUP):
            landed(landing[d - 1].at[:, pl.ds(a * HEADS[d] * HD, HEADS[d] * HD)], row_recv.at[a, d - 1])
    for copy in own:
        copy.wait()
    for copy in started:
        copy.wait_send()


def gather(queries, out_grad, keys, values, ranks):
    shard = queries.shape[0]
    bf16 = jnp.bfloat16
    any_spec = pl.BlockSpec(memory_space=pl.ANY)
    dma = pltpu.SemaphoreType.DMA
    return pl.pallas_call(
        gather_kernel,
        in_specs=[any_spec] * 4,
        out_specs=[any_spec] * 5,
        out_shape=[
            *[jax.ShapeDtypeStruct((shard, 2 * heads * HD), bf16) for heads in HEADS[1:]],
            jax.ShapeDtypeStruct((ranks * shard, HD), bf16),
            jax.ShapeDtypeStruct((ranks * shard, HD), bf16),
        ],
        scratch_shapes=[
            dma((2,)), dma((2, 9)), dma((2, 9)), dma((2, 10)), dma((2, 10)), dma((2, 3)), dma((2, 3)),
        ],
        compiler_params=pltpu.CompilerParams(collective_id=0, has_side_effects=True, vmem_limit_bytes=62 * 2**20),
        name="gather",
    )(queries, out_grad, keys, values)


def dot(a, b):
    return jnp.dot(a, b, preferred_element_type=jnp.float32)


def attend_block(
    heads, block, first, len_ref, inputs, outputs, k_ref, v_ref, kt_ref, vt_ref, dka_ref, dva_ref,
    p_ref, qt_ref, gt_ref, qn_ref, gn_ref, ds_ref, acc_ref, shift_ref,
):
    f32, bf16 = jnp.float32, jnp.bfloat16
    cols = block * heads
    docs = len_ref.shape[0]
    scale = 1.0 / math.sqrt(HD)
    scale2 = scale * math.log2(math.e)
    row_pos = first + lax.rem(lax.broadcasted_iota(jnp.int32, (1, cols), 1), block)
    row_start = jnp.zeros((1, cols), jnp.int32)
    first_start, last_start, end = jnp.int32(0), jnp.int32(0), jnp.int32(0)
    for d in range(docs):
        end = end + len_ref[d]
        row_start = jnp.where(row_pos >= end, end, row_start)
        first_start = jnp.where(first >= end, end, first_start)
        last_start = jnp.where(first + block - 1 >= end, end, last_start)
    low = lax.div(first_start, TILE)
    high = lax.div(first + block - 1, TILE) + 1

    own_keys = kt_ref[:, rows_at(first, block)].astype(f32)
    shift = []
    for h in range(heads):
        for chosen, q_ref, g_ref in inputs:

            @pl.when(chosen)
            def _(h=h, q_ref=q_ref, g_ref=g_ref):
                qt_ref[:, h * block : (h + 1) * block] = q_ref[:, h * HD : (h + 1) * HD].T
                gt_ref[:, h * block : (h + 1) * block] = g_ref[:, h * HD : (h + 1) * HD].T

        q_t = qt_ref[:, h * block : (h + 1) * block]
        shift.append(jnp.sum(q_t.astype(f32) * own_keys, axis=0, keepdims=True) * scale2)
    shift = jnp.concatenate(shift, axis=1)

    def keep(result, at):
        for chosen, r_ref in outputs:

            @pl.when(chosen)
            def _(r_ref=r_ref):
                for h in range(heads):
                    cut = result[h * block : (h + 1) * block, :]
                    r_ref[:, (at + h) * HD : (at + h + 1) * HD] = cut

    def key_rows(t, count):
        return pl.ds(pl.multiple_of(t * TILE, TILE), count)

    def kept_rows(t, count):
        return pl.ds(pl.multiple_of((t - low) * TILE, TILE), count)

    def sweep(piece):
        count = high - low
        groups = lax.div(count, SPAN)

        def one(g, carry):
            piece(low + g * SPAN, SPAN * TILE, False)
            return carry

        lax.fori_loop(0, groups, one, 0)
        left = count - groups * SPAN
        for size in range(1, SPAN):

            @pl.when(left == size)
            def _(size=size):
                piece(low + groups * SPAN, size * TILE, True)

    def forward(carry):
        tries, _ = carry
        acc_ref[...] = jnp.zeros(acc_ref.shape, f32)
        shift = shift_ref[0:1, 0:cols]

        def piece(t, rows, last):
            def run(mask):
                keys, kept = key_rows(t, rows), kept_rows(t, rows)
                s = dot(k_ref[keys, :], qt_ref[...]) * scale2 - shift
                if mask:
                    pos = t * TILE + lax.broadcasted_iota(jnp.int32, s.shape, 0)
                    s = jnp.where((pos >= row_start) & (pos <= row_pos), s, NEG_FILL)
                p_ref[kept, :] = jnp.exp2(s).astype(bf16)
                acc_ref[...] += dot(vt_ref[:, keys], p_ref[kept, :])

            if last:
                run(True)
            else:
                edge = (t * TILE < last_start) | (t * TILE + rows - 1 > first)
                pl.when(edge)(lambda: run(True))
                pl.when(jnp.logical_not(edge))(lambda: run(False))

        sweep(piece)
        large = jnp.logical_not(jnp.max(acc_ref[HD : HD + 1, :]) < LARGE)

        @pl.when(large)
        def _():
            def peak_pass(t, peak):
                s = dot(k_ref[key_rows(t, TILE), :], qt_ref[...]) * scale2
                pos = t * TILE + lax.broadcasted_iota(jnp.int32, s.shape, 0)
                s = jnp.where((pos >= row_start) & (pos <= row_pos), s, NEG_FILL)
                return jnp.maximum(peak, jnp.max(s.reshape(TILE // 8, 8, cols), axis=0))

            peak = lax.fori_loop(low, high, peak_pass, jnp.full((8, cols), NEG_FILL, f32))
            shift_ref[0:1, 0:cols] = jnp.max(peak, axis=0, keepdims=True)

        return tries + 1, large.astype(jnp.int32)

    shift_ref[0:1, 0:cols] = shift
    lax.while_loop(lambda carry: (carry[0] < 2) & (carry[1] > 0), forward, (jnp.int32(0), jnp.int32(1)))

    inverse = 1.0 / acc_ref[HD : HD + 1, :]
    out = (acc_ref[0:HD, :] * inverse).astype(bf16)
    grad_t = gt_ref[...].astype(f32)
    grad_dot = jnp.sum(out.astype(f32) * grad_t, axis=0, keepdims=True)
    gn_ref[...] = (grad_t * inverse).astype(bf16).T
    qn_ref[...] = (qt_ref[...].astype(f32) * inverse).astype(bf16).T
    keep(out.T, 0)
    acc_ref[0:HD, :] = jnp.zeros((HD, cols), f32)

    def backward(t, rows, last):
        keys, kept = key_rows(t, rows), kept_rows(t, rows)
        grad_p = dot(v_ref[keys, :], gt_ref[...])
        ds_ref[0:rows, :] = (p_ref[kept, :].astype(f32) * (grad_p - grad_dot)).astype(bf16)
        dva_ref[keys, :] += dot(p_ref[kept, :], gn_ref[...])
        dka_ref[keys, :] += dot(ds_ref[0:rows, :], qn_ref[...])
        acc_ref[0:HD, :] += dot(kt_ref[:, keys], ds_ref[0:rows, :])

    sweep(backward)
    query_grad = (acc_ref[0:HD, :] * (inverse * scale)).astype(bf16).T
    keep(query_grad, heads)


def attend_kernel(
    len_ref, owner_ref, q0_ref, g0_ref, q1_ref, g1_ref, q2_ref, g2_ref, q3_ref, g3_ref, k_ref, v_ref,
    r0_ref, r1_ref, r2_ref, r3_ref, dk_ref, dv_ref, pair_ref,
    kt_ref, vt_ref, p_ref, qt_ref, gt_ref, qn_ref, gn_ref, dka_ref, dva_ref, ds_ref, acc_ref, shift_ref,
):
    blk = pl.program_id(0)
    block = q0_ref.shape[0]
    tokens = k_ref.shape[0]
    docs = len_ref.shape[0]
    f32, bf16 = jnp.float32, jnp.bfloat16
    scale = 1.0 / math.sqrt(HD)
    x, y, core = place()
    per_chip = tokens // (2 * YS)
    per_core = pl.num_programs(0) // GROUP

    reach = []
    for chip in (y, YS + y):
        begin, end = jnp.int32(0), jnp.int32(0)
        for d in range(docs):
            end = end + len_ref[d]
            begin = jnp.where(chip * per_chip >= end, end, begin)
        reach.append((lax.div(begin, PASS), lax.div((chip + 1) * per_chip, PASS)))
    reach[1] = (jnp.maximum(reach[1][0], reach[0][1]), reach[1][1])

    @pl.when(blk == 0)
    def _():
        def prepare(i, carry):
            rows = rows_at(i * PASS, PASS)
            kt_ref[:, rows] = k_ref[rows, :].T
            vt_ref[0:HD, rows] = v_ref[rows, :].T
            vt_ref[HD:, rows] = jnp.ones((ONES, PASS), bf16)
            dka_ref[rows, :] = jnp.zeros((PASS, HD), f32)
            dva_ref[rows, :] = jnp.zeros((PASS, HD), f32)
            return carry

        for low_chunk, high_chunk in reach:
            lax.fori_loop(low_chunk, high_chunk, prepare, 0)
        blocks = owner_ref.shape[1]
        block_rows = tokens // blocks
        shape = (block_rows, blocks)
        pos = lax.broadcasted_iota(jnp.int32, shape, 1) * block_rows
        pos = pos + lax.broadcasted_iota(jnp.int32, shape, 0)
        begin, end = jnp.zeros(shape, jnp.int32), jnp.int32(0)
        for d in range(docs):
            end = end + len_ref[d]
            begin = jnp.where(pos >= end, end, begin)
        counts = (pos - begin + 1).astype(f32)
        counts = jnp.where(owner_ref[...] == lax.axis_index("context"), counts, 0.0)
        pair_ref[0] = jnp.sum(counts)

    part = lax.div(blk, per_core)
    chip = lax.rem(x + lax.div(part, 2), 2) * YS + y
    row_core = lax.rem(core + part, 2)
    first = chip * per_chip + row_core * (per_chip // 2) + lax.rem(blk, per_core) * block

    def work(heads, inputs, outputs):
        cols = block * heads
        scratch = (
            p_ref.at[:, 0:cols], qt_ref.at[:, 0:cols], gt_ref.at[:, 0:cols], qn_ref.at[0:cols], gn_ref.at[0:cols],
            ds_ref.at[:, 0:cols], acc_ref.at[:, 0:cols], shift_ref,
        )
        attend_block(
            heads, block, first, len_ref, inputs, outputs, k_ref, v_ref, kt_ref, vt_ref, dka_ref, dva_ref, *scratch
        )

    inputs = ((q0_ref, g0_ref), (q1_ref, g1_ref), (q2_ref, g2_ref), (q3_ref, g3_ref))
    outputs = (r0_ref, r1_ref, r2_ref, r3_ref)
    for heads in sorted(set(HEADS)):
        parts = [n for n in range(GROUP) if HEADS[n] == heads]
        chosen = [part == n for n in parts]

        @pl.when(functools.reduce(jnp.logical_or, chosen))
        def _(heads=heads, parts=parts, chosen=chosen):
            work(
                heads, [(c, *inputs[n]) for c, n in zip(chosen, parts)],
                [(c, outputs[n]) for c, n in zip(chosen, parts)],
            )

    @pl.when(blk == pl.num_programs(0) - 1)
    def _():
        def finish(i, carry):
            rows = rows_at(i * PASS, PASS)
            inside = jnp.bool_(False)
            for low_chunk, high_chunk in reach:
                inside = inside | ((i >= low_chunk) & (i < high_chunk))
            for sums, out_ref, factor in ((dka_ref, dk_ref, scale), (dva_ref, dv_ref, 1.0)):

                @pl.when(inside)
                def _(sums=sums, out_ref=out_ref, factor=factor):
                    out_ref[rows, :] = (sums[rows, :] * factor).astype(bf16)

                @pl.when(jnp.logical_not(inside))
                def _(out_ref=out_ref):
                    out_ref[rows, :] = jnp.zeros((PASS, HD), bf16)

            return carry

        lax.fori_loop(0, tokens // PASS, finish, 0)


def attend(queries, out_grad, rows, keys, values, lengths, block_owner):
    tokens = keys.shape[0]
    shard = queries.shape[0]
    per_core = shard // QBLOCK
    span = ((DOC_MAX + QBLOCK + TILE - 2) // TILE + 1) * TILE
    qcols = QBLOCK * max(HEADS)

    def spec(n, width, col):
        return pl.BlockSpec((QBLOCK, width), lambda i, *_: (jnp.clip(i - n * per_core, 0, per_core - 1), col))

    row_specs, row_args = [spec(0, HEADS[0] * HD, 0)] * 2, [queries, out_grad]
    for n in range(1, GROUP):
        row_specs += [spec(n, HEADS[n] * HD, 0), spec(n, HEADS[n] * HD, 1)]
        row_args += [rows[n - 1]] * 2
    full_spec = pl.BlockSpec((tokens, HD), lambda i, *_: (0, 0))
    bf16, f32 = jnp.bfloat16, jnp.float32
    owner_spec = pl.BlockSpec((1, block_owner.shape[0]), lambda i, *_: (0, 0))
    return pl.pallas_call(
        attend_kernel,
        grid_spec=pltpu.PrefetchScalarGridSpec(
            num_scalar_prefetch=1,
            grid=(GROUP * per_core,),
            in_specs=[
                owner_spec, *row_specs, full_spec, full_spec,
            ],
            out_specs=[spec(n, 2 * HEADS[n] * HD, 0) for n in range(GROUP)]
            + [full_spec, full_spec, pl.BlockSpec(memory_space=pltpu.SMEM)],
            scratch_shapes=[
                pltpu.VMEM((HD, tokens), bf16),
                pltpu.VMEM((HD + ONES, tokens), bf16),
                pltpu.VMEM((span, qcols), bf16),
                pltpu.VMEM((HD, qcols), bf16),
                pltpu.VMEM((HD, qcols), bf16),
                pltpu.VMEM((qcols, HD), bf16),
                pltpu.VMEM((qcols, HD), bf16),
                pltpu.VMEM((tokens, HD), f32),
                pltpu.VMEM((tokens, HD), f32),
                pltpu.VMEM((SPAN * TILE, qcols), bf16),
                pltpu.VMEM((HD + ONES, qcols), f32),
                pltpu.VMEM((8, qcols), f32),
            ],
        ),
        out_shape=[jax.ShapeDtypeStruct((shard, 2 * heads * HD), bf16) for heads in HEADS]
        + [jax.ShapeDtypeStruct((tokens, HD), bf16)] * 2
        + [jax.ShapeDtypeStruct((1,), f32)],
        cost_estimate=pl.CostEstimate(flops=2 * 10**10, bytes_accessed=2 * 10**7, transcendentals=5 * 10**6),
        compiler_params=pltpu.CompilerParams(vmem_limit_bytes=62 * 2**20),
        name="attend",
    )(lengths, block_owner.reshape(1, -1), *row_args, keys, values)


def scatter_kernel(
    dk_ref, dv_ref, rows_ref, back_ref, key_ref, value_ref,
    part, from_core, from_far, from_near, from_x,
    part_sem, core_send, core_recv, far_send, far_recv, near_send, near_recv,
    x_send, x_recv, row_send, row_recv,
):
    x, y, core = place()
    shard = key_ref.shape[0]
    half = shard // 2
    up, down, far = (y + 1) % YS, (y + YS - 1) % YS, (y + 2) % YS
    x_rank = rank_of(1 - x, y, core)
    core_rank = rank_of(x, y, 1 - core)
    up_rank, down_rank = rank_of(x, up, core), rank_of(x, down, core)
    started = []

    def send(src, dst, send_sem, recv_sem, rank):
        copy = remote(src, dst, send_sem, recv_sem, rank)
        copy.start()
        started.append(copy)

    def landed(ref, recv_sem):
        remote(ref, ref, recv_sem, recv_sem, x_rank).wait_recv()

    pairs = (dk_ref, dv_ref)
    order = [(1 - x, far), (x, far), (1 - x, up), (x, up), (1 - x, down), (x, down), (1 - x, y), (x, y)]
    loads = []
    for n, (sx, sy) in enumerate(order):
        for a, src in enumerate(pairs):
            rows = rows_at(rank_of(sx, sy, core) * shard, shard)
            copy = pltpu.make_async_copy(src.at[rows], part.at[a, n], part_sem.at[a, n])
            copy.start()
            loads.append(copy)
    enter(x, y, core)
    for n, (sx, sy) in enumerate(order):
        for a, src in enumerate(pairs):
            rows = rows_at(rank_of(sx, sy, 1 - core) * shard, shard)
            send(src.at[rows], from_core.at[a, n], core_send.at[a, n], core_recv.at[a, n], core_rank)

    send(rows_ref, back_ref, row_send, row_recv, core_rank)

    def add(ref, other):
        ref[...] = (ref[...].astype(jnp.float32) + other[...].astype(jnp.float32)).astype(jnp.bfloat16)

    def core_sum(a, n):
        loads[2 * n + a].wait()
        landed(from_core.at[a, n], core_recv.at[a, n])
        add(part.at[a, n], from_core.at[a, n])

    for n in range(2):
        for a in range(2):
            core_sum(a, n)
            for h, rank in ((0, up_rank), (1, down_rank)):
                send(
                    part.at[a, n, pl.ds(h * half, half)], from_far.at[a, n, h],
                    far_send.at[a, n, h], far_recv.at[a, n, h], rank,
                )
    for n in range(2):
        for a in range(2):
            for j, rank in ((0, up_rank), (1, down_rank)):
                core_sum(a, 2 + 2 * j + n)
                free = 1 - j
                send(
                    part.at[a, 2 + 2 * j + n, pl.ds(free * half, half)],
                    from_near.at[a, n, j, pl.ds(free * half, half)],
                    near_send.at[a, n, j, free], near_recv.at[a, n, j, free], rank,
                )
    for n in range(2):
        for a in range(2):
            for j, rank in ((0, up_rank), (1, down_rank)):
                landed(from_far.at[a, n, j], far_recv.at[a, n, j])
                mine = part.at[a, 2 + 2 * j + n, pl.ds(j * half, half)]
                add(mine, from_far.at[a, n, j])
                send(
                    mine, from_near.at[a, n, j, pl.ds(j * half, half)],
                    near_send.at[a, n, j, j], near_recv.at[a, n, j, j], rank,
                )
    for n in range(2):
        for a in range(2):
            core_sum(a, 6 + n)
            for j in range(2):
                for h in (1 - j, j):
                    landed(from_near.at[a, n, j, pl.ds(h * half, half)], near_recv.at[a, n, j, h])
            total = part[a, 6 + n].astype(jnp.float32)
            total = total + from_near[a, n, 0].astype(jnp.float32)
            total = total + from_near[a, n, 1].astype(jnp.float32)
            part[a, 6 + n] = total.astype(jnp.bfloat16)
            if n == 0:
                send(part.at[a, 6], from_x.at[a], x_send.at[a], x_recv.at[a], x_rank)
    for a, dst in enumerate((key_ref, value_ref)):
        landed(from_x.at[a], x_recv.at[a])
        dst[...] = (part[a, 7].astype(jnp.float32) + from_x[a].astype(jnp.float32)).astype(jnp.bfloat16)
    landed(back_ref, row_recv)
    for copy in started:
        copy.wait_send()


def scatter(key_terms, value_terms, rows, ranks):
    tokens = key_terms.shape[0]
    shard = tokens // ranks
    half = shard // 2
    bf16 = jnp.bfloat16
    any_spec = pl.BlockSpec(memory_space=pl.ANY)
    vmem_spec = pl.BlockSpec(memory_space=pltpu.VMEM)
    dma = pltpu.SemaphoreType.DMA
    return pl.pallas_call(
        scatter_kernel,
        in_specs=[any_spec] * 3,
        out_specs=[any_spec, vmem_spec, vmem_spec],
        out_shape=[
            jax.ShapeDtypeStruct(rows.shape, bf16),
            jax.ShapeDtypeStruct((shard, HD), bf16),
            jax.ShapeDtypeStruct((shard, HD), bf16),
        ],
        scratch_shapes=[
            pltpu.VMEM((2, ranks // 2, shard, HD), bf16),
            pltpu.VMEM((2, ranks // 2, shard, HD), bf16),
            pltpu.VMEM((2, 2, 2, half, HD), bf16),
            pltpu.VMEM((2, 2, 2, shard, HD), bf16),
            pltpu.VMEM((2, shard, HD), bf16),
            dma((2, 8)), dma((2, 8)), dma((2, 8)), dma((2, 2, 2)), dma((2, 2, 2)),
            dma((2, 2, 2, 2)), dma((2, 2, 2, 2)), dma((2,)), dma((2,)), dma, dma,
        ],
        cost_estimate=pl.CostEstimate(flops=2 * 10**7, bytes_accessed=2 * 10**7, transcendentals=0),
        compiler_params=pltpu.CompilerParams(
            collective_id=1, has_side_effects=True, vmem_limit_bytes=62 * 2**20
        ),
        name="scatter",
    )(key_terms, value_terms, rows)


def place_kernel(a_ref, b_ref, c_ref, d_ref, k_ref, v_ref, o_ref, q_ref, key_ref, value_ref):
    for d, ref in enumerate((a_ref, b_ref, c_ref, d_ref)):
        cols = head_cols(d)
        width = ref.shape[1] // 2
        o_ref[:, cols] = ref[:, :width]
        q_ref[:, cols] = ref[:, width:]
    key_ref[...] = k_ref[...]
    value_ref[...] = v_ref[...]


def place_columns(pieces, key_grad, value_grad):
    shard = key_grad.shape[0]
    block = shard // 2
    feature = sum(piece.shape[1] for piece in pieces) // 2

    def spec(width):
        return pl.BlockSpec((block, width), lambda i: (i, 0))

    return pl.pallas_call(
        place_kernel,
        grid=(shard // block,),
        in_specs=[spec(piece.shape[1]) for piece in pieces] + [spec(HD)] * 2,
        out_specs=[spec(feature)] * 2 + [spec(HD)] * 2,
        out_shape=[jax.ShapeDtypeStruct((shard, feature), jnp.bfloat16)] * 2
        + [jax.ShapeDtypeStruct((shard, HD), jnp.bfloat16)] * 2,
        compiler_params=pltpu.CompilerParams(vmem_limit_bytes=62 * 2**20),
        name="place",
    )(*pieces, key_grad, value_grad)


def body(queries, key_rows, values, out_grad, lengths, block_owner):
    ranks = lax.axis_size("context")
    chips = [(a, b, c) for a in range(2) for b in range(YS) for c in range(2)]
    same = [(rank_of(a, b, c), rank_of(1 - a, b, c)) for a, b, c in chips]
    cross = [(rank_of(a, b, c), rank_of(1 - a, b, 1 - c)) for a, b, c in chips]
    *rows, keys, all_values = gather(queries, out_grad, key_rows, values, ranks)
    own, near, far_same, far_cross, dk, dv, pair_count = attend(
        queries, out_grad, rows, keys, all_values, lengths, block_owner
    )
    far_same = lax.ppermute(far_same, "context", same)
    far_cross = lax.ppermute(far_cross, "context", cross)
    near, key_grad, value_grad = scatter(dk, dv, near, ranks)
    out, query_grad, key_grad, value_grad = place_columns(
        (own, near, far_same, far_cross), key_grad, value_grad
    )
    return out, query_grad, key_grad, value_grad, pair_count


def solution(mesh):
    rows = P(("dp", "context"), None)
    return jax.shard_map(
        body,
        mesh=mesh,
        in_specs=(rows, rows, rows, rows, P("dp"), P("dp")),
        out_specs=(rows, rows, rows, rows, P(("dp", "context"))),
        check_vma=False,
    )
```

```python
import functools
import math

import jax
import jax.numpy as jnp
from jax import lax
from jax.experimental import pallas as pl
from jax.experimental.pallas import tpu as pltpu
from jax.sharding import PartitionSpec as P

NEG_FILL = -1e30
MESH = pl.DeviceIdType.MESH
YS = 4
HD = 128
HEADS = (3, 2, 2, 1)
GROUP = 4
TILE = 256
SPAN = 4
PASS = 512
ONES = 16
LARGE = 1e12
QBLOCK = 256
DOC_MAX = 4096


def place():
    me = lax.axis_index("context")
    return me // (2 * YS), (me // 2) % YS, me % 2


def rank_of(x, y, core):
    return (x * YS + y) * 2 + core


def remote(src, dst, send_sem, recv_sem, rank):
    return pltpu.make_async_remote_copy(
        src_ref=src,
        dst_ref=dst,
        send_sem=send_sem,
        recv_sem=recv_sem,
        device_id={"context": rank},
        device_id_type=MESH,
    )


def enter(x, y, core, rows=False):
    barrier = pltpu.get_barrier_semaphore()
    others = [
        rank_of(x, y, 1 - core),
        rank_of(1 - x, y, core),
        rank_of(x, (y + 1) % YS, core),
        rank_of(x, (y + YS - 1) % YS, core),
    ]
    if rows:
        others.append(rank_of(1 - x, y, 1 - core))
    for other in others:
        pl.semaphore_signal(barrier, inc=1, device_id={"context": other}, device_id_type=MESH)
    pl.semaphore_wait(barrier, len(others))


def rows_at(begin, count):
    return pl.ds(pl.multiple_of(begin, count), count)


def head_cols(d):
    return pl.ds(sum(HEADS[:d]) * HD, HEADS[d] * HD)


def gather_kernel(
    q_ref, g_ref, k_ref, v_ref, rows1_ref, rows2_ref, rows3_ref, ka_ref, va_ref,
    own_sem, kv_send, kv_recv, core_send, core_recv, row_send, row_recv,
):
    x, y, core = place()
    shard = k_ref.shape[0]
    half = shard // 2
    up, down, far = (y + 1) % YS, (y + YS - 1) % YS, (y + 2) % YS
    x_rank = rank_of(1 - x, y, core)
    core_rank = rank_of(x, y, 1 - core)
    up_rank, down_rank = rank_of(x, up, core), rank_of(x, down, core)
    enter(x, y, core, rows=True)
    started = []

    def send(src, dst, send_sem, recv_sem, rank):
        copy = remote(src, dst, send_sem, recv_sem, rank)
        copy.start()
        started.append(copy)

    def landed(ref, recv_sem):
        remote(ref, ref, recv_sem, recv_sem, x_rank).wait_recv()

    own = []
    pairs = ((k_ref, ka_ref), (v_ref, va_ref))
    my_rows = rows_at(rank_of(x, y, core) * shard, shard)
    for a, (src, dst) in enumerate(pairs):
        send(src, dst.at[my_rows], kv_send.at[a, 0], kv_recv.at[a, 0], x_rank)
        send(src, dst.at[my_rows], kv_send.at[a, 1], kv_recv.at[a, 1], up_rank)
        send(src, dst.at[my_rows], kv_send.at[a, 2], kv_recv.at[a, 2], down_rank)
        send(src, dst.at[my_rows], core_send.at[a, 0], core_recv.at[a, 0], core_rank)
        copy = pltpu.make_async_copy(src, dst.at[my_rows], own_sem.at[a])
        copy.start()
        own.append(copy)

    landing = (rows1_ref, rows2_ref, rows3_ref)
    for a, src in enumerate((q_ref, g_ref)):
        for d in range(1, GROUP):
            tx, tc = (x + d // 2) % 2, (core + d % 2) % 2
            send(
                src.at[:, head_cols(d)], landing[d - 1].at[:, pl.ds(a * HEADS[d] * HD, HEADS[d] * HD)],
                row_send.at[a, d - 1], row_recv.at[a, d - 1], rank_of(tx, y, tc),
            )

    def forward(a, n, ref, rows, rank, relay):
        send(ref.at[rows], ref.at[rows], relay[0].at[a, n], relay[1].at[a, n], rank)

    y_relay, c_relay = (kv_send, kv_recv), (core_send, core_recv)

    def shard_rows(sx, sy, sc):
        return rows_at(rank_of(sx, sy, sc) * shard, shard)

    def half_rows(sx, sy, sc, h):
        return rows_at(rank_of(sx, sy, sc) * shard + h * half, half)

    for a, (_, dst) in enumerate(pairs):
        rows = shard_rows(1 - x, y, core)
        landed(dst.at[rows], kv_recv.at[a, 0])
        forward(a, 3, dst, rows, up_rank, y_relay)
        forward(a, 4, dst, rows, down_rank, y_relay)
        forward(a, 1, dst, rows, core_rank, c_relay)
    for n, sx in ((1, x), (3, 1 - x)):
        for a, (_, dst) in enumerate(pairs):
            landed(dst.at[shard_rows(sx, down, core)], kv_recv.at[a, n])
            forward(a, 4 + n, dst, half_rows(sx, down, core, 0), up_rank, y_relay)
            landed(dst.at[shard_rows(sx, up, core)], kv_recv.at[a, n + 1])
            forward(a, 5 + n, dst, half_rows(sx, up, core, 1), down_rank, y_relay)
            forward(a, 1 + n, dst, shard_rows(sx, down, core), core_rank, c_relay)
            forward(a, 2 + n, dst, shard_rows(sx, up, core), core_rank, c_relay)
    for n, sx in ((1, x), (3, 1 - x)):
        for a, (_, dst) in enumerate(pairs):
            for h in range(2):
                rows = half_rows(sx, far, core, h)
                landed(dst.at[rows], kv_recv.at[a, 4 + n + h])
                forward(a, 5 + n + h, dst, rows, core_rank, c_relay)
    for a, (_, dst) in enumerate(pairs):
        oc = 1 - core
        whole = ((x, y), (1 - x, y), (x, down), (x, up), (1 - x, down), (1 - x, up))
        for n, (sx, sy) in enumerate(whole):
            landed(dst.at[shard_rows(sx, sy, oc)], core_recv.at[a, n])
        for n, sx in ((1, x), (3, 1 - x)):
            for h in range(2):
                landed(dst.at[half_rows(sx, far, oc, h)], core_recv.at[a, 5 + n + h])
    for a in range(2):
        for d in range(1, GROUP):
            landed(landing[d - 1].at[:, pl.ds(a * HEADS[d] * HD, HEADS[d] * HD)], row_recv.at[a, d - 1])
    for copy in own:
        copy.wait()
    for copy in started:
        copy.wait_send()


def gather(queries, out_grad, keys, values, ranks):
    shard = queries.shape[0]
    bf16 = jnp.bfloat16
    any_spec = pl.BlockSpec(memory_space=pl.ANY)
    dma = pltpu.SemaphoreType.DMA
    return pl.pallas_call(
        gather_kernel,
        in_specs=[any_spec] * 4,
        out_specs=[any_spec] * 5,
        out_shape=[
            *[jax.ShapeDtypeStruct((shard, 2 * heads * HD), bf16) for heads in HEADS[1:]],
            jax.ShapeDtypeStruct((ranks * shard, HD), bf16),
            jax.ShapeDtypeStruct((ranks * shard, HD), bf16),
        ],
        scratch_shapes=[
            dma((2,)), dma((2, 9)), dma((2, 9)), dma((2, 10)), dma((2, 10)), dma((2, 3)), dma((2, 3)),
        ],
        compiler_params=pltpu.CompilerParams(collective_id=0, has_side_effects=True, vmem_limit_bytes=62 * 2**20),
        name="gather",
    )(queries, out_grad, keys, values)


def dot(a, b):
    return jnp.dot(a, b, preferred_element_type=jnp.float32)


def attend_block(
    heads, block, first, len_ref, inputs, outputs, k_ref, v_ref, kt_ref, vt_ref, dka_ref, dva_ref,
    p_ref, qt_ref, gt_ref, qn_ref, gn_ref, ds_ref, acc_ref,
):
    f32, bf16 = jnp.float32, jnp.bfloat16
    cols = block * heads
    docs = len_ref.shape[0]
    scale = 1.0 / math.sqrt(HD)
    scale2 = scale * math.log2(math.e)
    row_pos = first + lax.rem(lax.broadcasted_iota(jnp.int32, (1, cols), 1), block)
    row_start = jnp.zeros((1, cols), jnp.int32)
    first_start, last_start, end = jnp.int32(0), jnp.int32(0), jnp.int32(0)
    for d in range(docs):
        end = end + len_ref[d]
        row_start = jnp.where(row_pos >= end, end, row_start)
        first_start = jnp.where(first >= end, end, first_start)
        last_start = jnp.where(first + block - 1 >= end, end, last_start)
    low = lax.div(first_start, TILE)
    high = lax.div(first + block - 1, TILE) + 1

    own_keys = kt_ref[:, rows_at(first, block)].astype(f32)
    shift = []
    for h in range(heads):
        for chosen, q_ref, g_ref in inputs:

            @pl.when(chosen)
            def _(h=h, q_ref=q_ref, g_ref=g_ref):
                qt_ref[:, h * block : (h + 1) * block] = q_ref[:, h * HD : (h + 1) * HD].T
                gt_ref[:, h * block : (h + 1) * block] = g_ref[:, h * HD : (h + 1) * HD].T

        q_t = qt_ref[:, h * block : (h + 1) * block]
        shift.append(jnp.sum(q_t.astype(f32) * own_keys, axis=0, keepdims=True) * scale2)
    shift = jnp.concatenate(shift, axis=1)

    def keep(result, at):
        for chosen, r_ref in outputs:

            @pl.when(chosen)
            def _(r_ref=r_ref):
                for h in range(heads):
                    cut = result[h * block : (h + 1) * block, :]
                    r_ref[:, (at + h) * HD : (at + h + 1) * HD] = cut

    def key_rows(t, count):
        return pl.ds(pl.multiple_of(t * TILE, TILE), count)

    def kept_rows(t, count):
        return pl.ds(pl.multiple_of((t - low) * TILE, TILE), count)

    def sweep(piece):
        count = high - low
        groups = lax.div(count, SPAN)

        def one(g, carry):
            piece(low + g * SPAN, SPAN * TILE, False)
            return carry

        lax.fori_loop(0, groups, one, 0)
        at = low + groups * SPAN
        size = SPAN // 2
        while size:
            has = lax.rem(lax.div(count, size), 2)

            @pl.when(has == 1)
            def _(at=at, size=size):
                piece(at, size * TILE, True)

            at = at + has * size
            size //= 2

    def forward(shift):
        acc_ref[...] = jnp.zeros(acc_ref.shape, f32)

        def piece(t, rows, last):
            def run(mask):
                acc = None
                part = rows
                for i in range(0, rows, part):
                    tile = t + i // TILE
                    s = dot(k_ref[key_rows(tile, part), :], qt_ref[...]) * scale2 - shift
                    if mask:
                        pos = t * TILE + i + lax.broadcasted_iota(jnp.int32, s.shape, 0)
                        s = jnp.where((pos >= row_start) & (pos <= row_pos), s, NEG_FILL)
                    p_ref[kept_rows(tile, part), :] = jnp.exp2(s).astype(bf16)
                    term = dot(vt_ref[:, key_rows(tile, part)], p_ref[kept_rows(tile, part), :])
                    acc = term if acc is None else acc + term
                acc_ref[...] += acc

            if last:
                run(True)
            else:
                edge = (t * TILE < last_start) | (t * TILE + rows - 1 > first)
                pl.when(edge)(lambda: run(True))
                pl.when(jnp.logical_not(edge))(lambda: run(False))

        sweep(piece)

    forward(shift)

    @pl.when(jnp.logical_not(jnp.max(acc_ref[HD : HD + 1, :]) < LARGE))
    def _():
        def peak_pass(t, peak):
            s = dot(k_ref[key_rows(t, TILE), :], qt_ref[...]) * scale2
            pos = t * TILE + lax.broadcasted_iota(jnp.int32, s.shape, 0)
            s = jnp.where((pos >= row_start) & (pos <= row_pos), s, NEG_FILL)
            return jnp.maximum(peak, jnp.max(s.reshape(TILE // 8, 8, cols), axis=0))

        peak = lax.fori_loop(low, high, peak_pass, jnp.full((8, cols), NEG_FILL, f32))
        forward(jnp.max(peak, axis=0, keepdims=True))

    inverse = 1.0 / acc_ref[HD : HD + 1, :]
    out = (acc_ref[0:HD, :] * inverse).astype(bf16)
    grad_t = gt_ref[...].astype(f32)
    grad_dot = jnp.sum(out.astype(f32) * grad_t, axis=0, keepdims=True)
    gn_ref[...] = (grad_t * inverse).astype(bf16).T
    qn_ref[...] = (qt_ref[...].astype(f32) * inverse).astype(bf16).T
    keep(out.T, 0)
    acc_ref[0:HD, :] = jnp.zeros((HD, cols), f32)

    def backward(t, rows, last):
        keys, kept = key_rows(t, rows), kept_rows(t, rows)
        grad_p = dot(v_ref[keys, :], gt_ref[...])
        ds_ref[0:rows, :] = (p_ref[kept, :].astype(f32) * (grad_p - grad_dot)).astype(bf16)
        dva_ref[keys, :] += dot(p_ref[kept, :], gn_ref[...])
        dka_ref[keys, :] += dot(ds_ref[0:rows, :], qn_ref[...])
        acc_ref[0:HD, :] += dot(kt_ref[:, keys], ds_ref[0:rows, :])

    sweep(backward)
    query_grad = (acc_ref[0:HD, :] * (inverse * scale)).astype(bf16).T
    keep(query_grad, heads)


def attend_kernel(
    len_ref, owner_ref, q0_ref, g0_ref, q1_ref, g1_ref, q2_ref, g2_ref, q3_ref, g3_ref, k_ref, v_ref,
    r0_ref, r1_ref, r2_ref, r3_ref, dk_ref, dv_ref, pair_ref,
    kt_ref, vt_ref, p_ref, qt_ref, gt_ref, qn_ref, gn_ref, dka_ref, dva_ref, ds_ref, acc_ref,
):
    blk = pl.program_id(0)
    block = q0_ref.shape[0]
    tokens = k_ref.shape[0]
    docs = len_ref.shape[0]
    f32, bf16 = jnp.float32, jnp.bfloat16
    scale = 1.0 / math.sqrt(HD)
    x, y, core = place()
    per_chip = tokens // (2 * YS)
    per_core = pl.num_programs(0) // GROUP

    reach = []
    for chip in (y, YS + y):
        begin, end = jnp.int32(0), jnp.int32(0)
        for d in range(docs):
            end = end + len_ref[d]
            begin = jnp.where(chip * per_chip >= end, end, begin)
        reach.append((lax.div(begin, PASS), lax.div((chip + 1) * per_chip, PASS)))
    reach[1] = (jnp.maximum(reach[1][0], reach[0][1]), reach[1][1])

    @pl.when(blk == 0)
    def _():
        def prepare(i, carry):
            rows = rows_at(i * PASS, PASS)
            kt_ref[:, rows] = k_ref[rows, :].T
            vt_ref[0:HD, rows] = v_ref[rows, :].T
            vt_ref[HD:, rows] = jnp.ones((ONES, PASS), bf16)
            dka_ref[rows, :] = jnp.zeros((PASS, HD), f32)
            dva_ref[rows, :] = jnp.zeros((PASS, HD), f32)
            return carry

        for low_chunk, high_chunk in reach:
            lax.fori_loop(low_chunk, high_chunk, prepare, 0)
        blocks = owner_ref.shape[1]
        block_rows = tokens // blocks
        shape = (block_rows, blocks)
        pos = lax.broadcasted_iota(jnp.int32, shape, 1) * block_rows
        pos = pos + lax.broadcasted_iota(jnp.int32, shape, 0)
        begin, end = jnp.zeros(shape, jnp.int32), jnp.int32(0)
        for d in range(docs):
            end = end + len_ref[d]
            begin = jnp.where(pos >= end, end, begin)
        counts = (pos - begin + 1).astype(f32)
        counts = jnp.where(owner_ref[...] == lax.axis_index("context"), counts, 0.0)
        pair_ref[0] = jnp.sum(counts)

    part = lax.div(blk, per_core)
    chip = lax.rem(x + lax.div(part, 2), 2) * YS + y
    row_core = lax.rem(core + part, 2)
    first = chip * per_chip + row_core * (per_chip // 2) + lax.rem(blk, per_core) * block

    def work(heads, inputs, outputs):
        cols = block * heads
        scratch = (
            p_ref.at[:, 0:cols], qt_ref.at[:, 0:cols], gt_ref.at[:, 0:cols], qn_ref.at[0:cols], gn_ref.at[0:cols],
            ds_ref.at[:, 0:cols], acc_ref.at[:, 0:cols],
        )
        attend_block(
            heads, block, first, len_ref, inputs, outputs, k_ref, v_ref, kt_ref, vt_ref, dka_ref, dva_ref, *scratch
        )

    inputs = ((q0_ref, g0_ref), (q1_ref, g1_ref), (q2_ref, g2_ref), (q3_ref, g3_ref))
    outputs = (r0_ref, r1_ref, r2_ref, r3_ref)
    for heads in sorted(set(HEADS)):
        parts = [n for n in range(GROUP) if HEADS[n] == heads]
        chosen = [part == n for n in parts]

        @pl.when(functools.reduce(jnp.logical_or, chosen))
        def _(heads=heads, parts=parts, chosen=chosen):
            work(
                heads, [(c, *inputs[n]) for c, n in zip(chosen, parts)],
                [(c, outputs[n]) for c, n in zip(chosen, parts)],
            )

    @pl.when(blk == pl.num_programs(0) - 1)
    def _():
        def finish(i, carry):
            rows = rows_at(i * PASS, PASS)
            inside = jnp.bool_(False)
            for low_chunk, high_chunk in reach:
                inside = inside | ((i >= low_chunk) & (i < high_chunk))
            for sums, out_ref, factor in ((dka_ref, dk_ref, scale), (dva_ref, dv_ref, 1.0)):

                @pl.when(inside)
                def _(sums=sums, out_ref=out_ref, factor=factor):
                    out_ref[rows, :] = (sums[rows, :] * factor).astype(bf16)

                @pl.when(jnp.logical_not(inside))
                def _(out_ref=out_ref):
                    out_ref[rows, :] = jnp.zeros((PASS, HD), bf16)

            return carry

        lax.fori_loop(0, tokens // PASS, finish, 0)


def attend(queries, out_grad, rows, keys, values, lengths, block_owner):
    tokens = keys.shape[0]
    shard = queries.shape[0]
    per_core = shard // QBLOCK
    span = ((DOC_MAX + QBLOCK + TILE - 2) // TILE + 1) * TILE
    qcols = QBLOCK * max(HEADS)

    def spec(n, width, col):
        return pl.BlockSpec((QBLOCK, width), lambda i, *_: (jnp.clip(i - n * per_core, 0, per_core - 1), col))

    row_specs, row_args = [spec(0, HEADS[0] * HD, 0)] * 2, [queries, out_grad]
    for n in range(1, GROUP):
        row_specs += [spec(n, HEADS[n] * HD, 0), spec(n, HEADS[n] * HD, 1)]
        row_args += [rows[n - 1]] * 2
    full_spec = pl.BlockSpec((tokens, HD), lambda i, *_: (0, 0))
    bf16, f32 = jnp.bfloat16, jnp.float32
    owner_spec = pl.BlockSpec((1, block_owner.shape[0]), lambda i, *_: (0, 0))
    return pl.pallas_call(
        attend_kernel,
        grid_spec=pltpu.PrefetchScalarGridSpec(
            num_scalar_prefetch=1,
            grid=(GROUP * per_core,),
            in_specs=[
                owner_spec, *row_specs, full_spec, full_spec,
            ],
            out_specs=[spec(n, 2 * HEADS[n] * HD, 0) for n in range(GROUP)]
            + [full_spec, full_spec, pl.BlockSpec(memory_space=pltpu.SMEM)],
            scratch_shapes=[
                pltpu.VMEM((HD, tokens), bf16),
                pltpu.VMEM((HD + ONES, tokens), bf16),
                pltpu.VMEM((span, qcols), bf16),
                pltpu.VMEM((HD, qcols), bf16),
                pltpu.VMEM((HD, qcols), bf16),
                pltpu.VMEM((qcols, HD), bf16),
                pltpu.VMEM((qcols, HD), bf16),
                pltpu.VMEM((tokens, HD), f32),
                pltpu.VMEM((tokens, HD), f32),
                pltpu.VMEM((SPAN * TILE, qcols), bf16),
                pltpu.VMEM((HD + ONES, qcols), f32),
            ],
        ),
        out_shape=[jax.ShapeDtypeStruct((shard, 2 * heads * HD), bf16) for heads in HEADS]
        + [jax.ShapeDtypeStruct((tokens, HD), bf16)] * 2
        + [jax.ShapeDtypeStruct((1,), f32)],
        cost_estimate=pl.CostEstimate(flops=2 * 10**10, bytes_accessed=2 * 10**7, transcendentals=5 * 10**6),
        compiler_params=pltpu.CompilerParams(vmem_limit_bytes=62 * 2**20),
        name="attend",
    )(lengths, block_owner.reshape(1, -1), *row_args, keys, values)


def scatter_kernel(
    dk_ref, dv_ref, rows_ref, back_ref, key_ref, value_ref,
    part, from_core, from_far, from_near, from_x,
    part_sem, core_send, core_recv, far_send, far_recv, near_send, near_recv,
    x_send, x_recv, row_send, row_recv,
):
    x, y, core = place()
    shard = key_ref.shape[0]
    half = shard // 2
    up, down, far = (y + 1) % YS, (y + YS - 1) % YS, (y + 2) % YS
    x_rank = rank_of(1 - x, y, core)
    core_rank = rank_of(x, y, 1 - core)
    up_rank, down_rank = rank_of(x, up, core), rank_of(x, down, core)
    started = []

    def send(src, dst, send_sem, recv_sem, rank):
        copy = remote(src, dst, send_sem, recv_sem, rank)
        copy.start()
        started.append(copy)

    def landed(ref, recv_sem):
        remote(ref, ref, recv_sem, recv_sem, x_rank).wait_recv()

    pairs = (dk_ref, dv_ref)
    order = [(1 - x, far), (x, far), (1 - x, up), (x, up), (1 - x, down), (x, down), (1 - x, y), (x, y)]
    loads = []
    for n, (sx, sy) in enumerate(order):
        for a, src in enumerate(pairs):
            rows = rows_at(rank_of(sx, sy, core) * shard, shard)
            copy = pltpu.make_async_copy(src.at[rows], part.at[a, n], part_sem.at[a, n])
            copy.start()
            loads.append(copy)
    enter(x, y, core)
    for n, (sx, sy) in enumerate(order):
        for a, src in enumerate(pairs):
            rows = rows_at(rank_of(sx, sy, 1 - core) * shard, shard)
            send(src.at[rows], from_core.at[a, n], core_send.at[a, n], core_recv.at[a, n], core_rank)

    send(rows_ref, back_ref, row_send, row_recv, core_rank)

    def add(ref, other):
        ref[...] = (ref[...].astype(jnp.float32) + other[...].astype(jnp.float32)).astype(jnp.bfloat16)

    def core_sum(a, n):
        loads[2 * n + a].wait()
        landed(from_core.at[a, n], core_recv.at[a, n])
        add(part.at[a, n], from_core.at[a, n])

    for n in range(2):
        for a in range(2):
            core_sum(a, n)
            for h, rank in ((0, up_rank), (1, down_rank)):
                send(
                    part.at[a, n, pl.ds(h * half, half)], from_far.at[a, n, h],
                    far_send.at[a, n, h], far_recv.at[a, n, h], rank,
                )
    for n in range(2):
        for a in range(2):
            for j, rank in ((0, up_rank), (1, down_rank)):
                core_sum(a, 2 + 2 * j + n)
                free = 1 - j
                send(
                    part.at[a, 2 + 2 * j + n, pl.ds(free * half, half)],
                    from_near.at[a, n, j, pl.ds(free * half, half)],
                    near_send.at[a, n, j, free], near_recv.at[a, n, j, free], rank,
                )
    for n in range(2):
        for a in range(2):
            for j, rank in ((0, up_rank), (1, down_rank)):
                landed(from_far.at[a, n, j], far_recv.at[a, n, j])
                mine = part.at[a, 2 + 2 * j + n, pl.ds(j * half, half)]
                add(mine, from_far.at[a, n, j])
                send(
                    mine, from_near.at[a, n, j, pl.ds(j * half, half)],
                    near_send.at[a, n, j, j], near_recv.at[a, n, j, j], rank,
                )
    for n in range(2):
        for a in range(2):
            core_sum(a, 6 + n)
            for j in range(2):
                for h in (1 - j, j):
                    landed(from_near.at[a, n, j, pl.ds(h * half, half)], near_recv.at[a, n, j, h])
            total = part[a, 6 + n].astype(jnp.float32)
            total = total + from_near[a, n, 0].astype(jnp.float32)
            total = total + from_near[a, n, 1].astype(jnp.float32)
            part[a, 6 + n] = total.astype(jnp.bfloat16)
            if n == 0:
                send(part.at[a, 6], from_x.at[a], x_send.at[a], x_recv.at[a], x_rank)
    for a, dst in enumerate((key_ref, value_ref)):
        landed(from_x.at[a], x_recv.at[a])
        dst[...] = (part[a, 7].astype(jnp.float32) + from_x[a].astype(jnp.float32)).astype(jnp.bfloat16)
    landed(back_ref, row_recv)
    for copy in started:
        copy.wait_send()


def scatter(key_terms, value_terms, rows, ranks):
    tokens = key_terms.shape[0]
    shard = tokens // ranks
    half = shard // 2
    bf16 = jnp.bfloat16
    any_spec = pl.BlockSpec(memory_space=pl.ANY)
    vmem_spec = pl.BlockSpec(memory_space=pltpu.VMEM)
    dma = pltpu.SemaphoreType.DMA
    return pl.pallas_call(
        scatter_kernel,
        in_specs=[any_spec] * 3,
        out_specs=[any_spec, vmem_spec, vmem_spec],
        out_shape=[
            jax.ShapeDtypeStruct(rows.shape, bf16),
            jax.ShapeDtypeStruct((shard, HD), bf16),
            jax.ShapeDtypeStruct((shard, HD), bf16),
        ],
        scratch_shapes=[
            pltpu.VMEM((2, ranks // 2, shard, HD), bf16),
            pltpu.VMEM((2, ranks // 2, shard, HD), bf16),
            pltpu.VMEM((2, 2, 2, half, HD), bf16),
            pltpu.VMEM((2, 2, 2, shard, HD), bf16),
            pltpu.VMEM((2, shard, HD), bf16),
            dma((2, 8)), dma((2, 8)), dma((2, 8)), dma((2, 2, 2)), dma((2, 2, 2)),
            dma((2, 2, 2, 2)), dma((2, 2, 2, 2)), dma((2,)), dma((2,)), dma, dma,
        ],
        cost_estimate=pl.CostEstimate(flops=2 * 10**7, bytes_accessed=2 * 10**7, transcendentals=0),
        compiler_params=pltpu.CompilerParams(
            collective_id=1, has_side_effects=True, vmem_limit_bytes=62 * 2**20
        ),
        name="scatter",
    )(key_terms, value_terms, rows)


def place_kernel(a_ref, b_ref, c_ref, d_ref, k_ref, v_ref, o_ref, q_ref, key_ref, value_ref):
    for d, ref in enumerate((a_ref, b_ref, c_ref, d_ref)):
        cols = head_cols(d)
        width = ref.shape[1] // 2
        o_ref[:, cols] = ref[:, :width]
        q_ref[:, cols] = ref[:, width:]
    key_ref[...] = k_ref[...]
    value_ref[...] = v_ref[...]


def place_columns(pieces, key_grad, value_grad):
    shard = key_grad.shape[0]
    block = shard // 2
    feature = sum(piece.shape[1] for piece in pieces) // 2

    def spec(width):
        return pl.BlockSpec((block, width), lambda i: (i, 0))

    return pl.pallas_call(
        place_kernel,
        grid=(shard // block,),
        in_specs=[spec(piece.shape[1]) for piece in pieces] + [spec(HD)] * 2,
        out_specs=[spec(feature)] * 2 + [spec(HD)] * 2,
        out_shape=[jax.ShapeDtypeStruct((shard, feature), jnp.bfloat16)] * 2
        + [jax.ShapeDtypeStruct((shard, HD), jnp.bfloat16)] * 2,
        compiler_params=pltpu.CompilerParams(vmem_limit_bytes=62 * 2**20),
        name="place",
    )(*pieces, key_grad, value_grad)


def body(queries, key_rows, values, out_grad, lengths, block_owner):
    ranks = lax.axis_size("context")
    chips = [(a, b, c) for a in range(2) for b in range(YS) for c in range(2)]
    same = [(rank_of(a, b, c), rank_of(1 - a, b, c)) for a, b, c in chips]
    cross = [(rank_of(a, b, c), rank_of(1 - a, b, 1 - c)) for a, b, c in chips]
    *rows, keys, all_values = gather(queries, out_grad, key_rows, values, ranks)
    own, near, far_same, far_cross, dk, dv, pair_count = attend(
        queries, out_grad, rows, keys, all_values, lengths, block_owner
    )
    far_same = lax.ppermute(far_same, "context", same)
    far_cross = lax.ppermute(far_cross, "context", cross)
    near, key_grad, value_grad = scatter(dk, dv, near, ranks)
    out, query_grad, key_grad, value_grad = place_columns(
        (own, near, far_same, far_cross), key_grad, value_grad
    )
    return out, query_grad, key_grad, value_grad, pair_count


def solution(mesh):
    rows = P(("dp", "context"), None)
    return jax.shard_map(
        body,
        mesh=mesh,
        in_specs=(rows, rows, rows, rows, P("dp"), P("dp")),
        out_specs=(rows, rows, rows, rows, P(("dp", "context"))),
        check_vma=False,
    )
```
